32 devices in a mesh: blk: 8 (over z, x), pair: 4 (over y, core).
Axes of the slice: x: 2, y: 2, z: 4, core: 2. Of those that a mesh axis runs over, the one named last changes fastest.
Arguments:
- features: float32 [64, 65536], P(None, 'blk'), may hold values from -6 to 6
- inv_scale: float32 [64], replicated, may hold values from 0.03125 to 20
- signal: float32 [1], replicated, may hold values from 0.110485435 to 0.44194174
- noise_var: float32 [65536], P('blk'), may hold values from 0.5 to 2
- right_side: float32 [32, 65536], P(None, 'blk'), may hold values from -30 to 30
- block_pairs: int32 [128, 2], P(('blk', 'pair')), may hold values from -1 to 31, as said below
Outputs:
- solution: float32 [32, 65536], P(None, 'blk')
- residual: float32 [32, 65536], P(None, 'blk')
The draws below stay inside these ranges and needn't reach their ends.
Inputs may be any that keep to these rules, and one draw needn't show every extreme that they name: `block_pairs`: rows run over the blk index, then the pair index, then 4 slots of one device. In each device's slots the live pairs come first; dead slots hold -1 in both columns. A live pair (i, j) has block i among blocks blk index * 4 to blk index * 4 + 3 of the device's blk index, and j equal to i or i + 1. Every block's pair (i, i) is listed once and no pair twice. In each blk index some device has all its slots live.
All inputs are finite; a program needn't handle non-finite values.
Results may differ from the reference program's by a relative error of at most 0.0011.
Values sent between devices are 32-bit elements; how exact they have to be, the bound alone decides.
No kernel may reach another device: no remote copies, remote signals or barrier semaphores. Data moves between devices by JAX's collectives and lax.ppermute only.
A program may use at most 64 MiB of HBM per device.

```python
import math
import jax
import jax.numpy as jnp
from jax import lax

BS = 2048
F = 64
R = 32
ITERS = 2
BLK_DEV = 4
PAIRS_DEV = 4
NOBS = 65536
N_BLK = 8
N_PAIR = 4


def draw_block_pairs(key, part):
    groups = N_BLK
    options = 2 * BLK_DEV
    coin_key, score_key, deal_key = jax.random.split(jax.random.fold_in(key, 11), 3)
    column = jnp.arange(options, dtype=jnp.int32)[None, :]
    group_ids = jnp.arange(groups, dtype=jnp.int32)[:, None]
    row_block = group_ids * BLK_DEV + column % BLK_DEV
    col_block = row_block + column // BLK_DEV
    allowed = col_block < BLK_DEV * N_BLK
    coin_flips = jax.random.randint(coin_key, (groups, options), 0, 5) < 3
    living = allowed & ((column < BLK_DEV) | coin_flips)
    scores = jax.random.randint(score_key, (groups, options), 0, 4096) * options + column
    keyed = jnp.where(living, scores, 8192 * options + column)
    ordering = jnp.argsort(keyed, axis=1, stable=True)
    counted = jnp.sum(living.astype(jnp.int32), axis=1)
    dealing = jax.vmap(lambda sub_key: jax.random.permutation(sub_key, N_PAIR))(jax.random.split(deal_key, groups))
    placing = jnp.argsort(dealing, axis=1)
    positions = placing[:, :, None] * PAIRS_DEV + jnp.arange(PAIRS_DEV, dtype=jnp.int32)[None, None, :]
    filled = positions < counted[:, None, None]
    flat_positions = jnp.minimum(positions, options - 1).reshape(groups, -1)
    picked = jnp.take_along_axis(ordering, flat_positions, axis=1)
    row_pick = jnp.take_along_axis(jnp.broadcast_to(row_block, (groups, options)), picked, axis=1).reshape(filled.shape)
    col_pick = jnp.take_along_axis(jnp.broadcast_to(col_block, (groups, options)), picked, axis=1).reshape(filled.shape)
    result = jnp.stack([jnp.where(filled, row_pick, -1), jnp.where(filled, col_pick, -1)], axis=-1)
    return result.reshape(groups * N_PAIR * PAIRS_DEV, 2).astype(jnp.int32)


def draw_inv_scale(key, part):
    small_key, large_key, pick_key = jax.random.split(jax.random.fold_in(key, 37), 3)
    highest = 5 * F // 16 * 1.0
    lowest_large = 0.6 * highest
    smallest = 2.0 ** (-5)
    largest_small = 0.5
    order = jax.random.permutation(pick_key, F)
    picked_large = order < 2
    small_values = jnp.exp(jax.random.uniform(small_key, (F,), minval=jnp.log(smallest), maxval=jnp.log(largest_small)))
    large_values = jnp.exp(jax.random.uniform(large_key, (F,), minval=jnp.log(lowest_large), maxval=jnp.log(highest)))
    values = jnp.where(picked_large, large_values, small_values)
    return jnp.clip(values, smallest, highest).astype(jnp.float32)


def draw_right_side(key, part):
    base_key = jax.random.fold_in(jax.random.fold_in(key, 23), 0)
    columns = NOBS
    rising = jnp.sqrt(1.0 + 2.0 * jnp.arange(columns, dtype=jnp.float32) / columns)
    values = jax.random.normal(base_key, (R, columns))
    return jnp.clip(values * rising[None, :], -30.0, 30.0).astype(jnp.float32)


def steps_of(stream_key, dims, shards, low, high):
    gain, own = 1.0, jax.random.fold_in(stream_key, 6)
    for axis_at, shards_of in shards:
        heights = jnp.exp(jax.random.uniform(jax.random.fold_in(own, axis_at), (shards_of,), jnp.float32, low / len(shards), high / len(shards)))
        gain = gain * jnp.repeat(heights, dims[axis_at] // shards_of).reshape([-1 if axis == axis_at else 1 for axis in range(len(dims))])
    return gain


def scatter_about(rng, dims, scale, bound, shards=(), held_as=jnp.bfloat16):
    entries = scale * jax.random.normal(rng, dims, jnp.float32)
    if shards:
        entries = entries * steps_of(rng, dims, shards, -0.22, 0.18)
    return jnp.clip(entries, -bound, bound).astype(held_as)


def setup_inputs(seed: int = 0) -> dict:
    keys = jax.random.split(jax.random.key(seed), 7)
    features = scatter_about(keys[0], (F, NOBS), 1.0, 6.0, ((1, 8),), jnp.float32)
    inv_scale = draw_inv_scale(jax.random.fold_in(keys[6], 71), 0)
    signal = jnp.clip(jnp.exp(jax.random.uniform(keys[2], (1,), jnp.float32, math.log(0.110485435), math.log(0.44194174))), 0.110485435, 0.44194174)
    noise_var = jnp.clip(jnp.exp(math.log(2.0) - 1.3862944 * jax.random.uniform(keys[3], (NOBS,), jnp.float32) ** steps_of(keys[3], (NOBS,), ((0, 8),), -0.2, 0.2)), 0.5, 2.0)
    right_side = draw_right_side(jax.random.fold_in(keys[6], 71), 0)
    block_pairs = draw_block_pairs(jax.random.fold_in(keys[6], 71), 0)
    return dict(features=features, inv_scale=inv_scale, signal=signal, noise_var=noise_var, right_side=right_side, block_pairs=block_pairs)


root_three = 1.7320508075688772
taper_radius = 2.0

def kernel_tile(left_scaled, right_scaled, amplitude):
    cross = lax.dot_general(left_scaled, right_scaled, (((0,), (0,)), ((), ())), precision=lax.Precision.HIGHEST, preferred_element_type=jnp.float32)
    left_norms = lax.optimization_barrier(jnp.sum(left_scaled * left_scaled, axis=0))
    right_norms = lax.optimization_barrier(jnp.sum(right_scaled * right_scaled, axis=0))
    squared = (left_norms[:, None] + right_norms[None, :] - 2.0 * cross) / left_scaled.shape[0]
    distance = jnp.sqrt(jnp.maximum(squared, 0.0))
    stretched = root_three * distance
    ratio = distance / taper_radius
    taper = jnp.maximum(1.0 - ratio, 0.0) ** 4 * (1.0 + 4.0 * ratio)
    return amplitude * (1.0 + stretched) * jnp.exp(-stretched) * taper

def apply_operator(direction, scaled, block_pairs, amplitude, noise_var):
    halved = direction.astype(jnp.bfloat16)

    def visit(summed, listed):
        row_block = listed[0].astype(jnp.int32)
        col_block = listed[1].astype(jnp.int32)

        def work(summed):
            row_start = (row_block * BS).astype(jnp.int32)
            col_start = (col_block * BS).astype(jnp.int32)
            kernel_block = kernel_tile(lax.dynamic_slice_in_dim(scaled, row_start, BS, 1), lax.dynamic_slice_in_dim(scaled, col_start, BS, 1), amplitude)
            block_half = kernel_block.astype(jnp.bfloat16)
            crossing = (row_block != col_block).astype(jnp.float32)
            left_dir = lax.dynamic_slice_in_dim(direction, row_start, BS, 1)
            right_dir = lax.dynamic_slice_in_dim(direction, col_start, BS, 1)
            left_half = lax.dynamic_slice_in_dim(halved, row_start, BS, 1)
            right_half = lax.dynamic_slice_in_dim(halved, col_start, BS, 1)
            term_left = lax.dot_general(right_half, block_half, (((1,), (1,)), ((), ())), preferred_element_type=jnp.float32) + crossing * lax.optimization_barrier(jnp.sum(kernel_block, axis=1))[None, :] * left_dir
            term_right = crossing * (jnp.dot(left_half, block_half, preferred_element_type=jnp.float32) + lax.optimization_barrier(jnp.sum(kernel_block, axis=0))[None, :] * right_dir)
            summed = lax.dynamic_update_slice_in_dim(summed, lax.dynamic_slice_in_dim(summed, row_start, BS, 1) + term_left, row_start, 1)
            summed = lax.dynamic_update_slice_in_dim(summed, lax.dynamic_slice_in_dim(summed, col_start, BS, 1) + term_right, col_start, 1)
            return summed
        return (lax.cond(row_block >= 0, work, lambda unchanged: unchanged, summed), None)
    summed, _ = lax.scan(visit, jnp.zeros(direction.shape, jnp.float32), block_pairs)
    return noise_var[None, :] * direction + summed

def reference(features, inv_scale, signal, noise_var, right_side, block_pairs):
    scaled = features * inv_scale[:, None]
    amplitude = signal[0]
    solution = jnp.zeros_like(right_side)
    residual = right_side
    direction = right_side
    norm_now = lax.optimization_barrier(jnp.sum(residual * residual, axis=1))
    for iteration in range(ITERS):
        applied = apply_operator(direction, scaled, block_pairs, amplitude, noise_var)
        step_size = norm_now / lax.optimization_barrier(jnp.sum(direction * applied, axis=1))
        solution = solution + step_size[:, None] * direction
        residual = residual - step_size[:, None] * applied
        if iteration + 1 < ITERS:
            norm_next = lax.optimization_barrier(jnp.sum(residual * residual, axis=1))
            direction = residual + (norm_next / norm_now)[:, None] * direction
            norm_now = norm_next
    return (solution, residual)
```

```python
import functools
import math

import jax
import jax.numpy as jnp
from jax import lax
from jax.experimental import pallas as pl
from jax.experimental.pallas import tpu as pltpu
from jax.sharding import PartitionSpec as P

BS = 2048
ITERS = 2

f32 = jnp.float32
bf16 = jnp.bfloat16
root_three = 1.7320508075688772
taper_radius = 2.0
BOTH = ("blk", "pair")
NT = (((1,), (1,)), ((), ()))
STRIP = 512
VMEM_LIMIT = 48 << 20


def parts_of(x):
    high = x.astype(bf16)
    rest = x - high.astype(f32)
    middle = rest.astype(bf16)
    low = (rest - middle.astype(f32)).astype(bf16)
    return high, middle, low


def left_parts(scaled, shrink):
    turned = scaled.T
    high, middle, _ = parts_of(turned)
    norms = jnp.sum(turned * turned, axis=1, keepdims=True) * shrink
    n_high, n_middle, n_low = (x.astype(f32) for x in parts_of(norms))
    lane = lax.broadcasted_iota(jnp.int32, turned.shape, 1)
    extra = jnp.where(
        lane == 0,
        n_high,
        jnp.where(lane == 1, n_middle, jnp.where(lane == 2, n_low, jnp.where(lane < 6, 1.0, 0.0))),
    ).astype(bf16)
    return jnp.concatenate([high, high, middle, extra], axis=1)


def right_parts(scaled, shrink):
    high, middle, _ = parts_of(scaled * (-2.0 * shrink))
    norms = jnp.sum(scaled * scaled, axis=0, keepdims=True) * shrink
    n_high, n_middle, n_low = (x.astype(f32) for x in parts_of(norms))
    row = lax.broadcasted_iota(jnp.int32, scaled.shape, 0)
    extra = jnp.where(
        row < 3,
        1.0,
        jnp.where(
            row == 3,
            n_high,
            jnp.where(row == 4, n_middle, jnp.where(row == 5, n_low, 0.0)),
        ),
    ).astype(bf16)
    return jnp.concatenate([high, middle, high, extra], axis=0)


def kernel_values(q, amplitude):
    q = jnp.maximum(q, 1e-30)
    t = q * lax.rsqrt(q)
    slope = taper_radius * root_three
    u = jnp.maximum(1.0 - t, 0.0)
    u2 = u * u
    poly = amplitude + t * (amplitude * (4.0 + slope) + (amplitude * (4.0 * slope)) * t)
    decay = jnp.exp2(t * (-slope * math.log2(math.e)))
    return (poly * decay) * (u2 * u2)


def dot(a, b):
    return jnp.dot(a, b, preferred_element_type=f32)


def dot_nt(a, b):
    return lax.dot_general(a, b, NT, preferred_element_type=f32)


def lanes_of(columns, rows):
    lane = lax.broadcasted_iota(jnp.int32, (rows, 128), 1)
    out = jnp.zeros((rows, 128), f32)
    for at, column in enumerate(columns):
        out = jnp.where(lane == at, column, out)
    return out


def row_dot(a, b):
    return jnp.sum(a * b, axis=1, keepdims=True)


def diagonal_kernel(place, signal, features, inv_scale, direction, tile, own, left, right, half):
    step = pl.program_id(0)
    strip = tile.shape[0]
    size = tile.shape[1]
    amplitude = signal[0]
    shrink = 1.0 / (taper_radius * taper_radius * features.shape[0])

    @pl.when(step == 0)
    def _():
        scaled = features[...] * inv_scale[...]
        left[...] = left_parts(scaled, shrink)
        right[...] = right_parts(scaled, shrink)
        half[...] = direction[...].astype(bf16)
        own[...] = jnp.zeros_like(own)

    for at in range(size // strip):

        @pl.when(step == at)
        def _(at=at):
            rows = slice(at * strip, (at + 1) * strip)
            for col in range(at * strip, size, strip):
                cols = slice(col, col + strip)
                q = dot(left[rows, :], right[:, cols])
                block = kernel_values(q, amplitude).astype(bf16)
                tile[:, cols] = block
                own[:, cols] += dot(half[:, rows], block)
                if col > at * strip:
                    own[:, rows] += dot_nt(half[:, cols], block)


def crossing_kernel(
    place,
    signal,
    features_left,
    features_here,
    features_sent,
    inv_scale,
    dir_left,
    dir_here,
    dir_sent,
    noise,
    diagonal,
    tile,
    row_sums,
    col_sums,
    own,
    over,
    dir_next,
    sums,
    left,
    right,
    half_left,
    half_right,
    col_part,
):
    step = pl.program_id(0)
    steps = pl.num_programs(0)
    strip = tile.shape[0]
    size = tile.shape[1]
    amplitude = signal[0]
    shrink = 1.0 / (taper_radius * taper_radius * features_left.shape[0])
    live = place[1] > 0
    last = place[2] > 0

    @pl.when(step == 0)
    def _():
        dir_next[...] = jnp.where(last, dir_sent[...], dir_here[...])
        own[...] = jnp.zeros_like(own)
        over[...] = jnp.zeros_like(over)
        row_sums[...] = jnp.zeros_like(row_sums)
        col_part[...] = jnp.zeros_like(col_part)

        @pl.when(live)
        def _():
            scale = inv_scale[...]
            left[...] = left_parts(features_left[...] * scale, shrink)
            there = jnp.where(last, features_sent[...], features_here[...])
            right[...] = right_parts(there * scale, shrink)
            half_left[...] = dir_left[...].astype(bf16)
            half_right[...] = dir_next[...].astype(bf16)

    @pl.when(live)
    def _():
        rows = pl.ds(pl.multiple_of(step * strip, strip), strip)
        left_rows = left[rows, :]
        half_rows = half_left[:, rows]
        toward = jnp.zeros((dir_left.shape[0], strip), f32)
        row_part = jnp.zeros((strip, 128), f32)
        for col in range(0, size, strip):
            cols = slice(col, col + strip)
            values = kernel_values(dot(left_rows, right[:, cols]), amplitude)
            block = values.astype(bf16)
            tile[:, cols] = block
            toward = toward + dot_nt(half_right[:, cols], block)
            over[:, cols] += dot(half_rows, block)
            for lane in range(0, strip, 128):
                row_part = row_part + values[:, lane : lane + 128]
            col_part[:, cols] += jnp.sum(values.reshape(strip // 8, 8, strip), axis=0)
        own[:, rows] = toward
        row_sums[:, rows] = lax.dot_general(
            jnp.ones((8, 128), f32),
            row_part,
            NT,
            precision=lax.Precision.HIGHEST,
            preferred_element_type=f32,
        )

    @pl.when(step == steps - 1)
    def _():
        here = dir_left[...]
        ahead = dir_next[...]
        columns = jnp.sum(col_part[...], axis=0, keepdims=True)
        col_sums[...] = columns
        mine = own[...] + diagonal[...] + (noise[...] + row_sums[0:1, :]) * here
        theirs = over[...] + columns * ahead
        own[...] = mine
        over[...] = theirs
        curvature = row_dot(here, mine) + row_dot(ahead, theirs)
        sums[...] = lanes_of([row_dot(here, here), curvature], here.shape[0])


def second_kernel(
    place,
    diagonal,
    crossing,
    row_sums,
    col_sums,
    dir_here,
    dir_ahead,
    image_here,
    image_part,
    image_over,
    noise,
    totals,
    own,
    over,
    sums,
    res_here,
    res_ahead,
    half_here,
    half_ahead,
):
    step = pl.program_id(0)
    steps = pl.num_programs(0)
    strip = diagonal.shape[0]
    size = diagonal.shape[1]
    strips = size // strip
    live = place[1] > 0

    @pl.when(step == 0)
    def _():
        alpha = totals[:, 0:1] / totals[:, 1:2]
        here = dir_here[...] - alpha * image_here[...]
        ahead = dir_ahead[...] - alpha * (image_part[...] + image_over[...])
        res_here[...] = here
        res_ahead[...] = ahead
        half_here[...] = here.astype(bf16)
        half_ahead[...] = ahead.astype(bf16)
        own[...] = jnp.zeros_like(own)
        over[...] = jnp.zeros_like(over)

    for at in range(strips):

        @pl.when(step == at)
        def _(at=at):
            rows = slice(at * strip, (at + 1) * strip)
            tail = slice(at * strip, size)
            own[:, tail] += dot(half_here[:, rows], diagonal[:, tail])
            if at + 1 < strips:
                rest = slice((at + 1) * strip, size)
                own[:, rows] += dot_nt(half_here[:, rest], diagonal[:, rest])

    @pl.when((step >= strips) & live)
    def _():
        rows = pl.ds(pl.multiple_of((step - strips) * strip, strip), strip)
        own[:, rows] += dot_nt(half_ahead[...], crossing[...])
        over[...] += dot(half_here[:, rows], crossing[...])

    @pl.when(step == steps - 1)
    def _():
        here = res_here[...]
        ahead = res_ahead[...]
        mine = own[...] + (noise[...] + row_sums[0:1, :]) * here
        theirs = over[...] + col_sums[...] * ahead
        own[...] = mine
        over[...] = theirs
        own_form = row_dot(here, mine) + row_dot(ahead, theirs)
        cross_form = row_dot(dir_here[...], mine) + row_dot(dir_ahead[...], theirs)
        other_form = row_dot(here, image_here[...])
        sums[...] = lanes_of(
            [row_dot(here, here), own_form, cross_form, other_form], here.shape[0]
        )


def final_kernel(place, right_side, first, second, *rest):
    pieces = (len(rest) - 2) // 2
    images, images2 = rest[:pieces], rest[pieces : 2 * pieces]
    solved, residual = rest[2 * pieces :]
    step = pl.program_id(0)
    rho = first[:, 0:1]
    curvature = first[:, 1:2]
    alpha = rho / curvature
    new = second[:, 0:1]
    beta = new / rho
    curvature2 = (
        second[:, 1:2] + beta * (second[:, 2:3] + second[:, 3:4]) + beta * beta * curvature
    )
    alpha2 = new / curvature2
    for at in range(pieces):

        @pl.when(step == at)
        def _(at=at):
            begin = right_side[...]
            image = images[at][...]
            after = begin - alpha * image
            direction = after + beta * begin
            solved[...] = alpha * begin + alpha2 * direction
            residual[...] = after - alpha2 * (images2[at][...] + beta * image)


def params():
    return pltpu.CompilerParams(vmem_limit_bytes=VMEM_LIMIT)


def whole(shape):
    return pl.BlockSpec(shape, lambda *_: (0,) * len(shape))


def at_place(shape, shift=0, top=None):
    if top is None:
        return pl.BlockSpec(shape, lambda s, place: (0, place[0] + shift))
    return pl.BlockSpec(shape, lambda s, place: (0, jnp.minimum(place[0] + shift, top)))


def shaped(*shape, dtype=f32):
    return jax.ShapeDtypeStruct(shape, dtype)


SCALARS = pl.BlockSpec(memory_space=pltpu.SMEM)


def diagonal_call(place, signal, features, inv_scale, right_side, size):
    depth = features.shape[0]
    probes = right_side.shape[0]
    return pl.pallas_call(
        diagonal_kernel,
        grid_spec=pltpu.PrefetchScalarGridSpec(
            num_scalar_prefetch=1,
            grid=(size // STRIP,),
            in_specs=[
                SCALARS,
                at_place((depth, size)),
                whole((depth, 1)),
                at_place((probes, size)),
            ],
            out_specs=[
                pl.BlockSpec((STRIP, size), lambda s, place: (s, 0)),
                whole((probes, size)),
            ],
            scratch_shapes=[
                pltpu.VMEM((size, 4 * depth), bf16),
                pltpu.VMEM((4 * depth, size), bf16),
                pltpu.VMEM((probes, size), bf16),
            ],
        ),
        out_shape=[shaped(size, size, dtype=bf16), shaped(probes, size)],
        compiler_params=params(),
    )(place, signal, features, inv_scale, right_side)


def crossing_call(
    place, signal, features, sent_features, inv_scale, right_side, sent_dir, noise, diagonal, size
):
    depth = features.shape[0]
    probes = right_side.shape[0]
    top = features.shape[1] // size - 1
    block = whole((probes, size))
    return pl.pallas_call(
        crossing_kernel,
        grid_spec=pltpu.PrefetchScalarGridSpec(
            num_scalar_prefetch=1,
            grid=(size // STRIP,),
            in_specs=[
                SCALARS,
                at_place((depth, size)),
                at_place((depth, size), 1, top),
                whole((depth, size)),
                whole((depth, 1)),
                at_place((probes, size)),
                at_place((probes, size), 1, top),
                block,
                at_place((1, size)),
                block,
            ],
            out_specs=[
                pl.BlockSpec((STRIP, size), lambda s, place: (s, 0)),
                whole((8, size)),
                whole((1, size)),
                block,
                block,
                block,
                whole((probes, 128)),
            ],
            scratch_shapes=[
                pltpu.VMEM((size, 4 * depth), bf16),
                pltpu.VMEM((4 * depth, size), bf16),
                pltpu.VMEM((probes, size), bf16),
                pltpu.VMEM((probes, size), bf16),
                pltpu.VMEM((8, size), f32),
            ],
        ),
        out_shape=[
            shaped(size, size, dtype=bf16),
            shaped(8, size),
            shaped(1, size),
            shaped(probes, size),
            shaped(probes, size),
            shaped(probes, size),
            shaped(probes, 128),
        ],
        compiler_params=params(),
    )(
        place,
        signal,
        features,
        features,
        sent_features,
        inv_scale,
        right_side,
        right_side,
        sent_dir,
        noise,
        diagonal,
    )


def second_call(
    place,
    tile_here,
    tile_over,
    row_sums,
    col_sums,
    right_side,
    dir_ahead,
    image_here,
    image_part,
    image_over,
    noise,
    totals,
):
    size = tile_here.shape[0]
    probes = right_side.shape[0]
    strips = size // STRIP
    block = whole((probes, size))
    return pl.pallas_call(
        second_kernel,
        grid_spec=pltpu.PrefetchScalarGridSpec(
            num_scalar_prefetch=1,
            grid=(2 * strips,),
            in_specs=[
                pl.BlockSpec((STRIP, size), lambda s, place: (jnp.minimum(s, strips - 1), 0)),
                pl.BlockSpec((STRIP, size), lambda s, place: (jnp.maximum(s - strips, 0), 0)),
                whole((8, size)),
                whole((1, size)),
                at_place((probes, size)),
                block,
                block,
                block,
                block,
                at_place((1, size)),
                whole((probes, 128)),
            ],
            out_specs=[block, block, whole((probes, 128))],
            scratch_shapes=[
                pltpu.VMEM((probes, size), f32),
                pltpu.VMEM((probes, size), f32),
                pltpu.VMEM((probes, size), bf16),
                pltpu.VMEM((probes, size), bf16),
            ],
        ),
        out_shape=[shaped(probes, size), shaped(probes, size), shaped(probes, 128)],
        compiler_params=params(),
    )(
        place,
        tile_here,
        tile_over,
        row_sums,
        col_sums,
        right_side,
        dir_ahead,
        image_here,
        image_part,
        image_over,
        noise,
        totals,
    )


def final_call(place, right_side, first, second, images, images2, size):
    probes = right_side.shape[0]
    pieces = len(images)
    turned = pl.BlockSpec((probes, size), lambda s, place: (0, place[0] ^ s))
    piece = whole((probes, size))
    return pl.pallas_call(
        final_kernel,
        grid_spec=pltpu.PrefetchScalarGridSpec(
            num_scalar_prefetch=1,
            grid=(pieces,),
            in_specs=[turned, whole((probes, 128)), whole((probes, 128))] + [piece] * (2 * pieces),
            out_specs=[turned, turned],
        ),
        out_shape=[shaped(*right_side.shape), shaped(*right_side.shape)],
        compiler_params=params(),
    )(place, right_side, first, second, *images, *images2)


def moved(x, distance):
    count = lax.axis_size(BOTH[0]) * lax.axis_size(BOTH[1])
    route = [(i, i + distance) for i in range(count) if 0 <= i + distance < count]
    return lax.ppermute(x, BOTH, route)


def exchanged(x, axes, distance):
    count = math.prod(lax.axis_size(a) for a in axes)
    return lax.ppermute(x, axes, [(i, i ^ distance) for i in range(count)])


def summed_over_all(x):
    count = lax.axis_size(BOTH[0]) * lax.axis_size(BOTH[1])
    distance = 1
    while distance < count:
        x = x + exchanged(x, BOTH, distance)
        distance *= 2
    return x


def gathered(x):
    members = lax.axis_size("pair")
    pieces = {0: x}
    distance = members // 2
    while distance:
        for at in list(pieces):
            pieces[at ^ distance] = exchanged(pieces[at], ("pair",), distance)
        distance //= 2
    return [pieces[at] for at in range(members)]


def sent_from_next_group(x, spread):
    members = lax.axis_size("pair")
    route = [
        ((g + 1) * members + spread % members, g * members + members - 1)
        for g in range(lax.axis_size("blk") - 1)
    ]
    return lax.ppermute(x, BOTH, route)


def own_block_body(features, inv_scale, signal, noise_var, right_side, block_pairs):
    members = lax.axis_size("pair")
    size = features.shape[1] // members
    half_depth = features.shape[0] // 2
    mine = lax.axis_index("pair").astype(jnp.int32)
    base = lax.axis_index("blk").astype(jnp.int32) * members

    sent_dir = sent_from_next_group(right_side[:, :size], 2)
    sent_features = jnp.concatenate(
        [
            sent_from_next_group(features[:half_depth, :size], 3),
            sent_from_next_group(features[half_depth:, :size], 1),
        ],
        axis=0,
    )
    wanted = base + jnp.arange(members, dtype=jnp.int32)
    listed = jnp.any(
        (block_pairs[:, 0:1] == wanted[None, :]) & (block_pairs[:, 1:2] == wanted[None, :] + 1),
        axis=0,
    )
    listed = jnp.where(listed, 1.0, 0.0).astype(f32)[None, :]
    anywhere = sum(
        lax.ppermute(listed, "pair", [(i, (i + k) % members) for i in range(members)])
        for k in range(1, members)
    )
    anywhere = anywhere + listed
    live = jnp.sum(jnp.where(jnp.arange(members) == mine, anywhere[0], 0.0)) > 0.0

    scale = inv_scale[:, None]
    noise = noise_var[None, :]
    spot = jnp.stack([mine, mine, mine])
    place = jnp.stack([mine, live.astype(jnp.int32), (mine == members - 1).astype(jnp.int32)])

    tile_here, diagonal = diagonal_call(spot, signal, features, scale, right_side, size)
    tile_over, row_sums, col_sums, own, over, dir_ahead, sums = crossing_call(
        place,
        signal,
        features,
        sent_features,
        scale,
        right_side,
        sent_dir,
        noise,
        diagonal,
        size,
    )
    image_part = moved(own, -1)
    image = own + moved(over, 1)
    first = summed_over_all(sums)
    own2, over2, sums2 = second_call(
        place,
        tile_here,
        tile_over,
        row_sums,
        col_sums,
        right_side,
        dir_ahead,
        image,
        image_part,
        over,
        noise,
        first,
    )
    images = gathered(image)
    images2 = gathered(own2 + moved(over2, 1))
    second = summed_over_all(sums2)
    return tuple(final_call(place, right_side, first, second, images, images2, size))


def passed_along(block, axis, distance):
    devices = range(lax.axis_size(axis))
    route = [(i - distance, i) for i in devices if i - distance in devices]
    return lax.ppermute(block, axis, route)


def kernel_tile(left_scaled, right_scaled, amplitude):
    cross = lax.dot_general(
        left_scaled,
        right_scaled,
        (((0,), (0,)), ((), ())),
        precision=lax.Precision.HIGHEST,
        preferred_element_type=jnp.float32,
    )
    left_norms = jnp.sum(left_scaled * left_scaled, axis=0)
    right_norms = jnp.sum(right_scaled * right_scaled, axis=0)
    squared = (left_norms[:, None] + right_norms[None, :] - 2.0 * cross) / left_scaled.shape[0]
    distance = jnp.sqrt(jnp.maximum(squared, 0.0))
    stretched = root_three * distance
    ratio = distance / taper_radius
    taper = jnp.maximum(1.0 - ratio, 0.0) ** 4 * (1.0 + 4.0 * ratio)
    return amplitude * (1.0 + stretched) * jnp.exp(-stretched) * taper


def block_terms(left_scaled, right_scaled, left_dir, right_dir, amplitude):
    block_rows = left_scaled.shape[1]
    row_step = min(512, block_rows)
    left_half = left_dir.astype(jnp.bfloat16)
    right_half = right_dir.astype(jnp.bfloat16)

    def rows_visit(position, carried):
        toward_left, toward_right, row_sums, col_sums = carried
        offset = position * row_step
        kernel_rows = kernel_tile(
            lax.dynamic_slice_in_dim(left_scaled, offset, row_step, 1), right_scaled, amplitude
        )
        rows_half = kernel_rows.astype(jnp.bfloat16)
        product = lax.dot_general(
            right_half, rows_half, (((1,), (1,)), ((), ())), preferred_element_type=jnp.float32
        )
        toward_left = lax.dynamic_update_slice_in_dim(toward_left, product, offset, 1)
        toward_right = toward_right + jnp.dot(
            lax.dynamic_slice_in_dim(left_half, offset, row_step, 1),
            rows_half,
            preferred_element_type=jnp.float32,
        )
        row_sums = lax.dynamic_update_slice_in_dim(
            row_sums, jnp.sum(kernel_rows, axis=1), offset, 0
        )
        col_sums = col_sums + jnp.sum(kernel_rows, axis=0)
        return (toward_left, toward_right, row_sums, col_sums)

    zeros_dir = jnp.zeros(left_dir.shape, jnp.float32)
    zeros_row = jnp.zeros((block_rows,), jnp.float32)
    return lax.fori_loop(
        0, block_rows // row_step, rows_visit, (zeros_dir, zeros_dir, zeros_row, zeros_row)
    )


def body(features, inv_scale, signal, noise_var, right_side, block_pairs):
    local_rows = features.shape[1]
    blocks_here = local_rows // BS
    amplitude = signal[0]
    scaled = features * inv_scale[:, None]
    beyond = passed_along(scaled[:, :BS], "blk", -1)
    reach_scaled = jnp.concatenate([scaled, beyond], axis=1)
    base_block = lax.axis_index("blk") * blocks_here
    members = lax.axis_size("pair")
    listing = lax.all_gather(block_pairs, "pair", axis=0, tiled=True)
    living = (listing[:, 0] >= 0).astype(jnp.int32)
    ranked = jnp.cumsum(living) - living
    wanted = lax.axis_index("pair") + members * jnp.arange(block_pairs.shape[0], dtype=jnp.int32)
    matched = (ranked[None, :] == wanted[:, None]) & (living[None, :] > 0)
    chosen = jnp.sum(jnp.where(matched[:, :, None], listing[None, :, :], 0), axis=1)
    my_pairs = jnp.where(jnp.any(matched, axis=1)[:, None], chosen, -1)
    active = jnp.maximum((jnp.sum(living) - lax.axis_index("pair") + members - 1) // members, 0)
    row_local = my_pairs[:, 0] - base_block
    col_local = my_pairs[:, 1] - base_block
    solution = jnp.zeros_like(right_side)
    residual = right_side
    direction = right_side
    norm_now = lax.psum(jnp.sum(residual * residual, axis=1), "blk")
    for iteration in range(ITERS):
        ahead_dir = passed_along(direction[:, :BS], "blk", -1)
        reach_dir = jnp.concatenate([direction, ahead_dir], axis=1)

        def visit(slot_index, summed):
            row_start = row_local[slot_index] * BS
            col_start = col_local[slot_index] * BS
            crossing = (row_local[slot_index] != col_local[slot_index]).astype(jnp.float32)
            left_dir = lax.dynamic_slice_in_dim(reach_dir, row_start, BS, 1)
            right_dir = lax.dynamic_slice_in_dim(reach_dir, col_start, BS, 1)
            toward_left, toward_right, row_sums, col_sums = block_terms(
                lax.dynamic_slice_in_dim(reach_scaled, row_start, BS, 1),
                lax.dynamic_slice_in_dim(reach_scaled, col_start, BS, 1),
                left_dir,
                right_dir,
                amplitude,
            )
            term_left = toward_left + crossing * row_sums[None, :] * left_dir
            term_right = crossing * (toward_right + col_sums[None, :] * right_dir)
            summed = lax.dynamic_update_slice_in_dim(
                summed, lax.dynamic_slice_in_dim(summed, row_start, BS, 1) + term_left, row_start, 1
            )
            summed = lax.dynamic_update_slice_in_dim(
                summed,
                lax.dynamic_slice_in_dim(summed, col_start, BS, 1) + term_right,
                col_start,
                1,
            )
            return summed

        summed = lax.fori_loop(0, active, visit, jnp.zeros(reach_dir.shape, jnp.float32))
        own_part = summed[:, :local_rows]
        next_part = summed[:, local_rows:]
        own_sum, next_sum = lax.psum((own_part, next_part), "pair")
        entering = passed_along(next_sum, "blk", 1)
        coupled = jnp.concatenate([own_sum[:, :BS] + entering, own_sum[:, BS:]], axis=1)
        applied = noise_var[None, :] * direction + coupled
        last_turn = iteration + 1 == ITERS
        curvature = lax.psum(jnp.sum(direction * applied, axis=1), "blk")
        step_size = norm_now / curvature
        solution = solution + step_size[:, None] * direction
        residual = residual - step_size[:, None] * applied
        if not last_turn:
            norm_next = lax.psum(jnp.sum(residual * residual, axis=1), "blk")
            direction = residual + (norm_next / norm_now)[:, None] * direction
            norm_now = norm_next
    return (solution, residual)


def solution(mesh):
    members = mesh.shape["pair"]
    groups = mesh.shape["blk"]

    def chosen(features, *rest):
        one_block_each = features.shape[1] == members * BS and BS % STRIP == 0
        powers = members & (members - 1) == 0 and groups & (groups - 1) == 0
        each = own_block_body if one_block_each and powers else body
        return each(features, *rest)

    placed = (P(None, "blk"), P(), P(), P("blk"), P(None, "blk"), P(("blk", "pair"), None))
    return jax.shard_map(
        chosen,
        mesh=mesh,
        in_specs=placed,
        out_specs=(P(None, "blk"), P(None, "blk")),
        check_vma=False,
    )
```

```python
import functools
import math

import jax
import jax.numpy as jnp
from jax import lax
from jax.experimental import pallas as pl
from jax.experimental.pallas import tpu as pltpu
from jax.sharding import PartitionSpec as P

BS = 2048
ITERS = 2

f32 = jnp.float32
bf16 = jnp.bfloat16
root_three = 1.7320508075688772
taper_radius = 2.0
BOTH = ("blk", "pair")
NT = (((1,), (1,)), ((), ()))
CHUNK = 256

RATE = taper_radius * root_three * math.log2(math.e)
NEAR = math.log2(math.e)
FAR = RATE / 4.0
UNIT = NEAR * FAR * RATE**4


def parts_of(x):
    high = x.astype(bf16)
    rest = x - high.astype(f32)
    middle = rest.astype(bf16)
    low = (rest - middle.astype(f32)).astype(bf16)
    return high, middle, low


def norm_parts(points, axis, first):
    norms = jnp.sum(points * points, axis=axis, keepdims=True)
    high, middle, low = (x.astype(f32) for x in parts_of(norms))
    at = lax.broadcasted_iota(jnp.int32, points.shape, axis)
    ones = jnp.where(at < 6, 1.0, 0.0)
    placed = jnp.where(at == first + 2, low, ones)
    placed = jnp.where(at == first + 1, middle, placed)
    return jnp.where(at == first, high, placed).astype(bf16)


def left_parts(points):
    turned = points.T
    high, middle, _ = parts_of(turned)
    return jnp.concatenate([high, high, middle, norm_parts(turned, 1, 0)], axis=1)


def right_parts(points):
    high, middle, _ = parts_of(-2.0 * points)
    return jnp.concatenate([high, middle, high, norm_parts(points, 0, 3)], axis=0)


def points_of(features, inv_scale):
    depth = features.shape[0]
    scale = jnp.broadcast_to(inv_scale, (8, depth)).T[:, 0:1]
    return features * scale * (RATE / (taper_radius * math.sqrt(depth)))


def level_of(signal):
    return jnp.log2(jnp.full((1, CHUNK), signal * (1.0 / UNIT), f32))


def kernel_values(squared, level):
    squared = jnp.maximum(squared, 1e-30)
    s = squared * lax.rsqrt(squared)
    decay = jnp.exp2(level - s)
    u = jnp.maximum(RATE - s, 0.0)
    u2 = u * u
    return ((s + NEAR) * (s + FAR) * decay) * (u2 * u2)


def dot(a, b):
    return jnp.dot(a, b, preferred_element_type=f32)


def dot_nt(a, b):
    return lax.dot_general(a, b, NT, preferred_element_type=f32)


def cut(at):
    return slice(at * CHUNK, (at + 1) * CHUNK)


def two_sum(a, b):
    total = a + b
    back = total - a
    return total, (a - (total - back)) + (b - back)


def two_product(a, b):
    def halves(x):
        big = x * 4097.0
        high = big - (big - x)
        return high, x - high

    product = a * b
    a_high, a_low = halves(a)
    b_high, b_low = halves(b)
    error = ((a_high * b_high - product) + a_high * b_low + a_low * b_high) + a_low * b_low
    return product, error


def plus(x, y):
    total, error = two_sum(x[0], y[0])
    return two_sum(total, error + (x[1] + y[1]))


def times(x, factor):
    product, error = two_product(x[0], factor)
    return two_sum(product, error + x[1] * factor)


def lane_tiles_sum(x):
    high = x[:, 0:128]
    low = jnp.zeros_like(high)
    for at in range(128, x.shape[1], 128):
        high, error = two_sum(high, x[:, at : at + 128])
        low = low + error
    return high, low


def lanes_sum(high, low):
    shift = 64
    while shift:
        high, error = two_sum(high, pltpu.roll(high, shift, 1))
        low = low + pltpu.roll(low, shift, 1) + error
        shift //= 2
    return high, low


def diagonal_kernel(
    signal, features, inv_scale, right_side, tile, own, left, direction, raw, right, half, ahead, sems
):
    size = tile.shape[0]
    mine = lax.axis_index("pair")
    block = pl.ds(pl.multiple_of(mine * size, size), size)
    get_features = pltpu.make_async_copy(features.at[:, block], raw, sems.at[0])
    get_direction = pltpu.make_async_copy(right_side.at[:, block], direction, sems.at[1])
    get_features.start()
    get_direction.start()
    level = level_of(signal[0])
    get_features.wait()
    points = points_of(raw[...], inv_scale[...])
    left[...] = left_parts(points)
    right[...] = right_parts(points)
    get_direction.wait()
    half[...] = direction[...].astype(bf16)
    own[...] = jnp.zeros_like(own)

    count = size // CHUNK
    order = [(row, col) for row in range(count) for col in range(row, count)]

    def argument(k):
        row, col = order[k]
        ahead[k % 2] = dot(left[cut(row), :], right[:, cut(col)])

    def product(k):
        row, col = order[k]
        block = tile[cut(row), cut(col)]
        own[:, cut(col)] += dot(half[:, cut(row)], block)
        if col > row:
            own[:, cut(row)] += dot_nt(half[:, cut(col)], block)

    argument(0)
    for k, (row, col) in enumerate(order):
        if k + 1 < len(order):
            argument(k + 1)
        if k:
            product(k - 1)
        tile[cut(row), cut(col)] = kernel_values(ahead[k % 2], level).astype(bf16)
    product(len(order) - 1)


def crossing_kernel(
    signal,
    flags,
    features,
    sent_top,
    sent_bottom,
    inv_scale,
    left,
    right_side,
    sent_dir,
    direction,
    noise,
    diagonal,
    tile,
    row_sums,
    col_sums,
    own,
    over,
    next_dir,
    raw,
    right,
    half,
    half_next,
    ahead,
    col_part,
    row_part,
    sems,
):
    size = tile.shape[0]
    members = lax.axis_size("pair")
    mine = lax.axis_index("pair")
    last = mine == members - 1
    top = raw.shape[0] // 2

    @pl.when(last)
    def _():
        copies = [
            pltpu.make_async_copy(sent_top, raw.at[:top], sems.at[0]),
            pltpu.make_async_copy(sent_bottom, raw.at[top:], sems.at[1]),
            pltpu.make_async_copy(sent_dir, next_dir, sems.at[2]),
        ]
        for copy in copies:
            copy.start()
        for copy in copies:
            copy.wait()

    @pl.when(jnp.logical_not(last))
    def _():
        block = pl.ds(pl.multiple_of((mine + 1) * size, size), size)
        copies = [
            pltpu.make_async_copy(features.at[:, block], raw, sems.at[0]),
            pltpu.make_async_copy(right_side.at[:, block], next_dir, sems.at[1]),
        ]
        for copy in copies:
            copy.start()
        for copy in copies:
            copy.wait()

    listed = flags[0, mine]
    for k in range(1, members):
        listed = listed + flags[k, mine]
    live = listed > 0.0
    own[...] = jnp.zeros_like(own)
    over[...] = jnp.zeros_like(over)
    row_sums[...] = jnp.zeros_like(row_sums)
    col_sums[...] = jnp.zeros_like(col_sums)

    @pl.when(live)
    def _():
        level = level_of(signal[0])
        right[...] = right_parts(points_of(raw[...], inv_scale[...]))
        half[...] = direction[...].astype(bf16)
        half_next[...] = next_dir[...].astype(bf16)
        col_part[...] = jnp.zeros_like(col_part)
        row_part[...] = jnp.zeros_like(row_part)
        count = size // CHUNK
        order = [(row, col) for row in range(count) for col in range(count)]

        def argument(k):
            row, col = order[k]
            ahead[k % 2] = dot(left[cut(row), :], right[:, cut(col)])

        def product(k):
            row, col = order[k]
            block = tile[cut(row), cut(col)]
            over[:, cut(col)] += dot(half[:, cut(row)], block)
            own[:, cut(row)] += dot_nt(half_next[:, cut(col)], block)

        argument(0)
        for k, (row, col) in enumerate(order):
            if k + 1 < len(order):
                argument(k + 1)
            if k:
                product(k - 1)
            values = kernel_values(ahead[k % 2], level)
            tile[cut(row), cut(col)] = values.astype(bf16)
            col_part[:, cut(col)] += jnp.sum(values.reshape(CHUNK // 8, 8, CHUNK), axis=0)
            along = values[:, 0:128]
            for lane in range(128, CHUNK, 128):
                along = along + values[:, lane : lane + 128]
            row_part[cut(row), :] += along
        product(len(order) - 1)
        row_sums[...] = lax.dot_general(
            jnp.ones((8, 128), f32),
            row_part[...],
            NT,
            precision=lax.Precision.HIGHEST,
            preferred_element_type=f32,
        )
        col_sums[...] = jnp.sum(col_part[...], axis=0, keepdims=True)

    own[...] += diagonal[...] + (noise[...] + row_sums[0:1, :]) * direction[...]
    over[...] += col_sums[...] * next_dir[...]


def both_parts(x):
    high = x.astype(bf16)
    return jnp.concatenate([high, (x - high.astype(f32)).astype(bf16)], axis=0)


def folded(x):
    half = x.shape[0] // 2
    return x[:half] + x[half:]


def second_crossing_kernel(flags, tile, row_sums, col_sums, image, part, over, own2, over2):
    members = lax.axis_size("pair")
    mine = lax.axis_index("pair")
    listed = flags[0, mine]
    for k in range(1, members):
        listed = listed + flags[k, mine]
    live = listed > 0.0

    @pl.when(live)
    def _():
        here = image[...]
        there = part[...] + over[...]
        over2[...] = folded(dot(both_parts(here), tile[...])) + col_sums[...] * there
        own2[...] = folded(dot_nt(both_parts(there), tile[...])) + row_sums[0:1, :] * here

    @pl.when(jnp.logical_not(live))
    def _():
        over2[...] = jnp.zeros_like(over2)
        own2[...] = jnp.zeros_like(own2)


def second_diagonal_kernel(tile, noise, direction, next_dir, image, part, over, cross, over2, own2, sums, both):
    size = tile.shape[0]
    here = image[...]
    both[...] = both_parts(here)
    own2[...] = cross[...] + noise[...] * here
    wide = CHUNK
    for at in range(0, size, wide):
        rows = slice(at, at + wide)
        tail = slice(at, size)
        rest = slice(at + wide, size)
        own2[:, tail] += folded(dot(both[:, rows], tile[rows, tail]))
        if at + wide < size:
            own2[:, rows] += folded(dot_nt(both[:, rest], tile[rows, rest]))
    begin = direction[...]
    mine = own2[...]
    theirs = over2[...]
    there = part[...] + over[...]
    squares = here * here
    forms = [
        begin * begin,
        begin * here,
        squares,
        squares + begin * mine + next_dir[...] * theirs,
        here * mine + there * theirs,
    ]
    pairs = [lane_tiles_sum(x) for x in forms]
    probes = begin.shape[0]
    high, low = lanes_sum(
        jnp.concatenate([x for x, _ in pairs], axis=0), jnp.concatenate([x for _, x in pairs], axis=0)
    )
    lane = lax.broadcasted_iota(jnp.int32, (probes, 128), 1)
    for part_at, values in enumerate((high, low)):
        out = jnp.zeros((probes, 128), f32)
        for k in range(len(forms)):
            out = jnp.where(lane == k, values[k * probes : (k + 1) * probes], out)
        sums[part_at * probes : (part_at + 1) * probes, :] = out


def final_kernel(sums, right_side, *rest):
    members = lax.axis_size("pair")
    images, images2 = rest[:members], rest[members : 2 * members]
    solution_out, residual_out, begins, solved, left_over, get_sems, put_sems = rest[2 * members :]
    probes, size = images[0].shape
    mine = lax.axis_index("pair")

    def block(k):
        return pl.ds(pl.multiple_of((mine ^ k) * size, size), size)

    gets = [
        pltpu.make_async_copy(right_side.at[:, block(k)], begins.at[k], get_sems.at[k])
        for k in range(members)
    ]
    for get in gets:
        get.start()

    def total(k):
        return sums[:probes, k : k + 1], sums[probes:, k : k + 1]

    square, form, image_square, mixed, image_form = (total(k) for k in range(5))
    alpha = square[0] / form[0]
    new = plus(plus(square, times(form, -2.0 * alpha)), times(times(image_square, alpha), alpha))[0]
    beta = new / square[0]
    less = times(mixed, -alpha)
    curvature = plus(plus(form, less), times(times(image_form, alpha), alpha))
    curvature = plus(curvature, times(plus(times(form, 2.0), less), beta))
    curvature = plus(curvature, times(times(form, beta), beta))
    alpha2 = new / curvature[0]
    puts = []
    for k in range(members):
        gets[k].wait()
        begin = begins[k]
        image = images[k][...]
        after = begin - alpha * image
        solved[k] = alpha * begin + alpha2 * (after + beta * begin)
        left_over[k] = after - alpha2 * ((image - alpha * images2[k][...]) + beta * image)
        for at, (source, target) in enumerate(((solved, solution_out), (left_over, residual_out))):
            puts.append(
                pltpu.make_async_copy(source.at[k], target.at[:, block(k)], put_sems.at[at, k])
            )
            puts[-1].start()
    for put in puts:
        put.wait()


def params(mebibytes):
    return pltpu.CompilerParams(vmem_limit_bytes=mebibytes << 20)


def shaped(*shape):
    return jax.ShapeDtypeStruct(shape, f32)


VMEM = pl.BlockSpec(memory_space=pltpu.VMEM)
SMEM = pl.BlockSpec(memory_space=pltpu.SMEM)
HBM = pl.BlockSpec(memory_space=pltpu.HBM)
ANY = pl.BlockSpec(memory_space=pl.ANY)


def diagonal_call(signal, features, inv_scale, right_side, size):
    depth = features.shape[0]
    probes = right_side.shape[0]
    return pl.pallas_call(
        diagonal_kernel,
        in_specs=[SMEM, HBM, VMEM, HBM],
        out_specs=[VMEM] * 4,
        out_shape=[
            pltpu.VMEM((size, size), bf16),
            shaped(probes, size),
            pltpu.VMEM((size, 4 * depth), bf16),
            pltpu.VMEM((probes, size), f32),
        ],
        scratch_shapes=[
            pltpu.VMEM((depth, size), f32),
            pltpu.VMEM((4 * depth, size), bf16),
            pltpu.VMEM((probes, size), bf16),
            pltpu.VMEM((2, CHUNK, CHUNK), f32),
            pltpu.SemaphoreType.DMA((2,)),
        ],
        compiler_params=params(16),
    )(signal, features, inv_scale, right_side)


def crossing_call(
    signal, flags, features, sent, inv_scale, left, right_side, sent_dir, direction, noise, diagonal
):
    depth = features.shape[0]
    probes, size = direction.shape
    return pl.pallas_call(
        crossing_kernel,
        in_specs=[SMEM, SMEM, HBM, ANY, ANY, VMEM, VMEM, HBM, ANY, VMEM, VMEM, VMEM],
        out_specs=[VMEM] * 5 + [VMEM],
        out_shape=[
            pltpu.VMEM((size, size), bf16),
            shaped(8, size),
            shaped(1, size),
            shaped(probes, size),
            shaped(probes, size),
            shaped(probes, size),
        ],
        scratch_shapes=[
            pltpu.VMEM((depth, size), f32),
            pltpu.VMEM((4 * depth, size), bf16),
            pltpu.VMEM((probes, size), bf16),
            pltpu.VMEM((probes, size), bf16),
            pltpu.VMEM((2, CHUNK, CHUNK), f32),
            pltpu.VMEM((8, size), f32),
            pltpu.VMEM((size, 128), f32),
            pltpu.SemaphoreType.DMA((3,)),
        ],
        compiler_params=params(16),
    )(
        signal,
        flags,
        features,
        *sent,
        inv_scale,
        left,
        right_side,
        sent_dir,
        direction,
        noise,
        diagonal,
    )


def second_crossing_call(flags, tile, row_sums, col_sums, image, part, over):
    return pl.pallas_call(
        second_crossing_kernel,
        in_specs=[SMEM] + [VMEM] * 6,
        out_specs=[VMEM] * 2,
        out_shape=[shaped(*image.shape)] * 2,
        compiler_params=params(16),
    )(flags, tile, row_sums, col_sums, image, part, over)


def second_diagonal_call(tile, noise, direction, next_dir, image, part, over, cross, over2):
    probes, size = image.shape
    return pl.pallas_call(
        second_diagonal_kernel,
        in_specs=[VMEM] * 9,
        out_specs=[VMEM] * 2,
        out_shape=[shaped(probes, size), shaped(2 * probes, 128)],
        scratch_shapes=[pltpu.VMEM((2 * probes, size), bf16)],
        compiler_params=params(16),
    )(tile, noise, direction, next_dir, image, part, over, cross, over2)


def final_call(sums, right_side, images, images2):
    probes, size = images[0].shape
    members = len(images)
    return pl.pallas_call(
        final_kernel,
        in_specs=[VMEM, HBM] + [VMEM] * (2 * members),
        out_specs=[HBM, HBM],
        out_shape=[shaped(*right_side.shape)] * 2,
        scratch_shapes=[
            pltpu.VMEM((members, probes, size), f32),
            pltpu.VMEM((members, probes, size), f32),
            pltpu.VMEM((members, probes, size), f32),
            pltpu.SemaphoreType.DMA((members,)),
            pltpu.SemaphoreType.DMA((2, members)),
        ],
        compiler_params=params(16),
    )(sums, right_side, *images, *images2)


def moved(x, distance):
    count = lax.axis_size(BOTH[0]) * lax.axis_size(BOTH[1])
    route = [(i, i + distance) for i in range(count) if 0 <= i + distance < count]
    return lax.ppermute(x, BOTH, route)


def exchanged(x, distance):
    count = lax.axis_size(BOTH[0]) * lax.axis_size(BOTH[1])
    return lax.ppermute(x, BOTH, [(i, i ^ distance) for i in range(count)])


def joined(x, distance):
    other = exchanged(x, distance)
    half = x.shape[0] // 2
    high, error = two_sum(x[:half], other[:half])
    return jnp.concatenate([high, (x[half:] + other[half:]) + error], axis=0)


def sent_from_next_group(x, spread):
    members = lax.axis_size("pair")
    route = [
        ((g + 1) * members + spread % members, g * members + members - 1)
        for g in range(lax.axis_size("blk") - 1)
    ]
    return lax.ppermute(x, BOTH, route)


def own_block_body(features, inv_scale, signal, noise_var, right_side, block_pairs):
    members = lax.axis_size("pair")
    groups = lax.axis_size("blk")
    size = features.shape[1] // members
    half_depth = features.shape[0] // 2
    mine = lax.axis_index("pair").astype(jnp.int32)
    base = lax.axis_index("blk").astype(jnp.int32) * members

    sent = (
        sent_from_next_group(features[:half_depth, :size], 3),
        sent_from_next_group(features[half_depth:, :size], 1),
    )
    sent_dir = sent_from_next_group(right_side[:, :size], 2)
    wanted = (base + jnp.arange(members, dtype=jnp.int32))[None, :]
    found = (block_pairs[:, 0:1] == wanted) & (block_pairs[:, 1:2] == wanted + 1)
    found = jnp.sum(jnp.where(found, 1.0, 0.0).astype(f32), axis=0, keepdims=True)
    flags = jnp.concatenate(
        [found]
        + [
            lax.ppermute(found, "pair", [(i, (i + k) % members) for i in range(members)])
            for k in range(1, members)
        ],
        axis=0,
    )
    scale = inv_scale[None, :]
    noise = lax.dynamic_slice_in_dim(noise_var, mine * size, size, 0)[None, :]

    tile, diagonal, left, direction = diagonal_call(signal, features, scale, right_side, size)
    cross_tile, row_sums, col_sums, own, over, next_dir = crossing_call(
        signal,
        flags,
        features,
        sent,
        scale,
        left,
        right_side,
        sent_dir,
        direction,
        noise,
        diagonal,
    )
    part = moved(own, -1)
    image = own + moved(over, 1)
    images = {0: image}
    distance = members // 2
    if distance:
        images[distance] = exchanged(image, distance)
    cross, over2 = second_crossing_call(flags, cross_tile, row_sums, col_sums, image, part, over)
    own2, sums = second_diagonal_call(
        tile, noise, direction, next_dir, image, part, over, cross, over2
    )
    step = members
    while step < members * groups:
        sums = joined(sums, step)
        step *= 2
    images2 = {0: own2 + moved(over2, 1)}
    while distance:
        sums = joined(sums, distance)
        for held in (images, images2):
            for at in list(held):
                if at ^ distance not in held:
                    held[at ^ distance] = exchanged(held[at], distance)
        distance //= 2
    return tuple(
        final_call(
            sums,
            right_side,
            [images[k] for k in range(members)],
            [images2[k] for k in range(members)],
        )
    )


def passed_along(block, axis, distance):
    devices = range(lax.axis_size(axis))
    route = [(i - distance, i) for i in devices if i - distance in devices]
    return lax.ppermute(block, axis, route)


def kernel_tile(left_scaled, right_scaled, amplitude):
    cross = lax.dot_general(
        left_scaled,
        right_scaled,
        (((0,), (0,)), ((), ())),
        precision=lax.Precision.HIGHEST,
        preferred_element_type=jnp.float32,
    )
    left_norms = jnp.sum(left_scaled * left_scaled, axis=0)
    right_norms = jnp.sum(right_scaled * right_scaled, axis=0)
    squared = (left_norms[:, None] + right_norms[None, :] - 2.0 * cross) / left_scaled.shape[0]
    distance = jnp.sqrt(jnp.maximum(squared, 0.0))
    stretched = root_three * distance
    ratio = distance / taper_radius
    taper = jnp.maximum(1.0 - ratio, 0.0) ** 4 * (1.0 + 4.0 * ratio)
    return amplitude * (1.0 + stretched) * jnp.exp(-stretched) * taper


def block_terms(left_scaled, right_scaled, left_dir, right_dir, amplitude):
    block_rows = left_scaled.shape[1]
    row_step = min(512, block_rows)
    left_half = left_dir.astype(jnp.bfloat16)
    right_half = right_dir.astype(jnp.bfloat16)

    def rows_visit(position, carried):
        toward_left, toward_right, row_sums, col_sums = carried
        offset = position * row_step
        kernel_rows = kernel_tile(
            lax.dynamic_slice_in_dim(left_scaled, offset, row_step, 1), right_scaled, amplitude
        )
        rows_half = kernel_rows.astype(jnp.bfloat16)
        product = lax.dot_general(
            right_half, rows_half, (((1,), (1,)), ((), ())), preferred_element_type=jnp.float32
        )
        toward_left = lax.dynamic_update_slice_in_dim(toward_left, product, offset, 1)
        toward_right = toward_right + jnp.dot(
            lax.dynamic_slice_in_dim(left_half, offset, row_step, 1),
            rows_half,
            preferred_element_type=jnp.float32,
        )
        row_sums = lax.dynamic_update_slice_in_dim(
            row_sums, jnp.sum(kernel_rows, axis=1), offset, 0
        )
        col_sums = col_sums + jnp.sum(kernel_rows, axis=0)
        return (toward_left, toward_right, row_sums, col_sums)

    zeros_dir = jnp.zeros(left_dir.shape, jnp.float32)
    zeros_row = jnp.zeros((block_rows,), jnp.float32)
    return lax.fori_loop(
        0, block_rows // row_step, rows_visit, (zeros_dir, zeros_dir, zeros_row, zeros_row)
    )


def body(features, inv_scale, signal, noise_var, right_side, block_pairs):
    local_rows = features.shape[1]
    blocks_here = local_rows // BS
    amplitude = signal[0]
    scaled = features * inv_scale[:, None]
    beyond = passed_along(scaled[:, :BS], "blk", -1)
    reach_scaled = jnp.concatenate([scaled, beyond], axis=1)
    base_block = lax.axis_index("blk") * blocks_here
    members = lax.axis_size("pair")
    listing = lax.all_gather(block_pairs, "pair", axis=0, tiled=True)
    living = (listing[:, 0] >= 0).astype(jnp.int32)
    ranked = jnp.cumsum(living) - living
    wanted = lax.axis_index("pair") + members * jnp.arange(block_pairs.shape[0], dtype=jnp.int32)
    matched = (ranked[None, :] == wanted[:, None]) & (living[None, :] > 0)
    chosen = jnp.sum(jnp.where(matched[:, :, None], listing[None, :, :], 0), axis=1)
    my_pairs = jnp.where(jnp.any(matched, axis=1)[:, None], chosen, -1)
    active = jnp.maximum((jnp.sum(living) - lax.axis_index("pair") + members - 1) // members, 0)
    row_local = my_pairs[:, 0] - base_block
    col_local = my_pairs[:, 1] - base_block
    solution = jnp.zeros_like(right_side)
    residual = right_side
    direction = right_side
    norm_now = lax.psum(jnp.sum(residual * residual, axis=1), "blk")
    for iteration in range(ITERS):
        ahead_dir = passed_along(direction[:, :BS], "blk", -1)
        reach_dir = jnp.concatenate([direction, ahead_dir], axis=1)

        def visit(slot_index, summed):
            row_start = row_local[slot_index] * BS
            col_start = col_local[slot_index] * BS
            crossing = (row_local[slot_index] != col_local[slot_index]).astype(jnp.float32)
            left_dir = lax.dynamic_slice_in_dim(reach_dir, row_start, BS, 1)
            right_dir = lax.dynamic_slice_in_dim(reach_dir, col_start, BS, 1)
            toward_left, toward_right, row_sums, col_sums = block_terms(
                lax.dynamic_slice_in_dim(reach_scaled, row_start, BS, 1),
                lax.dynamic_slice_in_dim(reach_scaled, col_start, BS, 1),
                left_dir,
                right_dir,
                amplitude,
            )
            term_left = toward_left + crossing * row_sums[None, :] * left_dir
            term_right = crossing * (toward_right + col_sums[None, :] * right_dir)
            summed = lax.dynamic_update_slice_in_dim(
                summed, lax.dynamic_slice_in_dim(summed, row_start, BS, 1) + term_left, row_start, 1
            )
            summed = lax.dynamic_update_slice_in_dim(
                summed,
                lax.dynamic_slice_in_dim(summed, col_start, BS, 1) + term_right,
                col_start,
                1,
            )
            return summed

        summed = lax.fori_loop(0, active, visit, jnp.zeros(reach_dir.shape, jnp.float32))
        own_part = summed[:, :local_rows]
        next_part = summed[:, local_rows:]
        own_sum, next_sum = lax.psum((own_part, next_part), "pair")
        entering = passed_along(next_sum, "blk", 1)
        coupled = jnp.concatenate([own_sum[:, :BS] + entering, own_sum[:, BS:]], axis=1)
        applied = noise_var[None, :] * direction + coupled
        last_turn = iteration + 1 == ITERS
        curvature = lax.psum(jnp.sum(direction * applied, axis=1), "blk")
        step_size = norm_now / curvature
        solution = solution + step_size[:, None] * direction
        residual = residual - step_size[:, None] * applied
        if not last_turn:
            norm_next = lax.psum(jnp.sum(residual * residual, axis=1), "blk")
            direction = residual + (norm_next / norm_now)[:, None] * direction
            norm_now = norm_next
    return (solution, residual)


def solution(mesh):
    members = mesh.shape["pair"]
    groups = mesh.shape["blk"]

    def chosen(features, *rest):
        one_block_each = features.shape[1] == members * BS and BS % CHUNK == 0
        powers = members & (members - 1) == 0 and groups & (groups - 1) == 0
        each = own_block_body if one_block_each and powers else body
        return each(features, *rest)

    placed = (P(None, "blk"), P(), P(), P("blk"), P(None, "blk"), P(("blk", "pair"), None))
    return jax.shard_map(
        chosen,
        mesh=mesh,
        in_specs=placed,
        out_specs=(P(None, "blk"), P(None, "blk")),
        check_vma=False,
    )
```

```python
import functools
import math

import jax
import jax.numpy as jnp
from jax import lax
from jax.experimental import pallas as pl
from jax.experimental.pallas import tpu as pltpu
from jax.sharding import PartitionSpec as P

BS = 2048
ITERS = 2

f32 = jnp.float32
bf16 = jnp.bfloat16
root_three = 1.7320508075688772
taper_radius = 2.0
BOTH = ("blk", "pair")
NT = (((1,), (1,)), ((), ()))
CHUNK = 256

RATE = taper_radius * root_three * math.log2(math.e)
NEAR = math.log2(math.e)
FAR = RATE / 4.0
UNIT = NEAR * FAR * RATE**4


def parts_of(x):
    high = x.astype(bf16)
    rest = x - high.astype(f32)
    middle = rest.astype(bf16)
    low = (rest - middle.astype(f32)).astype(bf16)
    return high, middle, low


def norm_parts(points, axis, first):
    norms = jnp.sum(points * points, axis=axis, keepdims=True)
    high, middle, low = (x.astype(f32) for x in parts_of(norms))
    at = lax.broadcasted_iota(jnp.int32, points.shape, axis)
    ones = jnp.where(at < 6, 1.0, 0.0)
    placed = jnp.where(at == first + 2, low, ones)
    placed = jnp.where(at == first + 1, middle, placed)
    return jnp.where(at == first, high, placed).astype(bf16)


def left_parts(points):
    turned = points.T
    high, middle, _ = parts_of(turned)
    return jnp.concatenate([high, high, middle, norm_parts(turned, 1, 0)], axis=1)


def right_parts(points):
    high, middle, _ = parts_of(-2.0 * points)
    return jnp.concatenate([high, middle, high, norm_parts(points, 0, 3)], axis=0)


def points_of(features, inv_scale):
    depth = features.shape[0]
    scale = jnp.broadcast_to(inv_scale, (8, depth)).T[:, 0:1]
    return features * scale * (RATE / (taper_radius * math.sqrt(depth)))


def level_of(signal):
    return jnp.log2(jnp.full((1, CHUNK), signal * (1.0 / UNIT), f32))


def kernel_values(squared, level):
    squared = jnp.maximum(squared, 1e-30)
    s = squared * lax.rsqrt(squared)
    decay = jnp.exp2(level - s)
    u = jnp.maximum(RATE - s, 0.0)
    u2 = u * u
    return ((s + NEAR) * (s + FAR) * decay) * (u2 * u2)


def dot(a, b):
    return jnp.dot(a, b, preferred_element_type=f32)


def dot_nt(a, b):
    return lax.dot_general(a, b, NT, preferred_element_type=f32)


def own_block():
    members = lax.axis_size("pair")
    return lax.axis_index("pair") ^ ((members - 1) * (lax.axis_index("blk") & 1))


def is_live(listings):
    first = lax.axis_index("blk") * lax.axis_size("pair") + own_block()
    found = jnp.zeros(listings[0][0:1, :].shape, f32)
    for listing in listings:
        match = (listing[0:1, :] == first) & (listing[1:2, :] == first + 1)
        found = found + jnp.where(match, 1.0, 0.0)
    return jnp.max(found) > 0.0


def cut(at):
    return slice(at * CHUNK, (at + 1) * CHUNK)


def two_sum(a, b):
    total = a + b
    back = total - a
    return total, (a - (total - back)) + (b - back)


def two_product(a, b):
    def halves(x):
        big = x * 4097.0
        high = big - (big - x)
        return high, x - high

    product = a * b
    a_high, a_low = halves(a)
    b_high, b_low = halves(b)
    error = ((a_high * b_high - product) + a_high * b_low + a_low * b_high) + a_low * b_low
    return product, error


def plus(x, y):
    total, error = two_sum(x[0], y[0])
    return two_sum(total, error + (x[1] + y[1]))


def times(x, factor):
    product, error = two_product(x[0], factor)
    return two_sum(product, error + x[1] * factor)


def lane_tiles_sum(x):
    high = x[:, 0:128]
    low = jnp.zeros_like(high)
    for at in range(128, x.shape[1], 128):
        high, error = two_sum(high, x[:, at : at + 128])
        low = low + error
    return high, low


def lanes_sum(high, low):
    shift = 64
    while shift:
        high, error = two_sum(high, pltpu.roll(high, shift, 1))
        low = low + pltpu.roll(low, shift, 1) + error
        shift //= 2
    return high, low


def loading_kernel(
    features,
    right_side,
    noise_var,
    inv_scale,
    send,
    raw,
    direction,
    raw_next,
    next_dir,
    noise,
    scale,
    sems,
):
    size = raw.shape[1]
    depth = raw.shape[0]
    mine = own_block()
    after = jnp.minimum(mine + 1, lax.axis_size("pair") - 1)
    here = pl.ds(pl.multiple_of(mine * size, size), size)
    there = pl.ds(pl.multiple_of(after * size, size), size)
    moves = [
        (features.at[:, :size], send.at[:depth]),
        (right_side.at[:, :size], send.at[depth:]),
        (features.at[:, here], raw),
        (right_side.at[:, here], direction),
        (features.at[:, there], raw_next),
        (right_side.at[:, there], next_dir),
        (noise_var.at[:, here], noise),
        (inv_scale, scale),
    ]
    copies = [
        pltpu.make_async_copy(source, target, sems.at[k])
        for k, (source, target) in enumerate(moves)
    ]
    for copy in copies:
        copy.start()
    for copy in copies:
        copy.wait()


def diagonal_kernel(signal, raw, scale, direction, tile, own, left, right, half, ahead):
    size = tile.shape[0]
    level = level_of(signal[0])
    points = points_of(raw[...], scale[...])
    left[...] = left_parts(points)
    right[...] = right_parts(points)
    half[...] = direction[...].astype(bf16)
    own[...] = jnp.zeros_like(own)

    count = size // CHUNK
    order = [(row, col) for row in range(count) for col in range(row, count)]

    def argument(k):
        row, col = order[k]
        ahead[k % 2] = dot(left[cut(row), :], right[:, cut(col)])

    def product(k):
        row, col = order[k]
        block = tile[cut(row), cut(col)]
        own[:, cut(col)] += dot(half[:, cut(row)], block)
        if col > row:
            own[:, cut(row)] += dot_nt(half[:, cut(col)], block)

    argument(0)
    for k, (row, col) in enumerate(order):
        if k + 1 < len(order):
            argument(k + 1)
        if k:
            product(k - 1)
        tile[cut(row), cut(col)] = kernel_values(ahead[k % 2], level).astype(bf16)
    product(len(order) - 1)


def crossing_kernel(
    members,
    signal,
    *refs,
):
    listings, refs = refs[:members], refs[members:]
    (raw_next, dir_next, sent, scale, left, direction, noise, diagonal) = refs[:8]
    (tile, row_sums, own, over, next_dir, mark) = refs[8:14]
    (right, half, half_next, ahead, col_part, row_part) = refs[14:]
    size = tile.shape[0]
    probes = own.shape[0]
    last = own_block() == members - 1
    depth = raw_next.shape[0]
    next_dir[...] = jnp.where(last, sent[depth:], dir_next[...])
    live = is_live(listings)
    mark[...] = jnp.where(live, jnp.ones(mark.shape, f32), jnp.zeros(mark.shape, f32))
    own[...] = jnp.zeros_like(own)
    over[...] = jnp.zeros_like(over)
    row_sums[...] = jnp.zeros_like(row_sums)

    @pl.when(live)
    def _():
        level = level_of(signal[0])
        raw = jnp.where(last, sent[:depth], raw_next[...])
        right[...] = right_parts(points_of(raw, scale[...]))
        half[...] = direction[...].astype(bf16)
        half_next[...] = next_dir[...].astype(bf16)
        col_part[...] = jnp.zeros_like(col_part)
        row_part[...] = jnp.zeros_like(row_part)
        count = size // CHUNK
        order = [(row, col) for row in range(count) for col in range(count)]

        def argument(k):
            row, col = order[k]
            ahead[k % 2] = dot(left[cut(row), :], right[:, cut(col)])

        def product(k):
            row, col = order[k]
            block = tile[cut(row), cut(col)]
            over[:probes, cut(col)] += dot(half[:, cut(row)], block)
            own[:, cut(row)] += dot_nt(half_next[:, cut(col)], block)

        argument(0)
        for k, (row, col) in enumerate(order):
            if k + 1 < len(order):
                argument(k + 1)
            if k:
                product(k - 1)
            values = kernel_values(ahead[k % 2], level)
            tile[cut(row), cut(col)] = values.astype(bf16)
            col_part[:, cut(col)] += jnp.sum(values.reshape(CHUNK // 8, 8, CHUNK), axis=0)
            along = values[:, 0:128]
            for lane in range(128, CHUNK, 128):
                along = along + values[:, lane : lane + 128]
            row_part[cut(row), :] += along
        product(len(order) - 1)
        row_sums[...] = lax.dot_general(
            jnp.ones((8, 128), f32),
            row_part[...],
            NT,
            precision=lax.Precision.HIGHEST,
            preferred_element_type=f32,
        )
        columns = jnp.sum(col_part[...], axis=0, keepdims=True)
        over[:probes] += columns * next_dir[...]
        over[probes : probes + 1] = columns

    own[...] += diagonal[...] + (noise[...] + row_sums[0:1, :]) * direction[...]


def both_parts(x):
    high = x.astype(bf16)
    return jnp.concatenate([high, (x - high.astype(f32)).astype(bf16)], axis=0)


def folded(x):
    half = x.shape[0] // 2
    return x[:half] + x[half:]


def over_kernel(mark, tile, image, over2):
    live = jnp.max(mark[...]) > 0.0

    @pl.when(live)
    def _():
        over2[...] = folded(dot(both_parts(image[...]), tile[...]))

    @pl.when(jnp.logical_not(live))
    def _():
        over2[...] = jnp.zeros_like(over2)


def second_kernel(
    mark,
    tile,
    cross_tile,
    row_sums,
    noise,
    direction,
    next_dir,
    image,
    part,
    over,
    got,
    over2,
    own2,
    sums,
    both,
):
    size = tile.shape[0]
    probes = image.shape[0]
    here = image[...]
    both[...] = both_parts(here)
    own2[...] = (noise[...] + row_sums[0:1, :] + got[probes : probes + 1, :]) * here
    for at in range(0, size, CHUNK):
        rows = slice(at, at + CHUNK)
        tail = slice(at, size)
        rest = slice(at + CHUNK, size)
        own2[:, tail] += folded(dot(both[:, rows], tile[rows, tail]))
        if at + CHUNK < size:
            own2[:, rows] += folded(dot_nt(both[:, rest], tile[rows, rest]))
    there = part[...] + over[:probes]

    @pl.when(jnp.max(mark[...]) > 0.0)
    def _():
        own2[...] += folded(dot_nt(both_parts(there), cross_tile[...]))

    begin = direction[...]
    mine = own2[...]
    theirs = over2[...]
    squares = here * here
    forms = [
        begin * begin,
        begin * here,
        squares,
        squares + begin * mine + next_dir[...] * theirs,
        here * mine + there * theirs,
    ]
    pairs = [lane_tiles_sum(x) for x in forms]
    high, low = lanes_sum(
        jnp.concatenate([x for x, _ in pairs], axis=0), jnp.concatenate([x for _, x in pairs], axis=0)
    )
    rows = [(high, 0), (low, 0), (high, 1), (low, 1), (high, 2), (low, 2), (high, 3), (high, 4)]
    lane = lax.broadcasted_iota(jnp.int32, (probes, 128), 1)
    out = jnp.zeros((probes, 128), f32)
    for k, (values, at) in enumerate(rows):
        out = jnp.where(lane == k, values[at * probes : (at + 1) * probes], out)
    square = jnp.concatenate([out, jnp.zeros((128 - probes, 128), f32)], axis=0)
    turned = square.T[: len(rows)]
    for k in range(sums.shape[0]):
        sums[k] = turned


def final_kernel(sums, right_side, *rest):
    members = lax.axis_size("pair")
    images, images2 = rest[:members], rest[members : 2 * members]
    solution_out, residual_out, begins, solved, left_over, get_sems, put_sems = rest[2 * members :]
    probes, size = images[0].shape
    mine = own_block()

    def block(k):
        return pl.ds(pl.multiple_of((mine ^ k) * size, size), size)

    gets = [
        pltpu.make_async_copy(right_side.at[:, block(k)], begins.at[k], get_sems.at[k])
        for k in range(members)
    ]
    for get in gets:
        get.start()

    total = sums[0]
    error = jnp.zeros_like(total)
    for k in range(1, sums.shape[0]):
        total, missed = two_sum(total, sums[k])
        error = error + missed
    empty = jnp.zeros((128 - total.shape[0], 128), f32)
    total = jnp.concatenate([total, empty], axis=0).T[:probes]
    error = jnp.concatenate([error, empty], axis=0).T[:probes]
    square, form, image_square = (
        (total[:, k : k + 1], total[:, k + 1 : k + 2] + error[:, k : k + 1]) for k in (0, 2, 4)
    )
    mixed, image_form = ((total[:, k : k + 1], error[:, k : k + 1]) for k in (6, 7))
    alpha = square[0] / form[0]
    new = plus(plus(square, times(form, -2.0 * alpha)), times(times(image_square, alpha), alpha))[0]
    beta = new / square[0]
    less = times(mixed, -alpha)
    curvature = plus(plus(form, less), times(times(image_form, alpha), alpha))
    curvature = plus(curvature, times(plus(times(form, 2.0), less), beta))
    curvature = plus(curvature, times(times(form, beta), beta))
    alpha2 = new / curvature[0]
    puts = []
    for k in range(members):
        gets[k].wait()
        begin = begins[k]
        image = images[k][...]
        after = begin - alpha * image
        solved[k] = alpha * begin + alpha2 * (after + beta * begin)
        left_over[k] = after - alpha2 * ((image - alpha * images2[k][...]) + beta * image)
        for at, (source, target) in enumerate(((solved, solution_out), (left_over, residual_out))):
            puts.append(
                pltpu.make_async_copy(source.at[k], target.at[:, block(k)], put_sems.at[at, k])
            )
            puts[-1].start()
    for put in puts:
        put.wait()


def params(mebibytes):
    return pltpu.CompilerParams(vmem_limit_bytes=mebibytes << 20)


def shaped(*shape):
    return jax.ShapeDtypeStruct(shape, f32)


VMEM = pl.BlockSpec(memory_space=pltpu.VMEM)
SMEM = pl.BlockSpec(memory_space=pltpu.SMEM)
HBM = pl.BlockSpec(memory_space=pltpu.HBM)
ANY = pl.BlockSpec(memory_space=pl.ANY)


def loading_call(features, right_side, noise_var, inv_scale, size):
    depth = features.shape[0]
    probes = right_side.shape[0]
    shapes = [
        (depth + probes, size),
        (depth, size),
        (probes, size),
        (depth, size),
        (probes, size),
        (1, size),
        (1, depth),
    ]
    return pl.pallas_call(
        loading_kernel,
        in_specs=[HBM] * 4,
        out_specs=[VMEM] * len(shapes),
        out_shape=[pltpu.VMEM(shape, f32) for shape in shapes],
        scratch_shapes=[pltpu.SemaphoreType.DMA((len(shapes) + 1,))],
        compiler_params=params(16),
    )(features, right_side, noise_var, inv_scale)


def diagonal_call(signal, raw, scale, direction):
    depth, size = raw.shape
    probes = direction.shape[0]
    return pl.pallas_call(
        diagonal_kernel,
        in_specs=[SMEM, VMEM, VMEM, VMEM],
        out_specs=[VMEM] * 3,
        out_shape=[
            pltpu.VMEM((size, size), bf16),
            pltpu.VMEM((probes, size), f32),
            pltpu.VMEM((size, 4 * depth), bf16),
        ],
        scratch_shapes=[
            pltpu.VMEM((4 * depth, size), bf16),
            pltpu.VMEM((probes, size), bf16),
            pltpu.VMEM((2, CHUNK, CHUNK), f32),
        ],
        compiler_params=params(16),
    )(signal, raw, scale, direction)


def crossing_call(signal, listings, *arrays):
    raw_next, direction = arrays[0], arrays[5]
    depth, size = raw_next.shape
    probes = direction.shape[0]
    return pl.pallas_call(
        functools.partial(crossing_kernel, len(listings)),
        in_specs=[SMEM] + [VMEM] * (len(listings) + len(arrays)),
        out_specs=[VMEM] * 6,
        out_shape=[
            pltpu.VMEM((size, size), bf16),
            pltpu.VMEM((8, size), f32),
            pltpu.VMEM((probes, size), f32),
            pltpu.VMEM((probes + 8, size), f32),
            pltpu.VMEM((probes, size), f32),
            pltpu.VMEM((8, 128), f32),
        ],
        scratch_shapes=[
            pltpu.VMEM((4 * depth, size), bf16),
            pltpu.VMEM((probes, size), bf16),
            pltpu.VMEM((probes, size), bf16),
            pltpu.VMEM((2, CHUNK, CHUNK), f32),
            pltpu.VMEM((8, size), f32),
            pltpu.VMEM((size, 128), f32),
        ],
        compiler_params=params(16),
    )(signal, *listings, *arrays)


def over_call(mark, tile, image):
    return pl.pallas_call(
        over_kernel,
        in_specs=[VMEM] * 3,
        out_specs=VMEM,
        out_shape=pltpu.VMEM(image.shape, f32),
        compiler_params=params(16),
    )(mark, tile, image)


def second_call(devices, *arrays):
    probes, size = arrays[5].shape
    return pl.pallas_call(
        second_kernel,
        in_specs=[VMEM] * len(arrays),
        out_specs=[VMEM] * 2,
        out_shape=[pltpu.VMEM((probes, size), f32), pltpu.VMEM((devices, 8, 128), f32)],
        scratch_shapes=[pltpu.VMEM((2 * probes, size), bf16)],
        compiler_params=params(16),
    )(*arrays)


def final_call(sums, right_side, images, images2):
    probes, size = images[0].shape
    members = len(images)
    return pl.pallas_call(
        final_kernel,
        in_specs=[VMEM, HBM] + [VMEM] * (2 * members),
        out_specs=[HBM, HBM],
        out_shape=[shaped(*right_side.shape)] * 2,
        scratch_shapes=[
            pltpu.VMEM((members, probes, size), f32),
            pltpu.VMEM((members, probes, size), f32),
            pltpu.VMEM((members, probes, size), f32),
            pltpu.SemaphoreType.DMA((members,)),
            pltpu.SemaphoreType.DMA((2, members)),
        ],
        compiler_params=params(16),
    )(sums, right_side, *images, *images2)


def device_of(block):
    members = lax.axis_size("pair")
    group, at = divmod(block, members)
    return group * members + (at ^ ((members - 1) * (group & 1)))


def moved(x, distance):
    count = lax.axis_size(BOTH[0]) * lax.axis_size(BOTH[1])
    route = [
        (device_of(i), device_of(i + distance)) for i in range(count) if 0 <= i + distance < count
    ]
    return lax.ppermute(x, BOTH, route)


def exchanged(x, distance):
    count = lax.axis_size(BOTH[0]) * lax.axis_size(BOTH[1])
    return lax.ppermute(x, BOTH, [(i, i ^ distance) for i in range(count)])


def sent_from_next_group(x):
    members = lax.axis_size("pair")
    route = []
    for g in range(lax.axis_size("blk") - 1):
        target = device_of(g * members + members - 1)
        route.append((target + members, target))
    return lax.ppermute(x, BOTH, route)


def own_block_body(features, inv_scale, signal, noise_var, right_side, block_pairs):
    members = lax.axis_size("pair")
    devices = members * lax.axis_size("blk")
    size = features.shape[1] // members
    probes = right_side.shape[0]

    features, right_side, scale, noise = (
        pltpu.with_memory_space_constraint(x, pltpu.HBM)
        for x in (features, right_side, inv_scale[None, :], noise_var[None, :])
    )
    send, raw, direction, raw_next, dir_next, noise, scale = loading_call(
        features, right_side, noise, scale, size
    )
    sent = sent_from_next_group(send)
    listing = block_pairs.T
    listings = [listing] + [exchanged(listing, k) for k in range(1, members)]

    tile, diagonal, left = diagonal_call(signal, raw, scale, direction)
    cross_tile, row_sums, own, over, next_dir, mark = crossing_call(
        signal, listings, raw_next, dir_next, sent, scale, left, direction, noise, diagonal
    )
    got = moved(over, 1)
    part = moved(own, -1)
    image = own + got[:probes]
    images = {0: image, 1: exchanged(image, 1)}
    spans = [1 << k for k in range(1, members.bit_length() - 1)]
    for span in spans:
        images[span] = exchanged(image, span)
    over2 = over_call(mark, cross_tile, image)
    own2, sums = second_call(
        devices,
        mark,
        tile,
        cross_tile,
        row_sums,
        noise,
        direction,
        next_dir,
        image,
        part,
        over,
        got,
        over2,
    )
    image2 = own2 + moved(over2, 1)
    images2 = {0: image2, 1: exchanged(image2, 1)}
    for span in spans:
        images2[span] = exchanged(image2, span)
    image2, images, sums = lax.optimization_barrier((image2, images, sums))
    sums = lax.all_to_all(sums, BOTH, 0, 0)
    images2, images, sums = lax.optimization_barrier((images2, images, sums))
    for held in (images, images2):
        for span in spans:
            for at in range(1, span):
                held[at + span] = exchanged(held[span], at)
    return tuple(
        final_call(
            sums,
            right_side,
            [images[k] for k in range(members)],
            [images2[k] for k in range(members)],
        )
    )


def passed_along(block, axis, distance):
    devices = range(lax.axis_size(axis))
    route = [(i - distance, i) for i in devices if i - distance in devices]
    return lax.ppermute(block, axis, route)


def kernel_tile(left_scaled, right_scaled, amplitude):
    cross = lax.dot_general(
        left_scaled,
        right_scaled,
        (((0,), (0,)), ((), ())),
        precision=lax.Precision.HIGHEST,
        preferred_element_type=jnp.float32,
    )
    left_norms = jnp.sum(left_scaled * left_scaled, axis=0)
    right_norms = jnp.sum(right_scaled * right_scaled, axis=0)
    squared = (left_norms[:, None] + right_norms[None, :] - 2.0 * cross) / left_scaled.shape[0]
    distance = jnp.sqrt(jnp.maximum(squared, 0.0))
    stretched = root_three * distance
    ratio = distance / taper_radius
    taper = jnp.maximum(1.0 - ratio, 0.0) ** 4 * (1.0 + 4.0 * ratio)
    return amplitude * (1.0 + stretched) * jnp.exp(-stretched) * taper


def block_terms(left_scaled, right_scaled, left_dir, right_dir, amplitude):
    block_rows = left_scaled.shape[1]
    row_step = min(512, block_rows)
    left_half = left_dir.astype(jnp.bfloat16)
    right_half = right_dir.astype(jnp.bfloat16)

    def rows_visit(position, carried):
        toward_left, toward_right, row_sums, col_sums = carried
        offset = position * row_step
        kernel_rows = kernel_tile(
            lax.dynamic_slice_in_dim(left_scaled, offset, row_step, 1), right_scaled, amplitude
        )
        rows_half = kernel_rows.astype(jnp.bfloat16)
        product = lax.dot_general(
            right_half, rows_half, (((1,), (1,)), ((), ())), preferred_element_type=jnp.float32
        )
        toward_left = lax.dynamic_update_slice_in_dim(toward_left, product, offset, 1)
        toward_right = toward_right + jnp.dot(
            lax.dynamic_slice_in_dim(left_half, offset, row_step, 1),
            rows_half,
            preferred_element_type=jnp.float32,
        )
        row_sums = lax.dynamic_update_slice_in_dim(
            row_sums, jnp.sum(kernel_rows, axis=1), offset, 0
        )
        col_sums = col_sums + jnp.sum(kernel_rows, axis=0)
        return (toward_left, toward_right, row_sums, col_sums)

    zeros_dir = jnp.zeros(left_dir.shape, jnp.float32)
    zeros_row = jnp.zeros((block_rows,), jnp.float32)
    return lax.fori_loop(
        0, block_rows // row_step, rows_visit, (zeros_dir, zeros_dir, zeros_row, zeros_row)
    )


def body(features, inv_scale, signal, noise_var, right_side, block_pairs):
    local_rows = features.shape[1]
    blocks_here = local_rows // BS
    amplitude = signal[0]
    scaled = features * inv_scale[:, None]
    beyond = passed_along(scaled[:, :BS], "blk", -1)
    reach_scaled = jnp.concatenate([scaled, beyond], axis=1)
    base_block = lax.axis_index("blk") * blocks_here
    members = lax.axis_size("pair")
    listing = lax.all_gather(block_pairs, "pair", axis=0, tiled=True)
    living = (listing[:, 0] >= 0).astype(jnp.int32)
    ranked = jnp.cumsum(living) - living
    wanted = lax.axis_index("pair") + members * jnp.arange(block_pairs.shape[0], dtype=jnp.int32)
    matched = (ranked[None, :] == wanted[:, None]) & (living[None, :] > 0)
    chosen = jnp.sum(jnp.where(matched[:, :, None], listing[None, :, :], 0), axis=1)
    my_pairs = jnp.where(jnp.any(matched, axis=1)[:, None], chosen, -1)
    active = jnp.maximum((jnp.sum(living) - lax.axis_index("pair") + members - 1) // members, 0)
    row_local = my_pairs[:, 0] - base_block
    col_local = my_pairs[:, 1] - base_block
    solution = jnp.zeros_like(right_side)
    residual = right_side
    direction = right_side
    norm_now = lax.psum(jnp.sum(residual * residual, axis=1), "blk")
    for iteration in range(ITERS):
        ahead_dir = passed_along(direction[:, :BS], "blk", -1)
        reach_dir = jnp.concatenate([direction, ahead_dir], axis=1)

        def visit(slot_index, summed):
            row_start = row_local[slot_index] * BS
            col_start = col_local[slot_index] * BS
            crossing = (row_local[slot_index] != col_local[slot_index]).astype(jnp.float32)
            left_dir = lax.dynamic_slice_in_dim(reach_dir, row_start, BS, 1)
            right_dir = lax.dynamic_slice_in_dim(reach_dir, col_start, BS, 1)
            toward_left, toward_right, row_sums, col_sums = block_terms(
                lax.dynamic_slice_in_dim(reach_scaled, row_start, BS, 1),
                lax.dynamic_slice_in_dim(reach_scaled, col_start, BS, 1),
                left_dir,
                right_dir,
                amplitude,
            )
            term_left = toward_left + crossing * row_sums[None, :] * left_dir
            term_right = crossing * (toward_right + col_sums[None, :] * right_dir)
            summed = lax.dynamic_update_slice_in_dim(
                summed, lax.dynamic_slice_in_dim(summed, row_start, BS, 1) + term_left, row_start, 1
            )
            summed = lax.dynamic_update_slice_in_dim(
                summed,
                lax.dynamic_slice_in_dim(summed, col_start, BS, 1) + term_right,
                col_start,
                1,
            )
            return summed

        summed = lax.fori_loop(0, active, visit, jnp.zeros(reach_dir.shape, jnp.float32))
        own_part = summed[:, :local_rows]
        next_part = summed[:, local_rows:]
        own_sum, next_sum = lax.psum((own_part, next_part), "pair")
        entering = passed_along(next_sum, "blk", 1)
        coupled = jnp.concatenate([own_sum[:, :BS] + entering, own_sum[:, BS:]], axis=1)
        applied = noise_var[None, :] * direction + coupled
        last_turn = iteration + 1 == ITERS
        curvature = lax.psum(jnp.sum(direction * applied, axis=1), "blk")
        step_size = norm_now / curvature
        solution = solution + step_size[:, None] * direction
        residual = residual - step_size[:, None] * applied
        if not last_turn:
            norm_next = lax.psum(jnp.sum(residual * residual, axis=1), "blk")
            direction = residual + (norm_next / norm_now)[:, None] * direction
            norm_now = norm_next
    return (solution, residual)


def solution(mesh):
    members = mesh.shape["pair"]
    groups = mesh.shape["blk"]

    def chosen(features, *rest):
        one_block_each = features.shape[1] == members * BS and BS % CHUNK == 0
        powers = members > 1 and members & (members - 1) == 0 and groups & (groups - 1) == 0
        each = own_block_body if one_block_each and powers else body
        return each(features, *rest)

    placed = (P(None, "blk"), P(), P(), P("blk"), P(None, "blk"), P(("blk", "pair"), None))
    return jax.shard_map(
        chosen,
        mesh=mesh,
        in_specs=placed,
        out_specs=(P(None, "blk"), P(None, "blk")),
        check_vma=False,
    )
```

```python
import functools
import math

import jax
import jax.numpy as jnp
from jax import lax
from jax.experimental import pallas as pl
from jax.experimental.pallas import tpu as pltpu
from jax.sharding import PartitionSpec as P

BS = 2048
ITERS = 2

f32 = jnp.float32
bf16 = jnp.bfloat16
root_three = 1.7320508075688772
taper_radius = 2.0
BOTH = ("blk", "pair")
NT = (((1,), (1,)), ((), ()))
CHUNK = 256
UPPER_STRIPS = 2

RATE = taper_radius * root_three * math.log2(math.e)
NEAR = math.log2(math.e)
FAR = RATE / 4.0
UNIT = NEAR * FAR * RATE**4


def parts_of(x):
    high = x.astype(bf16)
    rest = x - high.astype(f32)
    middle = rest.astype(bf16)
    low = (rest - middle.astype(f32)).astype(bf16)
    return high, middle, low


def norm_parts(points, axis, first):
    norms = jnp.sum(points * points, axis=axis, keepdims=True)
    high, middle, low = (x.astype(f32) for x in parts_of(norms))
    at = lax.broadcasted_iota(jnp.int32, points.shape, axis)
    ones = jnp.where(at < 6, 1.0, 0.0)
    placed = jnp.where(at == first + 2, low, ones)
    placed = jnp.where(at == first + 1, middle, placed)
    return jnp.where(at == first, high, placed).astype(bf16)


def left_parts(points):
    turned = points.T
    high, middle, _ = parts_of(turned)
    return jnp.concatenate([high, high, middle, norm_parts(turned, 1, 0)], axis=1)


def right_parts(points):
    high, middle, _ = parts_of(-2.0 * points)
    return jnp.concatenate([high, middle, high, norm_parts(points, 0, 3)], axis=0)


def points_of(features, inv_scale):
    depth = features.shape[0]
    scale = jnp.broadcast_to(inv_scale, (8, depth)).T[:, 0:1]
    return features * scale * (RATE / (taper_radius * math.sqrt(depth)))


def level_of(signal):
    return jnp.log2(jnp.full((1, CHUNK), signal * (1.0 / UNIT), f32))


def kernel_values(squared, level):
    squared = jnp.maximum(squared, 1e-30)
    s = squared * lax.rsqrt(squared)
    decay = jnp.exp2(level - s)
    u = jnp.maximum(RATE - s, 0.0)
    u2 = u * u
    return ((s + NEAR) * (s + FAR) * decay) * (u2 * u2)


def dot(a, b):
    return jnp.dot(a, b, preferred_element_type=f32)


def dot_nt(a, b):
    return lax.dot_general(a, b, NT, preferred_element_type=f32)


def own_block():
    members = lax.axis_size("pair")
    return lax.axis_index("pair") ^ ((members - 1) * (lax.axis_index("blk") & 1))


def found_in(listing, shape):
    wanted = lax.axis_index("blk") * lax.axis_size("pair") + lax.broadcasted_iota(jnp.int32, shape, 1)
    found = jnp.zeros(shape, f32)
    for slot in range(listing.shape[1]):
        first, second = listing[0:1, slot : slot + 1], listing[1:2, slot : slot + 1]
        found = jnp.where((first == wanted) & (second == wanted + 1), 1.0, found)
    return found


def is_live(found):
    lane = lax.broadcasted_iota(jnp.int32, found.shape, 1)
    return jnp.max(jnp.where(lane == own_block(), found, 0.0)) > 0.0


def cut(at):
    return slice(at * CHUNK, (at + 1) * CHUNK)


def two_sum(a, b):
    total = a + b
    back = total - a
    return total, (a - (total - back)) + (b - back)


def two_product(a, b):
    def halves(x):
        big = x * 4097.0
        high = big - (big - x)
        return high, x - high

    product = a * b
    a_high, a_low = halves(a)
    b_high, b_low = halves(b)
    error = ((a_high * b_high - product) + a_high * b_low + a_low * b_high) + a_low * b_low
    return product, error


def plus(x, y):
    total, error = two_sum(x[0], y[0])
    return two_sum(total, error + (x[1] + y[1]))


def times(x, factor):
    product, error = two_product(x[0], factor)
    return two_sum(product, error + x[1] * factor)


def lane_tiles_sum(x):
    high = x[:, 0:128]
    low = jnp.zeros_like(high)
    for at in range(128, x.shape[1], 128):
        high, error = two_sum(high, x[:, at : at + 128])
        low = low + error
    return high, low


def lanes_sum(high, low):
    shift = 64
    while shift:
        high, error = two_sum(high, pltpu.roll(high, shift, 1))
        low = low + pltpu.roll(low, shift, 1) + error
        shift //= 2
    return high, low


def loading_kernel(
    features,
    right_side,
    noise_var,
    inv_scale,
    block_pairs,
    send,
    send_rest,
    raw,
    direction,
    raw_next,
    next_dir,
    noise,
    scale,
    found,
    listing,
    sems,
):
    size = raw.shape[1]
    depth = raw.shape[0]
    cut_at = send.shape[0]
    mine = own_block()
    after = jnp.minimum(mine + 1, lax.axis_size("pair") - 1)
    here = pl.ds(pl.multiple_of(mine * size, size), size)
    there = pl.ds(pl.multiple_of(after * size, size), size)
    moves = [
        (features.at[:cut_at, :size], send),
        (features.at[cut_at:, :size], send_rest.at[: depth - cut_at]),
        (right_side.at[:, :size], send_rest.at[depth - cut_at :]),
        (features.at[:, here], raw),
        (right_side.at[:, here], direction),
        (features.at[:, there], raw_next),
        (right_side.at[:, there], next_dir),
        (noise_var.at[:, here], noise),
        (inv_scale, scale),
        (block_pairs, listing),
    ]
    copies = [
        pltpu.make_async_copy(source, target, sems.at[k])
        for k, (source, target) in enumerate(moves)
    ]
    for copy in copies:
        copy.start()
    for copy in copies:
        copy.wait()
    found[...] = found_in(listing, found.shape)


def diagonal_products(level, first, tile, own, left, right, half, ahead):
    size = tile.shape[1]
    count = size // CHUNK
    begin = first // CHUNK
    order = [
        (row, col) for row in range(begin, begin + tile.shape[0] // CHUNK) for col in range(row, count)
    ]

    def argument(k):
        row, col = order[k]
        ahead[k % 2] = dot(left[cut(row), :], right[:, cut(col)])

    def product(k):
        row, col = order[k]
        block = tile[cut(row - begin), cut(col)]
        own[:, cut(col)] += dot(half[:, cut(row)], block)
        if col > row:
            own[:, cut(row)] += dot_nt(half[:, cut(col)], block)

    argument(0)
    for k, (row, col) in enumerate(order):
        if k + 1 < len(order):
            argument(k + 1)
        if k:
            product(k - 1)
        tile[cut(row - begin), cut(col)] = kernel_values(ahead[k % 2], level).astype(bf16)
    product(len(order) - 1)


def diagonal_kernel(signal, raw, scale, direction, tile, own, left, right, half, ahead):
    points = points_of(raw[...], scale[...])
    left[...] = left_parts(points)
    right[...] = right_parts(points)
    half[...] = direction[...].astype(bf16)
    own[...] = jnp.zeros_like(own)
    diagonal_products(level_of(signal[0]), 0, tile, own, left, right, half, ahead)


def lower_diagonal_kernel(signal, left, right, half, upper, crossed, tile, own, ahead):
    own[...] = upper[...] + crossed[...]
    first = tile.shape[1] - tile.shape[0]
    diagonal_products(level_of(signal[0]), first, tile, own, left, right, half, ahead)


def crossing_kernel(
    signal,
    found,
    raw_next,
    dir_next,
    sent,
    sent_rest,
    scale,
    left,
    half,
    direction,
    noise,
    tile,
    row_sums,
    own,
    over,
    next_dir,
    mark,
    right,
    half_next,
    ahead,
    col_part,
    row_part,
):
    size = tile.shape[0]
    probes = own.shape[0]
    last = own_block() == lax.axis_size("pair") - 1
    rest = raw_next.shape[0] - sent.shape[0]
    next_dir[...] = jnp.where(last, sent_rest[rest:], dir_next[...])
    live = is_live(found[...])
    mark[...] = jnp.where(live, jnp.ones(mark.shape, f32), jnp.zeros(mark.shape, f32))
    own[...] = jnp.zeros_like(own)
    over[...] = jnp.zeros_like(over)
    row_sums[...] = jnp.zeros_like(row_sums)

    @pl.when(live)
    def _():
        level = level_of(signal[0])
        raw = jnp.concatenate([sent[...], sent_rest[:rest]], axis=0)
        raw = jnp.where(last, raw, raw_next[...])
        right[...] = right_parts(points_of(raw, scale[...]))
        half_next[...] = next_dir[...].astype(bf16)
        col_part[...] = jnp.zeros_like(col_part)
        row_part[...] = jnp.zeros_like(row_part)
        count = size // CHUNK
        order = [(row, col) for row in range(count) for col in range(count)]

        def argument(k):
            row, col = order[k]
            ahead[k % 2] = dot(left[cut(row), :], right[:, cut(col)])

        def product(k):
            row, col = order[k]
            block = tile[cut(row), cut(col)]
            over[:probes, cut(col)] += dot(half[:, cut(row)], block)
            own[:, cut(row)] += dot_nt(half_next[:, cut(col)], block)

        argument(0)
        for k, (row, col) in enumerate(order):
            if k + 1 < len(order):
                argument(k + 1)
            if k:
                product(k - 1)
            values = kernel_values(ahead[k % 2], level)
            tile[cut(row), cut(col)] = values.astype(bf16)
            col_part[:, cut(col)] += jnp.sum(values.reshape(CHUNK // 8, 8, CHUNK), axis=0)
            along = values[:, 0:128]
            for lane in range(128, CHUNK, 128):
                along = along + values[:, lane : lane + 128]
            row_part[cut(row), :] += along
        product(len(order) - 1)
        row_sums[...] = lax.dot_general(
            jnp.ones((8, 128), f32),
            row_part[...],
            NT,
            precision=lax.Precision.HIGHEST,
            preferred_element_type=f32,
        )
        columns = jnp.sum(col_part[...], axis=0, keepdims=True)
        over[:probes] += columns * next_dir[...]
        over[probes : probes + 1] = columns

    own[...] += (noise[...] + row_sums[0:1, :]) * direction[...]


def both_parts(x):
    high = x.astype(bf16)
    return jnp.concatenate([high, (x - high.astype(f32)).astype(bf16)], axis=0)


def folded(x):
    half = x.shape[0] // 2
    return x[:half] + x[half:]


def over_kernel(mark, tile, image, over2):
    live = jnp.max(mark[...]) > 0.0

    @pl.when(live)
    def _():
        over2[...] = folded(dot(both_parts(image[...]), tile[...]))

    @pl.when(jnp.logical_not(live))
    def _():
        over2[...] = jnp.zeros_like(over2)


def second_diagonal_kernel(upper, lower, row_sums, noise, image, got, own2, both):
    size = upper.shape[1]
    probes = image.shape[0]
    here = image[...]
    both[...] = both_parts(here)
    own2[...] = (noise[...] + row_sums[0:1, :] + got[probes : probes + 1, :]) * here
    for tile, first in ((upper, 0), (lower, upper.shape[0])):
        for at in range(first, first + tile.shape[0], CHUNK):
            rows = slice(at, at + CHUNK)
            inside = slice(at - first, at - first + CHUNK)
            rest = slice(at + CHUNK, size)
            own2[:, at:] += folded(dot(both[:, rows], tile[inside, at:]))
            if at + CHUNK < size:
                own2[:, rows] += folded(dot_nt(both[:, rest], tile[inside, rest]))


def second_kernel(
    mark, cross_tile, direction, next_dir, image, part, over, over2, partial, own2, sums
):
    probes = image.shape[0]
    here = image[...]
    own2[...] = partial[...]
    there = part[...] + over[:probes]

    @pl.when(jnp.max(mark[...]) > 0.0)
    def _():
        own2[...] += folded(dot_nt(both_parts(there), cross_tile[...]))

    begin = direction[...]
    mine = own2[...]
    theirs = over2[...]
    squares = here * here
    forms = [
        begin * begin,
        begin * here,
        squares,
        squares + begin * mine + next_dir[...] * theirs,
        here * mine + there * theirs,
    ]
    pairs = [lane_tiles_sum(x) for x in forms]
    high, low = lanes_sum(
        jnp.concatenate([x for x, _ in pairs], axis=0), jnp.concatenate([x for _, x in pairs], axis=0)
    )
    rows = [(high, 0), (low, 0), (high, 1), (low, 1), (high, 2), (low, 2), (high, 3), (high, 4)]
    lane = lax.broadcasted_iota(jnp.int32, (probes, 128), 1)
    out = jnp.zeros((probes, 128), f32)
    for k, (values, at) in enumerate(rows):
        out = jnp.where(lane == k, values[at * probes : (at + 1) * probes], out)
    square = jnp.concatenate([out, jnp.zeros((128 - probes, 128), f32)], axis=0)
    turned = square.T[: len(rows)]
    for k in range(sums.shape[0]):
        sums[k] = turned


def final_kernel(sums, right_side, *rest):
    members = lax.axis_size("pair")
    images, images2 = rest[:members], rest[members : 2 * members]
    solution_out, residual_out, solved, left_over, put_sems = rest[2 * members :]
    probes, size = solved.shape[1:]
    mine = own_block()

    def block(k):
        return pl.ds(pl.multiple_of((mine ^ k) * size, size), size)

    runs = [two_sum(sums[k], sums[k + 4]) for k in range(4)]
    for k in range(8, sums.shape[0]):
        total, error = runs[k % 4]
        total, missed = two_sum(total, sums[k])
        runs[k % 4] = (total, error + missed)
    while len(runs) > 1:
        joined = []
        for (a, a_error), (b, b_error) in zip(runs[::2], runs[1::2]):
            total, missed = two_sum(a, b)
            joined.append((total, a_error + b_error + missed))
        runs = joined
    total, error = runs[0]
    empty = jnp.zeros((128 - total.shape[0], 128), f32)
    total = jnp.concatenate([total, empty], axis=0).T[:probes]
    error = jnp.concatenate([error, empty], axis=0).T[:probes]
    square, form, image_square = (
        (total[:, k : k + 1], total[:, k + 1 : k + 2] + error[:, k : k + 1]) for k in (0, 2, 4)
    )
    mixed, image_form = (total[:, k : k + 1] for k in (6, 7))
    alpha = square[0] / form[0]
    new = plus(plus(square, times(form, -2.0 * alpha)), times(times(image_square, alpha), alpha))[0]
    beta = new / square[0]
    less = form[0] - alpha * mixed
    curvature = (less + alpha * alpha * image_form) + beta * ((form[0] + less) + beta * form[0])
    alpha2 = new / curvature
    puts = []
    for k in range(members):
        begin = right_side[:, block(k)]
        image = images[k][...]
        after = begin - alpha * image
        solved[k] = alpha * begin + alpha2 * (after + beta * begin)
        left_over[k] = after - alpha2 * ((image - alpha * images2[k][...]) + beta * image)
        for at, (source, target) in enumerate(((solved, solution_out), (left_over, residual_out))):
            puts.append(
                pltpu.make_async_copy(source.at[k], target.at[:, block(k)], put_sems.at[at, k])
            )
            puts[-1].start()
    for put in puts:
        put.wait()


def params(mebibytes):
    return pltpu.CompilerParams(vmem_limit_bytes=mebibytes << 20)


def shaped(*shape):
    return jax.ShapeDtypeStruct(shape, f32)


VMEM = pl.BlockSpec(memory_space=pltpu.VMEM)
SMEM = pl.BlockSpec(memory_space=pltpu.SMEM)
HBM = pl.BlockSpec(memory_space=pltpu.HBM)
ANY = pl.BlockSpec(memory_space=pl.ANY)


def loading_call(features, right_side, noise_var, inv_scale, block_pairs, size):
    depth = features.shape[0]
    probes = right_side.shape[0]
    half = min(depth, (depth + probes) // 16 * 8)
    shapes = [
        (half, size),
        (depth + probes - half, size),
        (depth, size),
        (probes, size),
        (depth, size),
        (probes, size),
        (1, size),
        (1, depth),
        (8, 128),
    ]
    return pl.pallas_call(
        loading_kernel,
        in_specs=[HBM] * 5,
        out_specs=[VMEM] * len(shapes),
        out_shape=[pltpu.VMEM(shape, f32) for shape in shapes],
        scratch_shapes=[
            pltpu.VMEM(block_pairs.shape, jnp.int32),
            pltpu.SemaphoreType.DMA((len(shapes) + 1,)),
        ],
        compiler_params=params(16),
    )(features, right_side, noise_var, inv_scale, block_pairs)


def diagonal_call(signal, raw, scale, direction, rows):
    depth, size = raw.shape
    probes = direction.shape[0]
    return pl.pallas_call(
        diagonal_kernel,
        in_specs=[SMEM, VMEM, VMEM, VMEM],
        out_specs=[VMEM] * 5,
        out_shape=[
            pltpu.VMEM((rows, size), bf16),
            pltpu.VMEM((probes, size), f32),
            pltpu.VMEM((size, 4 * depth), bf16),
            pltpu.VMEM((4 * depth, size), bf16),
            pltpu.VMEM((probes, size), bf16),
        ],
        scratch_shapes=[pltpu.VMEM((2, CHUNK, CHUNK), f32)],
        compiler_params=params(16),
    )(signal, raw, scale, direction)


def lower_diagonal_call(signal, left, right, half, upper, crossed, rows):
    probes, size = upper.shape
    return pl.pallas_call(
        lower_diagonal_kernel,
        in_specs=[SMEM] + [VMEM] * 5,
        out_specs=[VMEM] * 2,
        out_shape=[pltpu.VMEM((rows, size), bf16), pltpu.VMEM((probes, size), f32)],
        scratch_shapes=[pltpu.VMEM((2, CHUNK, CHUNK), f32)],
        compiler_params=params(16),
    )(signal, left, right, half, upper, crossed)


def crossing_call(signal, *arrays):
    raw_next, direction = arrays[1], arrays[8]
    depth, size = raw_next.shape
    probes = direction.shape[0]
    return pl.pallas_call(
        crossing_kernel,
        in_specs=[SMEM] + [VMEM] * len(arrays),
        out_specs=[VMEM] * 6,
        out_shape=[
            pltpu.VMEM((size, size), bf16),
            pltpu.VMEM((8, size), f32),
            pltpu.VMEM((probes, size), f32),
            pltpu.VMEM((probes + 8, size), f32),
            pltpu.VMEM((probes, size), f32),
            pltpu.VMEM((8, 128), f32),
        ],
        scratch_shapes=[
            pltpu.VMEM((4 * depth, size), bf16),
            pltpu.VMEM((probes, size), bf16),
            pltpu.VMEM((2, CHUNK, CHUNK), f32),
            pltpu.VMEM((8, size), f32),
            pltpu.VMEM((size, 128), f32),
        ],
        compiler_params=params(16),
    )(signal, *arrays)


def over_call(mark, tile, image):
    return pl.pallas_call(
        over_kernel,
        in_specs=[VMEM] * 3,
        out_specs=VMEM,
        out_shape=pltpu.VMEM(image.shape, f32),
        compiler_params=params(16),
    )(mark, tile, image)


def second_diagonal_call(upper, lower, row_sums, noise, image, got):
    probes, size = image.shape
    return pl.pallas_call(
        second_diagonal_kernel,
        in_specs=[VMEM] * 6,
        out_specs=VMEM,
        out_shape=pltpu.VMEM((probes, size), f32),
        scratch_shapes=[pltpu.VMEM((2 * probes, size), bf16)],
        compiler_params=params(16),
    )(upper, lower, row_sums, noise, image, got)


def second_call(devices, *arrays):
    probes, size = arrays[2].shape
    return pl.pallas_call(
        second_kernel,
        in_specs=[VMEM] * len(arrays),
        out_specs=[VMEM] * 2,
        out_shape=[pltpu.VMEM((probes, size), f32), pltpu.VMEM((devices, 8, 128), f32)],
        compiler_params=params(16),
    )(*arrays)


def final_call(sums, right_side, images, images2):
    probes = right_side.shape[0]
    size = images[0].shape[1]
    members = len(images)
    return pl.pallas_call(
        final_kernel,
        in_specs=[VMEM] * (2 + 2 * members),
        out_specs=[HBM, HBM],
        out_shape=[shaped(*right_side.shape)] * 2,
        scratch_shapes=[
            pltpu.VMEM((members, probes, size), f32),
            pltpu.VMEM((members, probes, size), f32),
            pltpu.SemaphoreType.DMA((2, members)),
        ],
        compiler_params=params(16),
    )(sums, right_side, *images, *images2)


def device_of(block):
    members = lax.axis_size("pair")
    group, at = divmod(block, members)
    return group * members + (at ^ ((members - 1) * (group & 1)))


def moved(x, distance):
    count = lax.axis_size(BOTH[0]) * lax.axis_size(BOTH[1])
    route = [
        (device_of(i), device_of(i + distance)) for i in range(count) if 0 <= i + distance < count
    ]
    return lax.ppermute(x, BOTH, route)


def exchanged(x, distance):
    count = lax.axis_size(BOTH[0]) * lax.axis_size(BOTH[1])
    return lax.ppermute(x, BOTH, [(i, i ^ distance) for i in range(count)])


def sent_from_next_group(x, aside):
    members = lax.axis_size("pair")
    route = []
    for g in range(lax.axis_size("blk") - 1):
        target = device_of(g * members + members - 1)
        route.append(((target + members) ^ aside, target))
    return lax.ppermute(x, BOTH, route)


def own_block_body(features, inv_scale, signal, noise_var, right_side, block_pairs):
    members = lax.axis_size("pair")
    devices = members * lax.axis_size("blk")
    size = features.shape[1] // members
    probes = right_side.shape[0]

    features, begins, scale, noise, listing = (
        pltpu.with_memory_space_constraint(x, pltpu.HBM)
        for x in (features, right_side, inv_scale[None, :], noise_var[None, :], block_pairs.T)
    )
    send, send_rest, raw, direction, raw_next, dir_next, noise, scale, found = loading_call(
        features, begins, noise, scale, listing, size
    )
    spans = [1 << k for k in range(members.bit_length() - 1)]
    sent = sent_from_next_group(send, 0)
    sent_rest = sent_from_next_group(send_rest, members // 2)
    found = found + exchanged(found, spans[-1])
    split = UPPER_STRIPS * CHUNK
    tile, diagonal, left, right, half = diagonal_call(signal, raw, scale, direction, split)
    for span in reversed(spans[:-1]):
        found, left = lax.optimization_barrier((found, left))
        found = found + exchanged(found, span)
    cross_tile, row_sums, crossed, over, next_dir, mark = crossing_call(
        signal, found, raw_next, dir_next, sent, sent_rest, scale, left, half, direction, noise
    )
    got = moved(over, 1)
    lower_tile, own = lower_diagonal_call(signal, left, right, half, diagonal, crossed, size - split)
    part = moved(own, -1)
    image = own + got[:probes]
    images = {0: image}
    for span in spans:
        images[span] = exchanged(image, span)
    over2 = over_call(mark, cross_tile, image)
    partial = second_diagonal_call(tile, lower_tile, row_sums, noise, image, got)
    own2, sums = second_call(
        devices, mark, cross_tile, direction, next_dir, image, part, over, over2, partial
    )
    image2 = own2 + moved(over2, 1)
    images2 = {0: image2}
    for span in spans:
        images2[span] = exchanged(image2, span)
    image2, images, sums = lax.optimization_barrier((image2, images, sums))
    sums = lax.all_to_all(sums, BOTH, 0, 0)
    images, images2, sums = lax.optimization_barrier((images, images2, sums))
    for held in (images, images2):
        for span in spans:
            for at in range(1, span):
                held[at + span] = exchanged(held[span], at)
    return tuple(
        final_call(
            sums,
            right_side,
            [images[k] for k in range(members)],
            [images2[k] for k in range(members)],
        )
    )


def passed_along(block, axis, distance):
    devices = range(lax.axis_size(axis))
    route = [(i - distance, i) for i in devices if i - distance in devices]
    return lax.ppermute(block, axis, route)


def kernel_tile(left_scaled, right_scaled, amplitude):
    cross = lax.dot_general(
        left_scaled,
        right_scaled,
        (((0,), (0,)), ((), ())),
        precision=lax.Precision.HIGHEST,
        preferred_element_type=jnp.float32,
    )
    left_norms = jnp.sum(left_scaled * left_scaled, axis=0)
    right_norms = jnp.sum(right_scaled * right_scaled, axis=0)
    squared = (left_norms[:, None] + right_norms[None, :] - 2.0 * cross) / left_scaled.shape[0]
    distance = jnp.sqrt(jnp.maximum(squared, 0.0))
    stretched = root_three * distance
    ratio = distance / taper_radius
    taper = jnp.maximum(1.0 - ratio, 0.0) ** 4 * (1.0 + 4.0 * ratio)
    return amplitude * (1.0 + stretched) * jnp.exp(-stretched) * taper


def block_terms(left_scaled, right_scaled, left_dir, right_dir, amplitude):
    block_rows = left_scaled.shape[1]
    row_step = min(512, block_rows)
    left_half = left_dir.astype(jnp.bfloat16)
    right_half = right_dir.astype(jnp.bfloat16)

    def rows_visit(position, carried):
        toward_left, toward_right, row_sums, col_sums = carried
        offset = position * row_step
        kernel_rows = kernel_tile(
            lax.dynamic_slice_in_dim(left_scaled, offset, row_step, 1), right_scaled, amplitude
        )
        rows_half = kernel_rows.astype(jnp.bfloat16)
        product = lax.dot_general(
            right_half, rows_half, (((1,), (1,)), ((), ())), preferred_element_type=jnp.float32
        )
        toward_left = lax.dynamic_update_slice_in_dim(toward_left, product, offset, 1)
        toward_right = toward_right + jnp.dot(
            lax.dynamic_slice_in_dim(left_half, offset, row_step, 1),
            rows_half,
            preferred_element_type=jnp.float32,
        )
        row_sums = lax.dynamic_update_slice_in_dim(
            row_sums, jnp.sum(kernel_rows, axis=1), offset, 0
        )
        col_sums = col_sums + jnp.sum(kernel_rows, axis=0)
        return (toward_left, toward_right, row_sums, col_sums)

    zeros_dir = jnp.zeros(left_dir.shape, jnp.float32)
    zeros_row = jnp.zeros((block_rows,), jnp.float32)
    return lax.fori_loop(
        0, block_rows // row_step, rows_visit, (zeros_dir, zeros_dir, zeros_row, zeros_row)
    )


def body(features, inv_scale, signal, noise_var, right_side, block_pairs):
    local_rows = features.shape[1]
    blocks_here = local_rows // BS
    amplitude = signal[0]
    scaled = features * inv_scale[:, None]
    beyond = passed_along(scaled[:, :BS], "blk", -1)
    reach_scaled = jnp.concatenate([scaled, beyond], axis=1)
    base_block = lax.axis_index("blk") * blocks_here
    members = lax.axis_size("pair")
    listing = lax.all_gather(block_pairs, "pair", axis=0, tiled=True)
    living = (listing[:, 0] >= 0).astype(jnp.int32)
    ranked = jnp.cumsum(living) - living
    wanted = lax.axis_index("pair") + members * jnp.arange(block_pairs.shape[0], dtype=jnp.int32)
    matched = (ranked[None, :] == wanted[:, None]) & (living[None, :] > 0)
    chosen = jnp.sum(jnp.where(matched[:, :, None], listing[None, :, :], 0), axis=1)
    my_pairs = jnp.where(jnp.any(matched, axis=1)[:, None], chosen, -1)
    active = jnp.maximum((jnp.sum(living) - lax.axis_index("pair") + members - 1) // members, 0)
    row_local = my_pairs[:, 0] - base_block
    col_local = my_pairs[:, 1] - base_block
    solution = jnp.zeros_like(right_side)
    residual = right_side
    direction = right_side
    norm_now = lax.psum(jnp.sum(residual * residual, axis=1), "blk")
    for iteration in range(ITERS):
        ahead_dir = passed_along(direction[:, :BS], "blk", -1)
        reach_dir = jnp.concatenate([direction, ahead_dir], axis=1)

        def visit(slot_index, summed):
            row_start = row_local[slot_index] * BS
            col_start = col_local[slot_index] * BS
            crossing = (row_local[slot_index] != col_local[slot_index]).astype(jnp.float32)
            left_dir = lax.dynamic_slice_in_dim(reach_dir, row_start, BS, 1)
            right_dir = lax.dynamic_slice_in_dim(reach_dir, col_start, BS, 1)
            toward_left, toward_right, row_sums, col_sums = block_terms(
                lax.dynamic_slice_in_dim(reach_scaled, row_start, BS, 1),
                lax.dynamic_slice_in_dim(reach_scaled, col_start, BS, 1),
                left_dir,
                right_dir,
                amplitude,
            )
            term_left = toward_left + crossing * row_sums[None, :] * left_dir
            term_right = crossing * (toward_right + col_sums[None, :] * right_dir)
            summed = lax.dynamic_update_slice_in_dim(
                summed, lax.dynamic_slice_in_dim(summed, row_start, BS, 1) + term_left, row_start, 1
            )
            summed = lax.dynamic_update_slice_in_dim(
                summed,
                lax.dynamic_slice_in_dim(summed, col_start, BS, 1) + term_right,
                col_start,
                1,
            )
            return summed

        summed = lax.fori_loop(0, active, visit, jnp.zeros(reach_dir.shape, jnp.float32))
        own_part = summed[:, :local_rows]
        next_part = summed[:, local_rows:]
        own_sum, next_sum = lax.psum((own_part, next_part), "pair")
        entering = passed_along(next_sum, "blk", 1)
        coupled = jnp.concatenate([own_sum[:, :BS] + entering, own_sum[:, BS:]], axis=1)
        applied = noise_var[None, :] * direction + coupled
        last_turn = iteration + 1 == ITERS
        curvature = lax.psum(jnp.sum(direction * applied, axis=1), "blk")
        step_size = norm_now / curvature
        solution = solution + step_size[:, None] * direction
        residual = residual - step_size[:, None] * applied
        if not last_turn:
            norm_next = lax.psum(jnp.sum(residual * residual, axis=1), "blk")
            direction = residual + (norm_next / norm_now)[:, None] * direction
            norm_now = norm_next
    return (solution, residual)


def solution(mesh):
    members = mesh.shape["pair"]
    groups = mesh.shape["blk"]

    def chosen(features, *rest):
        one_block_each = features.shape[1] == members * BS and BS % CHUNK == 0 and BS > UPPER_STRIPS * CHUNK
        powers = members > 1 and members & (members - 1) == 0 and groups & (groups - 1) == 0
        each = own_block_body if one_block_each and powers else body
        return each(features, *rest)

    placed = (P(None, "blk"), P(), P(), P("blk"), P(None, "blk"), P(("blk", "pair"), None))
    return jax.shard_map(
        chosen,
        mesh=mesh,
        in_specs=placed,
        out_specs=(P(None, "blk"), P(None, "blk")),
        check_vma=False,
    )
```

```python
import functools
import math

import jax
import jax.numpy as jnp
from jax import lax
from jax.experimental import pallas as pl
from jax.experimental.pallas import tpu as pltpu
from jax.sharding import PartitionSpec as P

BS = 2048
ITERS = 2

f32 = jnp.float32
bf16 = jnp.bfloat16
root_three = 1.7320508075688772
taper_radius = 2.0
BOTH = ("blk", "pair")
NT = (((1,), (1,)), ((), ()))
CHUNK = 256
UPPER_STRIPS = 2

RATE = taper_radius * root_three * math.log2(math.e)
NEAR = math.log2(math.e)
FAR = RATE / 4.0
UNIT = NEAR * FAR * RATE**4


def parts_of(x):
    high = x.astype(bf16)
    rest = x - high.astype(f32)
    middle = rest.astype(bf16)
    low = (rest - middle.astype(f32)).astype(bf16)
    return high, middle, low


def norm_parts(points, axis, first):
    norms = jnp.sum(points * points, axis=axis, keepdims=True)
    high, middle, low = (x.astype(f32) for x in parts_of(norms))
    at = lax.broadcasted_iota(jnp.int32, points.shape, axis)
    ones = jnp.where(at < 6, 1.0, 0.0)
    placed = jnp.where(at == first + 2, low, ones)
    placed = jnp.where(at == first + 1, middle, placed)
    return jnp.where(at == first, high, placed).astype(bf16)


def left_parts(points):
    turned = points.T
    high, middle, _ = parts_of(turned)
    return jnp.concatenate([high, high, middle, norm_parts(turned, 1, 0)], axis=1)


def right_parts(points):
    high, middle, _ = parts_of(-2.0 * points)
    return jnp.concatenate([high, middle, high, norm_parts(points, 0, 3)], axis=0)


def points_of(features, inv_scale):
    depth = features.shape[0]
    scale = jnp.broadcast_to(inv_scale, (8, depth)).T[:, 0:1]
    return features * scale * (RATE / (taper_radius * math.sqrt(depth)))


def level_of(signal):
    return jnp.log2(jnp.full((1, CHUNK), signal * (1.0 / UNIT), f32))


def kernel_values(squared, level):
    squared = jnp.maximum(squared, 1e-30)
    s = squared * lax.rsqrt(squared)
    decay = jnp.exp2(level - s)
    u = jnp.maximum(RATE - s, 0.0)
    u2 = u * u
    return ((s + NEAR) * (s + FAR) * decay) * (u2 * u2)


def dot(a, b):
    return jnp.dot(a, b, preferred_element_type=f32)


def dot_nt(a, b):
    return lax.dot_general(a, b, NT, preferred_element_type=f32)


def own_block():
    members = lax.axis_size("pair")
    return lax.axis_index("pair") ^ ((members - 1) * (lax.axis_index("blk") & 1))


def found_in(listing, shape):
    wanted = lax.axis_index("blk") * lax.axis_size("pair") + lax.broadcasted_iota(jnp.int32, shape, 1)
    found = jnp.zeros(shape, f32)
    for slot in range(listing.shape[1]):
        first, second = listing[0:1, slot : slot + 1], listing[1:2, slot : slot + 1]
        found = jnp.where((first == wanted) & (second == wanted + 1), 1.0, found)
    return found


def is_live(found):
    lane = lax.broadcasted_iota(jnp.int32, found.shape, 1)
    return jnp.max(jnp.where(lane == own_block(), found, 0.0)) > 0.0


def cut(at):
    return slice(at * CHUNK, (at + 1) * CHUNK)


def two_sum(a, b):
    total = a + b
    back = total - a
    return total, (a - (total - back)) + (b - back)


def two_product(a, b):
    def halves(x):
        big = x * 4097.0
        high = big - (big - x)
        return high, x - high

    product = a * b
    a_high, a_low = halves(a)
    b_high, b_low = halves(b)
    error = ((a_high * b_high - product) + a_high * b_low + a_low * b_high) + a_low * b_low
    return product, error


def plus(x, y):
    total, error = two_sum(x[0], y[0])
    return two_sum(total, error + (x[1] + y[1]))


def times(x, factor):
    product, error = two_product(x[0], factor)
    return two_sum(product, error + x[1] * factor)


def lane_tiles_sum(x):
    high = x[:, 0:128]
    low = jnp.zeros_like(high)
    for at in range(128, x.shape[1], 128):
        high, error = two_sum(high, x[:, at : at + 128])
        low = low + error
    return high, low


def lanes_sum(high, low):
    shift = 64
    while shift:
        high, error = two_sum(high, pltpu.roll(high, shift, 1))
        low = low + pltpu.roll(low, shift, 1) + error
        shift //= 2
    return high, low


def loading_kernel(
    features,
    right_side,
    noise_var,
    inv_scale,
    block_pairs,
    send,
    send_rest,
    raw,
    direction,
    raw_next,
    next_dir,
    noise,
    scale,
    found,
    listing,
    sems,
):
    size = raw.shape[1]
    depth = raw.shape[0]
    cut_at = send.shape[0]
    mine = own_block()
    after = jnp.minimum(mine + 1, lax.axis_size("pair") - 1)
    here = pl.ds(pl.multiple_of(mine * size, size), size)
    there = pl.ds(pl.multiple_of(after * size, size), size)
    moves = [
        (features.at[:cut_at, :size], send),
        (features.at[cut_at:, :size], send_rest.at[: depth - cut_at]),
        (right_side.at[:, :size], send_rest.at[depth - cut_at :]),
        (features.at[:, here], raw),
        (right_side.at[:, here], direction),
        (features.at[:, there], raw_next),
        (right_side.at[:, there], next_dir),
        (noise_var.at[:, here], noise),
        (inv_scale, scale),
        (block_pairs, listing),
    ]
    copies = [
        pltpu.make_async_copy(source, target, sems.at[k])
        for k, (source, target) in enumerate(moves)
    ]
    for copy in copies:
        copy.start()
    for copy in copies:
        copy.wait()
    found[...] = found_in(listing, found.shape)


def diagonal_products(level, first, tile, own, left, right, half, ahead):
    size = tile.shape[1]
    count = size // CHUNK
    begin = first // CHUNK
    order = [
        (row, col) for row in range(begin, begin + tile.shape[0] // CHUNK) for col in range(row, count)
    ]

    def argument(k):
        row, col = order[k]
        ahead[k % 2] = dot(left[cut(row), :], right[:, cut(col)])

    def product(k):
        row, col = order[k]
        block = tile[cut(row - begin), cut(col)]
        own[:, cut(col)] += dot(half[:, cut(row)], block)
        if col > row:
            own[:, cut(row)] += dot_nt(half[:, cut(col)], block)

    argument(0)
    for k, (row, col) in enumerate(order):
        if k + 1 < len(order):
            argument(k + 1)
        if k:
            product(k - 1)
        tile[cut(row - begin), cut(col)] = kernel_values(ahead[k % 2], level).astype(bf16)
    product(len(order) - 1)


def diagonal_kernel(signal, raw, scale, direction, tile, own, left, right, half, ahead):
    points = points_of(raw[...], scale[...])
    left[...] = left_parts(points)
    right[...] = right_parts(points)
    half[...] = direction[...].astype(bf16)
    own[...] = jnp.zeros_like(own)
    diagonal_products(level_of(signal[0]), 0, tile, own, left, right, half, ahead)


def lower_diagonal_kernel(signal, left, right, half, upper, crossed, tile, own, ahead):
    own[...] = upper[...] + crossed[...]
    first = tile.shape[1] - tile.shape[0]
    diagonal_products(level_of(signal[0]), first, tile, own, left, right, half, ahead)


def crossing_kernel(
    signal,
    found,
    raw_next,
    dir_next,
    sent,
    sent_rest,
    scale,
    left,
    half,
    direction,
    noise,
    tile,
    row_sums,
    own,
    over,
    next_dir,
    mark,
    right,
    half_next,
    ahead,
    col_part,
    row_part,
):
    size = tile.shape[0]
    probes = own.shape[0]
    last = own_block() == lax.axis_size("pair") - 1
    rest = raw_next.shape[0] - sent.shape[0]
    next_dir[...] = jnp.where(last, sent_rest[rest:], dir_next[...])
    live = is_live(found[...])
    mark[...] = jnp.where(live, jnp.ones(mark.shape, f32), jnp.zeros(mark.shape, f32))
    own[...] = jnp.zeros_like(own)
    over[...] = jnp.zeros_like(over)
    row_sums[...] = jnp.zeros_like(row_sums)

    @pl.when(live)
    def _():
        level = level_of(signal[0])
        raw = jnp.concatenate([sent[...], sent_rest[:rest]], axis=0)
        raw = jnp.where(last, raw, raw_next[...])
        right[...] = right_parts(points_of(raw, scale[...]))
        half_next[...] = next_dir[...].astype(bf16)
        col_part[...] = jnp.zeros_like(col_part)
        row_part[...] = jnp.zeros_like(row_part)
        count = size // CHUNK
        order = [(row, col) for row in range(count) for col in range(count)]

        def argument(k):
            row, col = order[k]
            ahead[k % 2] = dot(left[cut(row), :], right[:, cut(col)])

        def product(k):
            row, col = order[k]
            block = tile[cut(row), cut(col)]
            over[:probes, cut(col)] += dot(half[:, cut(row)], block)
            own[:, cut(row)] += dot_nt(half_next[:, cut(col)], block)

        argument(0)
        for k, (row, col) in enumerate(order):
            if k + 1 < len(order):
                argument(k + 1)
            if k:
                product(k - 1)
            values = kernel_values(ahead[k % 2], level)
            tile[cut(row), cut(col)] = values.astype(bf16)
            col_part[:, cut(col)] += jnp.sum(values.reshape(CHUNK // 8, 8, CHUNK), axis=0)
            along = values[:, 0:128]
            for lane in range(128, CHUNK, 128):
                along = along + values[:, lane : lane + 128]
            row_part[cut(row), :] += along
        product(len(order) - 1)
        row_sums[...] = lax.dot_general(
            jnp.ones((8, 128), f32),
            row_part[...],
            NT,
            precision=lax.Precision.HIGHEST,
            preferred_element_type=f32,
        )
        columns = jnp.sum(col_part[...], axis=0, keepdims=True)
        over[:probes] += columns * next_dir[...]
        over[probes : probes + 1] = columns

    own[...] += (noise[...] + row_sums[0:1, :]) * direction[...]


def both_parts(x):
    high = x.astype(bf16)
    return jnp.concatenate([high, (x - high.astype(f32)).astype(bf16)], axis=0)


def folded(x):
    half = x.shape[0] // 2
    return x[:half] + x[half:]


def over_kernel(mark, tile, image, over2):
    live = jnp.max(mark[...]) > 0.0

    @pl.when(live)
    def _():
        over2[...] = folded(dot(both_parts(image[...]), tile[...]))

    @pl.when(jnp.logical_not(live))
    def _():
        over2[...] = jnp.zeros_like(over2)


def second_diagonal_kernel(upper, lower, row_sums, noise, image, got, own2, both):
    size = upper.shape[1]
    probes = image.shape[0]
    here = image[...]
    both[...] = both_parts(here)
    own2[...] = (noise[...] + row_sums[0:1, :] + got[probes : probes + 1, :]) * here
    for tile, first in ((upper, 0), (lower, upper.shape[0])):
        for at in range(first, first + tile.shape[0], CHUNK):
            rows = slice(at, at + CHUNK)
            inside = slice(at - first, at - first + CHUNK)
            rest = slice(at + CHUNK, size)
            own2[:, at:] += folded(dot(both[:, rows], tile[inside, at:]))
            if at + CHUNK < size:
                own2[:, rows] += folded(dot_nt(both[:, rest], tile[inside, rest]))


def second_kernel(
    mark, cross_tile, direction, next_dir, image, part, over, over2, partial, own2, sums
):
    probes = image.shape[0]
    here = image[...]
    own2[...] = partial[...]
    there = part[...] + over[:probes]

    @pl.when(jnp.max(mark[...]) > 0.0)
    def _():
        own2[...] += folded(dot_nt(both_parts(there), cross_tile[...]))

    begin = direction[...]
    mine = own2[...]
    theirs = over2[...]
    squares = here * here
    forms = [
        begin * begin,
        begin * here,
        squares,
        squares + begin * mine + next_dir[...] * theirs,
        here * mine + there * theirs,
    ]
    pairs = [lane_tiles_sum(x) for x in forms]
    high, low = lanes_sum(
        jnp.concatenate([x for x, _ in pairs], axis=0), jnp.concatenate([x for _, x in pairs], axis=0)
    )
    rows = [(high, 0), (low, 0), (high, 1), (low, 1), (high, 2), (low, 2), (high, 3), (high, 4)]
    lane = lax.broadcasted_iota(jnp.int32, (probes, 128), 1)
    out = jnp.zeros((probes, 128), f32)
    for k, (values, at) in enumerate(rows):
        out = jnp.where(lane == k, values[at * probes : (at + 1) * probes], out)
    square = jnp.concatenate([out, jnp.zeros((128 - probes, 128), f32)], axis=0)
    turned = square.T[: len(rows)]
    for k in range(sums.shape[0]):
        sums[k] = turned


def final_kernel(sums, right_side, *rest):
    members = lax.axis_size("pair")
    images, images2 = rest[:members], rest[members : 2 * members]
    solution_out, residual_out, solved, left_over, put_sems = rest[2 * members :]
    probes, size = solved.shape[1:]
    mine = own_block()

    def block(k):
        return pl.ds(pl.multiple_of((mine ^ k) * size, size), size)

    runs = [two_sum(sums[k], sums[k + 4]) for k in range(4)]
    for k in range(8, sums.shape[0]):
        total, error = runs[k % 4]
        total, missed = two_sum(total, sums[k])
        runs[k % 4] = (total, error + missed)
    while len(runs) > 1:
        joined = []
        for (a, a_error), (b, b_error) in zip(runs[::2], runs[1::2]):
            total, missed = two_sum(a, b)
            joined.append((total, a_error + b_error + missed))
        runs = joined
    total, error = runs[0]
    empty = jnp.zeros((128 - total.shape[0], 128), f32)
    total = jnp.concatenate([total, empty], axis=0).T[:probes]
    error = jnp.concatenate([error, empty], axis=0).T[:probes]
    square, form, image_square = (
        (total[:, k : k + 1], total[:, k + 1 : k + 2] + error[:, k : k + 1]) for k in (0, 2, 4)
    )
    mixed, image_form = (total[:, k : k + 1] for k in (6, 7))
    alpha = square[0] / form[0]
    new = plus(plus(square, times(form, -2.0 * alpha)), times(times(image_square, alpha), alpha))[0]
    beta = new / square[0]
    less = form[0] - alpha * mixed
    curvature = (less + alpha * alpha * image_form) + beta * ((form[0] + less) + beta * form[0])
    alpha2 = new / curvature
    puts = []
    for k in range(members):
        begin = right_side[:, block(k)]
        image = images[k][...]
        after = begin - alpha * image
        solved[k] = alpha * begin + alpha2 * (after + beta * begin)
        left_over[k] = after - alpha2 * ((image - alpha * images2[k][...]) + beta * image)
        for at, (source, target) in enumerate(((solved, solution_out), (left_over, residual_out))):
            puts.append(
                pltpu.make_async_copy(source.at[k], target.at[:, block(k)], put_sems.at[at, k])
            )
            puts[-1].start()
    for put in puts:
        put.wait()


def params(mebibytes):
    return pltpu.CompilerParams(vmem_limit_bytes=mebibytes << 20)


def taking(microseconds):
    return pl.CostEstimate(
        flops=int(microseconds * 1.0e9), transcendentals=0, bytes_accessed=int(microseconds * 3.0e6)
    )


def shaped(*shape):
    return jax.ShapeDtypeStruct(shape, f32)


VMEM = pl.BlockSpec(memory_space=pltpu.VMEM)
SMEM = pl.BlockSpec(memory_space=pltpu.SMEM)
HBM = pl.BlockSpec(memory_space=pltpu.HBM)
ANY = pl.BlockSpec(memory_space=pl.ANY)


def loading_call(features, right_side, noise_var, inv_scale, block_pairs, size):
    depth = features.shape[0]
    probes = right_side.shape[0]
    half = min(depth, (depth + probes) // 16 * 8)
    shapes = [
        (half, size),
        (depth + probes - half, size),
        (depth, size),
        (probes, size),
        (depth, size),
        (probes, size),
        (1, size),
        (1, depth),
        (8, 128),
    ]
    return pl.pallas_call(
        loading_kernel,
        in_specs=[HBM] * 5,
        out_specs=[VMEM] * len(shapes),
        out_shape=[pltpu.VMEM(shape, f32) for shape in shapes],
        scratch_shapes=[
            pltpu.VMEM(block_pairs.shape, jnp.int32),
            pltpu.SemaphoreType.DMA((len(shapes) + 1,)),
        ],
        cost_estimate=taking(2),
        compiler_params=params(16),
    )(features, right_side, noise_var, inv_scale, block_pairs)


def diagonal_call(signal, raw, scale, direction, rows):
    depth, size = raw.shape
    probes = direction.shape[0]
    return pl.pallas_call(
        diagonal_kernel,
        in_specs=[SMEM, VMEM, VMEM, VMEM],
        out_specs=[VMEM] * 5,
        out_shape=[
            pltpu.VMEM((rows, size), bf16),
            pltpu.VMEM((probes, size), f32),
            pltpu.VMEM((size, 4 * depth), bf16),
            pltpu.VMEM((4 * depth, size), bf16),
            pltpu.VMEM((probes, size), bf16),
        ],
        scratch_shapes=[pltpu.VMEM((2, CHUNK, CHUNK), f32)],
        cost_estimate=taking(4),
        compiler_params=params(16),
    )(signal, raw, scale, direction)


def lower_diagonal_call(signal, left, right, half, upper, crossed, rows):
    probes, size = upper.shape
    return pl.pallas_call(
        lower_diagonal_kernel,
        in_specs=[SMEM] + [VMEM] * 5,
        out_specs=[VMEM] * 2,
        out_shape=[pltpu.VMEM((rows, size), bf16), pltpu.VMEM((probes, size), f32)],
        scratch_shapes=[pltpu.VMEM((2, CHUNK, CHUNK), f32)],
        cost_estimate=taking(4),
        compiler_params=params(16),
    )(signal, left, right, half, upper, crossed)


def crossing_call(signal, *arrays):
    raw_next, direction = arrays[1], arrays[8]
    depth, size = raw_next.shape
    probes = direction.shape[0]
    return pl.pallas_call(
        crossing_kernel,
        in_specs=[SMEM] + [VMEM] * len(arrays),
        out_specs=[VMEM] * 6,
        out_shape=[
            pltpu.VMEM((size, size), bf16),
            pltpu.VMEM((8, size), f32),
            pltpu.VMEM((probes, size), f32),
            pltpu.VMEM((probes + 8, size), f32),
            pltpu.VMEM((probes, size), f32),
            pltpu.VMEM((8, 128), f32),
        ],
        scratch_shapes=[
            pltpu.VMEM((4 * depth, size), bf16),
            pltpu.VMEM((probes, size), bf16),
            pltpu.VMEM((2, CHUNK, CHUNK), f32),
            pltpu.VMEM((8, size), f32),
            pltpu.VMEM((size, 128), f32),
        ],
        cost_estimate=taking(12),
        compiler_params=params(16),
    )(signal, *arrays)


def over_call(mark, tile, image):
    return pl.pallas_call(
        over_kernel,
        in_specs=[VMEM] * 3,
        out_specs=VMEM,
        out_shape=pltpu.VMEM(image.shape, f32),
        cost_estimate=taking(2),
        compiler_params=params(16),
    )(mark, tile, image)


def second_diagonal_call(upper, lower, row_sums, noise, image, got):
    probes, size = image.shape
    return pl.pallas_call(
        second_diagonal_kernel,
        in_specs=[VMEM] * 6,
        out_specs=VMEM,
        out_shape=pltpu.VMEM((probes, size), f32),
        scratch_shapes=[pltpu.VMEM((2 * probes, size), bf16)],
        cost_estimate=taking(2),
        compiler_params=params(16),
    )(upper, lower, row_sums, noise, image, got)


def second_call(devices, *arrays):
    probes, size = arrays[2].shape
    return pl.pallas_call(
        second_kernel,
        in_specs=[VMEM] * len(arrays),
        out_specs=[VMEM] * 2,
        out_shape=[pltpu.VMEM((probes, size), f32), pltpu.VMEM((devices, 8, 128), f32)],
        cost_estimate=taking(4),
        compiler_params=params(16),
    )(*arrays)


def final_call(sums, right_side, images, images2):
    probes = right_side.shape[0]
    size = images[0].shape[1]
    members = len(images)
    return pl.pallas_call(
        final_kernel,
        in_specs=[VMEM] * (2 + 2 * members),
        out_specs=[HBM, HBM],
        out_shape=[shaped(*right_side.shape)] * 2,
        scratch_shapes=[
            pltpu.VMEM((members, probes, size), f32),
            pltpu.VMEM((members, probes, size), f32),
            pltpu.SemaphoreType.DMA((2, members)),
        ],
        cost_estimate=taking(3),
        compiler_params=params(16),
    )(sums, right_side, *images, *images2)


def device_of(block):
    members = lax.axis_size("pair")
    group, at = divmod(block, members)
    return group * members + (at ^ ((members - 1) * (group & 1)))


def moved(x, distance):
    count = lax.axis_size(BOTH[0]) * lax.axis_size(BOTH[1])
    route = [
        (device_of(i), device_of(i + distance)) for i in range(count) if 0 <= i + distance < count
    ]
    return lax.ppermute(x, BOTH, route)


def exchanged(x, distance):
    count = lax.axis_size(BOTH[0]) * lax.axis_size(BOTH[1])
    return lax.ppermute(x, BOTH, [(i, i ^ distance) for i in range(count)])


def sent_from_next_group(x, aside):
    members = lax.axis_size("pair")
    route = []
    for g in range(lax.axis_size("blk") - 1):
        target = device_of(g * members + members - 1)
        route.append(((target + members) ^ aside, target))
    return lax.ppermute(x, BOTH, route)


def own_block_body(features, inv_scale, signal, noise_var, right_side, block_pairs):
    members = lax.axis_size("pair")
    devices = members * lax.axis_size("blk")
    size = features.shape[1] // members
    probes = right_side.shape[0]

    features, begins, scale, noise, listing = (
        pltpu.with_memory_space_constraint(x, pltpu.HBM)
        for x in (features, right_side, inv_scale[None, :], noise_var[None, :], block_pairs.T)
    )
    send, send_rest, raw, direction, raw_next, dir_next, noise, scale, found = loading_call(
        features, begins, noise, scale, listing, size
    )
    spans = [1 << k for k in range(members.bit_length() - 1)]
    sent = sent_from_next_group(send, 0)
    sent_rest = sent_from_next_group(send_rest, members // 2)
    found = found + exchanged(found, spans[-1])
    split = UPPER_STRIPS * CHUNK
    tile, diagonal, left, right, half = diagonal_call(signal, raw, scale, direction, split)
    for span in reversed(spans[:-1]):
        found, left = lax.optimization_barrier((found, left))
        found = found + exchanged(found, span)
    cross_tile, row_sums, crossed, over, next_dir, mark = crossing_call(
        signal, found, raw_next, dir_next, sent, sent_rest, scale, left, half, direction, noise
    )
    got = moved(over, 1)
    lower_tile, own = lower_diagonal_call(signal, left, right, half, diagonal, crossed, size - split)
    part = moved(own, -1)
    image = own + got[:probes]
    images = {0: image}
    for span in spans:
        images[span] = exchanged(image, span)
    over2 = over_call(mark, cross_tile, image)
    partial = second_diagonal_call(tile, lower_tile, row_sums, noise, image, got)
    own2, sums = second_call(
        devices, mark, cross_tile, direction, next_dir, image, part, over, over2, partial
    )
    image2 = own2 + moved(over2, 1)
    images2 = {0: image2}
    for span in spans:
        images2[span] = exchanged(image2, span)
    image2, images, sums = lax.optimization_barrier((image2, images, sums))
    sums = lax.all_to_all(sums, BOTH, 0, 0)
    images, images2, sums = lax.optimization_barrier((images, images2, sums))
    for held in (images, images2):
        for span in spans:
            for at in range(1, span):
                held[at + span] = exchanged(held[span], at)
    return tuple(
        final_call(
            sums,
            right_side,
            [images[k] for k in range(members)],
            [images2[k] for k in range(members)],
        )
    )


def passed_along(block, axis, distance):
    devices = range(lax.axis_size(axis))
    route = [(i - distance, i) for i in devices if i - distance in devices]
    return lax.ppermute(block, axis, route)


def kernel_tile(left_scaled, right_scaled, amplitude):
    cross = lax.dot_general(
        left_scaled,
        right_scaled,
        (((0,), (0,)), ((), ())),
        precision=lax.Precision.HIGHEST,
        preferred_element_type=jnp.float32,
    )
    left_norms = jnp.sum(left_scaled * left_scaled, axis=0)
    right_norms = jnp.sum(right_scaled * right_scaled, axis=0)
    squared = (left_norms[:, None] + right_norms[None, :] - 2.0 * cross) / left_scaled.shape[0]
    distance = jnp.sqrt(jnp.maximum(squared, 0.0))
    stretched = root_three * distance
    ratio = distance / taper_radius
    taper = jnp.maximum(1.0 - ratio, 0.0) ** 4 * (1.0 + 4.0 * ratio)
    return amplitude * (1.0 + stretched) * jnp.exp(-stretched) * taper


def block_terms(left_scaled, right_scaled, left_dir, right_dir, amplitude):
    block_rows = left_scaled.shape[1]
    row_step = min(512, block_rows)
    left_half = left_dir.astype(jnp.bfloat16)
    right_half = right_dir.astype(jnp.bfloat16)

    def rows_visit(position, carried):
        toward_left, toward_right, row_sums, col_sums = carried
        offset = position * row_step
        kernel_rows = kernel_tile(
            lax.dynamic_slice_in_dim(left_scaled, offset, row_step, 1), right_scaled, amplitude
        )
        rows_half = kernel_rows.astype(jnp.bfloat16)
        product = lax.dot_general(
            right_half, rows_half, (((1,), (1,)), ((), ())), preferred_element_type=jnp.float32
        )
        toward_left = lax.dynamic_update_slice_in_dim(toward_left, product, offset, 1)
        toward_right = toward_right + jnp.dot(
            lax.dynamic_slice_in_dim(left_half, offset, row_step, 1),
            rows_half,
            preferred_element_type=jnp.float32,
        )
        row_sums = lax.dynamic_update_slice_in_dim(
            row_sums, jnp.sum(kernel_rows, axis=1), offset, 0
        )
        col_sums = col_sums + jnp.sum(kernel_rows, axis=0)
        return (toward_left, toward_right, row_sums, col_sums)

    zeros_dir = jnp.zeros(left_dir.shape, jnp.float32)
    zeros_row = jnp.zeros((block_rows,), jnp.float32)
    return lax.fori_loop(
        0, block_rows // row_step, rows_visit, (zeros_dir, zeros_dir, zeros_row, zeros_row)
    )


def body(features, inv_scale, signal, noise_var, right_side, block_pairs):
    local_rows = features.shape[1]
    blocks_here = local_rows // BS
    amplitude = signal[0]
    scaled = features * inv_scale[:, None]
    beyond = passed_along(scaled[:, :BS], "blk", -1)
    reach_scaled = jnp.concatenate([scaled, beyond], axis=1)
    base_block = lax.axis_index("blk") * blocks_here
    members = lax.axis_size("pair")
    listing = lax.all_gather(block_pairs, "pair", axis=0, tiled=True)
    living = (listing[:, 0] >= 0).astype(jnp.int32)
    ranked = jnp.cumsum(living) - living
    wanted = lax.axis_index("pair") + members * jnp.arange(block_pairs.shape[0], dtype=jnp.int32)
    matched = (ranked[None, :] == wanted[:, None]) & (living[None, :] > 0)
    chosen = jnp.sum(jnp.where(matched[:, :, None], listing[None, :, :], 0), axis=1)
    my_pairs = jnp.where(jnp.any(matched, axis=1)[:, None], chosen, -1)
    active = jnp.maximum((jnp.sum(living) - lax.axis_index("pair") + members - 1) // members, 0)
    row_local = my_pairs[:, 0] - base_block
    col_local = my_pairs[:, 1] - base_block
    solution = jnp.zeros_like(right_side)
    residual = right_side
    direction = right_side
    norm_now = lax.psum(jnp.sum(residual * residual, axis=1), "blk")
    for iteration in range(ITERS):
        ahead_dir = passed_along(direction[:, :BS], "blk", -1)
        reach_dir = jnp.concatenate([direction, ahead_dir], axis=1)

        def visit(slot_index, summed):
            row_start = row_local[slot_index] * BS
            col_start = col_local[slot_index] * BS
            crossing = (row_local[slot_index] != col_local[slot_index]).astype(jnp.float32)
            left_dir = lax.dynamic_slice_in_dim(reach_dir, row_start, BS, 1)
            right_dir = lax.dynamic_slice_in_dim(reach_dir, col_start, BS, 1)
            toward_left, toward_right, row_sums, col_sums = block_terms(
                lax.dynamic_slice_in_dim(reach_scaled, row_start, BS, 1),
                lax.dynamic_slice_in_dim(reach_scaled, col_start, BS, 1),
                left_dir,
                right_dir,
                amplitude,
            )
            term_left = toward_left + crossing * row_sums[None, :] * left_dir
            term_right = crossing * (toward_right + col_sums[None, :] * right_dir)
            summed = lax.dynamic_update_slice_in_dim(
                summed, lax.dynamic_slice_in_dim(summed, row_start, BS, 1) + term_left, row_start, 1
            )
            summed = lax.dynamic_update_slice_in_dim(
                summed,
                lax.dynamic_slice_in_dim(summed, col_start, BS, 1) + term_right,
                col_start,
                1,
            )
            return summed

        summed = lax.fori_loop(0, active, visit, jnp.zeros(reach_dir.shape, jnp.float32))
        own_part = summed[:, :local_rows]
        next_part = summed[:, local_rows:]
        own_sum, next_sum = lax.psum((own_part, next_part), "pair")
        entering = passed_along(next_sum, "blk", 1)
        coupled = jnp.concatenate([own_sum[:, :BS] + entering, own_sum[:, BS:]], axis=1)
        applied = noise_var[None, :] * direction + coupled
        last_turn = iteration + 1 == ITERS
        curvature = lax.psum(jnp.sum(direction * applied, axis=1), "blk")
        step_size = norm_now / curvature
        solution = solution + step_size[:, None] * direction
        residual = residual - step_size[:, None] * applied
        if not last_turn:
            norm_next = lax.psum(jnp.sum(residual * residual, axis=1), "blk")
            direction = residual + (norm_next / norm_now)[:, None] * direction
            norm_now = norm_next
    return (solution, residual)


def solution(mesh):
    members = mesh.shape["pair"]
    groups = mesh.shape["blk"]

    def chosen(features, *rest):
        one_block_each = features.shape[1] == members * BS and BS % CHUNK == 0 and BS > UPPER_STRIPS * CHUNK
        powers = members > 1 and members & (members - 1) == 0 and groups & (groups - 1) == 0
        each = own_block_body if one_block_each and powers else body
        return each(features, *rest)

    placed = (P(None, "blk"), P(), P(), P("blk"), P(None, "blk"), P(("blk", "pair"), None))
    return jax.shard_map(
        chosen,
        mesh=mesh,
        in_specs=placed,
        out_specs=(P(None, "blk"), P(None, "blk")),
        check_vma=False,
    )
```

```python
import functools
import math

import jax
import jax.numpy as jnp
from jax import lax
from jax.experimental import pallas as pl
from jax.experimental.pallas import tpu as pltpu
from jax.sharding import PartitionSpec as P

BS = 2048
ITERS = 2

f32 = jnp.float32
bf16 = jnp.bfloat16
root_three = 1.7320508075688772
taper_radius = 2.0
BOTH = ("blk", "pair")
NT = (((1,), (1,)), ((), ()))
CHUNK = 256
UPPER_STRIPS = 2

RATE = taper_radius * root_three * math.log2(math.e)
NEAR = math.log2(math.e)
FAR = RATE / 4.0
UNIT = NEAR * FAR * RATE**4


def parts_of(x):
    high = x.astype(bf16)
    rest = x - high.astype(f32)
    middle = rest.astype(bf16)
    low = (rest - middle.astype(f32)).astype(bf16)
    return high, middle, low


def norm_parts(points, axis, first):
    norms = jnp.sum(points * points, axis=axis, keepdims=True)
    high, middle, low = (x.astype(f32) for x in parts_of(norms))
    at = lax.broadcasted_iota(jnp.int32, points.shape, axis)
    ones = jnp.where(at < 6, 1.0, 0.0)
    placed = jnp.where(at == first + 2, low, ones)
    placed = jnp.where(at == first + 1, middle, placed)
    return jnp.where(at == first, high, placed).astype(bf16)


def left_parts(points):
    turned = points.T
    high, middle, _ = parts_of(turned)
    return jnp.concatenate([high, high, middle, norm_parts(turned, 1, 0)], axis=1)


def right_parts(points):
    high, middle, _ = parts_of(-2.0 * points)
    return jnp.concatenate([high, middle, high, norm_parts(points, 0, 3)], axis=0)


def points_of(features, inv_scale):
    depth = features.shape[0]
    scale = jnp.broadcast_to(inv_scale, (8, depth)).T[:, 0:1]
    return features * scale * (RATE / (taper_radius * math.sqrt(depth)))


def level_of(signal):
    return jnp.log2(jnp.full((1, CHUNK), signal * (1.0 / UNIT), f32))


def kernel_values(squared, level):
    squared = jnp.maximum(squared, 1e-30)
    s = squared * lax.rsqrt(squared)
    decay = jnp.exp2(level - s)
    u = jnp.maximum(RATE - s, 0.0)
    u2 = u * u
    return ((s + NEAR) * (s + FAR) * decay) * (u2 * u2)


def dot(a, b):
    return jnp.dot(a, b, preferred_element_type=f32)


def dot_nt(a, b):
    return lax.dot_general(a, b, NT, preferred_element_type=f32)


def own_block():
    members = lax.axis_size("pair")
    return lax.axis_index("pair") ^ ((members - 1) * (lax.axis_index("blk") & 1))


def found_in(listing, shape):
    wanted = lax.axis_index("blk") * lax.axis_size("pair") + lax.broadcasted_iota(jnp.int32, shape, 1)
    found = jnp.zeros(shape, f32)
    for slot in range(listing.shape[1]):
        first, second = listing[0:1, slot : slot + 1], listing[1:2, slot : slot + 1]
        found = jnp.where((first == wanted) & (second == wanted + 1), 1.0, found)
    return found


def is_live(found):
    lane = lax.broadcasted_iota(jnp.int32, found.shape, 1)
    return jnp.max(jnp.where(lane == own_block(), found, 0.0)) > 0.0


def cut(at):
    return slice(at * CHUNK, (at + 1) * CHUNK)


def two_sum(a, b):
    total = a + b
    back = total - a
    return total, (a - (total - back)) + (b - back)


def two_product(a, b):
    def halves(x):
        big = x * 4097.0
        high = big - (big - x)
        return high, x - high

    product = a * b
    a_high, a_low = halves(a)
    b_high, b_low = halves(b)
    error = ((a_high * b_high - product) + a_high * b_low + a_low * b_high) + a_low * b_low
    return product, error


def plus(x, y):
    total, error = two_sum(x[0], y[0])
    return two_sum(total, error + (x[1] + y[1]))


def times(x, factor):
    product, error = two_product(x[0], factor)
    return two_sum(product, error + x[1] * factor)


def lane_tiles_sum(x):
    high = x[:, 0:128]
    low = jnp.zeros_like(high)
    for at in range(128, x.shape[1], 128):
        high, error = two_sum(high, x[:, at : at + 128])
        low = low + error
    return high, low


def rows_sum(high, low):
    parts = [(high[at : at + 8], low[at : at + 8]) for at in range(0, 128, 8)]
    while len(parts) > 1:
        parts = [
            (total, error + (x[1] + y[1]))
            for x, y in zip(parts[::2], parts[1::2])
            for total, error in (two_sum(x[0], y[0]),)
        ]
    high, low = parts[0]
    for shift in (4, 2, 1):
        high, error = two_sum(high, pltpu.roll(high, shift, 0))
        low = low + pltpu.roll(low, shift, 0) + error
    return high, low


def lane_tiles_plain(x):
    total = x[:, 0:128]
    for at in range(128, x.shape[1], 128):
        total = total + x[:, at : at + 128]
    return total


def padded(pieces):
    rows = sum(piece.shape[0] for piece in pieces)
    return jnp.concatenate([*pieces, jnp.zeros((128 - rows, 128), f32)], axis=0)


def loading_kernel(
    features,
    right_side,
    noise_var,
    inv_scale,
    block_pairs,
    send,
    send_rest,
    raw,
    direction,
    raw_next,
    next_dir,
    noise,
    scale,
    found,
    listing,
    sems,
):
    size = raw.shape[1]
    depth = raw.shape[0]
    cut_at = send.shape[0]
    mine = own_block()
    after = jnp.minimum(mine + 1, lax.axis_size("pair") - 1)
    here = pl.ds(pl.multiple_of(mine * size, size), size)
    there = pl.ds(pl.multiple_of(after * size, size), size)
    moves = [
        (features.at[:cut_at, :size], send),
        (features.at[cut_at:, :size], send_rest.at[: depth - cut_at]),
        (right_side.at[:, :size], send_rest.at[depth - cut_at :]),
        (features.at[:, here], raw),
        (right_side.at[:, here], direction),
        (features.at[:, there], raw_next),
        (right_side.at[:, there], next_dir),
        (noise_var.at[:, here], noise),
        (inv_scale, scale),
        (block_pairs, listing),
    ]
    copies = [
        pltpu.make_async_copy(source, target, sems.at[k])
        for k, (source, target) in enumerate(moves)
    ]
    for copy in copies:
        copy.start()
    for copy in copies:
        copy.wait()
    found[...] = found_in(listing, found.shape)


def diagonal_products(level, first, tile, own, left, right, half, ahead):
    size = tile.shape[1]
    count = size // CHUNK
    begin = first // CHUNK
    order = [
        (row, col) for row in range(begin, begin + tile.shape[0] // CHUNK) for col in range(row, count)
    ]

    def argument(k):
        row, col = order[k]
        ahead[k % 2] = dot(left[cut(row), :], right[:, cut(col)])

    def product(k):
        row, col = order[k]
        block = tile[cut(row - begin), cut(col)]
        own[:, cut(col)] += dot(half[:, cut(row)], block)
        if col > row:
            own[:, cut(row)] += dot_nt(half[:, cut(col)], block)

    argument(0)
    for k, (row, col) in enumerate(order):
        if k + 1 < len(order):
            argument(k + 1)
        if k:
            product(k - 1)
        tile[cut(row - begin), cut(col)] = kernel_values(ahead[k % 2], level).astype(bf16)
    product(len(order) - 1)


def diagonal_kernel(signal, raw, scale, direction, tile, own, left, right, half, ahead):
    points = points_of(raw[...], scale[...])
    left[...] = left_parts(points)
    right[...] = right_parts(points)
    half[...] = direction[...].astype(bf16)
    own[...] = jnp.zeros_like(own)
    diagonal_products(level_of(signal[0]), 0, tile, own, left, right, half, ahead)


def lower_diagonal_kernel(signal, left, right, half, upper, crossed, tile, own, ahead):
    own[...] = upper[...] + crossed[...]
    first = tile.shape[1] - tile.shape[0]
    diagonal_products(level_of(signal[0]), first, tile, own, left, right, half, ahead)


def crossing_kernel(
    signal,
    found,
    raw_next,
    dir_next,
    sent,
    sent_rest,
    scale,
    left,
    half,
    direction,
    noise,
    tile,
    row_sums,
    own,
    over,
    next_dir,
    mark,
    right,
    half_next,
    ahead,
    col_part,
    row_part,
):
    size = tile.shape[0]
    probes = own.shape[0]
    last = own_block() == lax.axis_size("pair") - 1
    rest = raw_next.shape[0] - sent.shape[0]
    next_dir[...] = jnp.where(last, sent_rest[rest:], dir_next[...])
    live = is_live(found[...])
    mark[...] = jnp.where(live, jnp.ones(mark.shape, f32), jnp.zeros(mark.shape, f32))
    own[...] = jnp.zeros_like(own)
    over[...] = jnp.zeros_like(over)
    row_sums[...] = jnp.zeros_like(row_sums)

    @pl.when(live)
    def _():
        level = level_of(signal[0])
        raw = jnp.concatenate([sent[...], sent_rest[:rest]], axis=0)
        raw = jnp.where(last, raw, raw_next[...])
        right[...] = right_parts(points_of(raw, scale[...]))
        half_next[...] = next_dir[...].astype(bf16)
        col_part[...] = jnp.zeros_like(col_part)
        row_part[...] = jnp.zeros_like(row_part)
        count = size // CHUNK
        order = [(row, col) for row in range(count) for col in range(count)]

        def argument(k):
            row, col = order[k]
            ahead[k % 2] = dot(left[cut(row), :], right[:, cut(col)])

        def product(k):
            row, col = order[k]
            block = tile[cut(row), cut(col)]
            over[:probes, cut(col)] += dot(half[:, cut(row)], block)
            own[:, cut(row)] += dot_nt(half_next[:, cut(col)], block)

        argument(0)
        for k, (row, col) in enumerate(order):
            if k + 1 < len(order):
                argument(k + 1)
            if k:
                product(k - 1)
            values = kernel_values(ahead[k % 2], level)
            tile[cut(row), cut(col)] = values.astype(bf16)
            col_part[:, cut(col)] += jnp.sum(values.reshape(CHUNK // 8, 8, CHUNK), axis=0)
            along = values[:, 0:128]
            for lane in range(128, CHUNK, 128):
                along = along + values[:, lane : lane + 128]
            row_part[cut(row), :] += along
        product(len(order) - 1)
        row_sums[...] = lax.dot_general(
            jnp.ones((8, 128), f32),
            row_part[...],
            NT,
            precision=lax.Precision.HIGHEST,
            preferred_element_type=f32,
        )
        columns = jnp.sum(col_part[...], axis=0, keepdims=True)
        over[:probes] += columns * next_dir[...]
        over[probes : probes + 1] = columns

    own[...] += (noise[...] + row_sums[0:1, :]) * direction[...]


def both_parts(x):
    high = x.astype(bf16)
    return jnp.concatenate([high, (x - high.astype(f32)).astype(bf16)], axis=0)


def folded(x):
    half = x.shape[0] // 2
    return x[:half] + x[half:]


def over_kernel(mark, tile, image, over2):
    live = jnp.max(mark[...]) > 0.0

    @pl.when(live)
    def _():
        over2[...] = folded(dot(both_parts(image[...]), tile[...]))

    @pl.when(jnp.logical_not(live))
    def _():
        over2[...] = jnp.zeros_like(over2)


def second_diagonal_kernel(upper, lower, row_sums, noise, image, got, own2, both):
    size = upper.shape[1]
    probes = image.shape[0]
    here = image[...]
    both[...] = both_parts(here)
    own2[...] = (noise[...] + row_sums[0:1, :] + got[probes : probes + 1, :]) * here
    for tile, first in ((upper, 0), (lower, upper.shape[0])):
        for at in range(first, first + tile.shape[0], CHUNK):
            rows = slice(at, at + CHUNK)
            inside = slice(at - first, at - first + CHUNK)
            rest = slice(at + CHUNK, size)
            own2[:, at:] += folded(dot(both[:, rows], tile[inside, at:]))
            if at + CHUNK < size:
                own2[:, rows] += folded(dot_nt(both[:, rest], tile[inside, rest]))


def second_kernel(
    mark, cross_tile, direction, next_dir, image, part, over, over2, partial, own2, sums
):
    probes = image.shape[0]
    here = image[...]
    own2[...] = partial[...]
    there = part[...] + over[:probes]

    @pl.when(jnp.max(mark[...]) > 0.0)
    def _():
        own2[...] += folded(dot_nt(both_parts(there), cross_tile[...]))

    begin = direction[...]
    mine = own2[...]
    theirs = over2[...]
    squares = here * here
    exact = [lane_tiles_sum(x) for x in (begin * begin, begin * here, squares)]
    plain = [
        lane_tiles_plain(x)
        for x in (squares + begin * mine + next_dir[...] * theirs, here * mine + there * theirs)
    ]
    high, low = rows_sum(padded([x for x, _ in exact]).T, padded([x for _, x in exact]).T)
    rest = jnp.sum(padded(plain).T, axis=0, keepdims=True)
    row = lax.broadcasted_iota(jnp.int32, high.shape, 0)
    tile = jnp.where(row == 0, high, jnp.where(row == 1, low, jnp.where(row == 2, rest, 0.0)))
    for k in range(sums.shape[0]):
        sums[k] = tile


def final_kernel(sums, right_side, *rest):
    members = lax.axis_size("pair")
    images, images2 = rest[:members], rest[members : 2 * members]
    solution_out, residual_out, solved, left_over, put_sems = rest[2 * members :]
    probes, size = solved.shape[1:]
    mine = own_block()

    def block(k):
        return pl.ds(pl.multiple_of((mine ^ k) * size, size), size)

    runs = [two_sum(sums[k], sums[k + 4]) for k in range(4)]
    for k in range(8, sums.shape[0]):
        total, error = runs[k % 4]
        total, missed = two_sum(total, sums[k])
        runs[k % 4] = (total, error + missed)
    while len(runs) > 1:
        joined = []
        for (a, a_error), (b, b_error) in zip(runs[::2], runs[1::2]):
            total, missed = two_sum(a, b)
            joined.append((total, a_error + b_error + missed))
        runs = joined
    total, error = runs[0]
    total, error = padded([total]).T, padded([error]).T
    square, form, image_square = (
        (total[at : at + probes, 0:1], total[at : at + probes, 1:2] + error[at : at + probes, 0:1])
        for at in (0, probes, 2 * probes)
    )
    mixed, image_form = (total[at : at + probes, 2:3] for at in (0, probes))
    alpha = square[0] / form[0]
    new = plus(plus(square, times(form, -2.0 * alpha)), times(times(image_square, alpha), alpha))[0]
    beta = new / square[0]
    less = form[0] - alpha * mixed
    curvature = (less + alpha * alpha * image_form) + beta * ((form[0] + less) + beta * form[0])
    alpha2 = new / curvature
    puts = []
    for k in range(members):
        begin = right_side[:, block(k)]
        image = images[k][...]
        after = begin - alpha * image
        solved[k] = alpha * begin + alpha2 * (after + beta * begin)
        left_over[k] = after - alpha2 * ((image - alpha * images2[k][...]) + beta * image)
        for at, (source, target) in enumerate(((solved, solution_out), (left_over, residual_out))):
            puts.append(
                pltpu.make_async_copy(source.at[k], target.at[:, block(k)], put_sems.at[at, k])
            )
            puts[-1].start()
    for put in puts:
        put.wait()


def params(mebibytes):
    return pltpu.CompilerParams(vmem_limit_bytes=mebibytes << 20)


def taking(microseconds):
    return pl.CostEstimate(
        flops=int(microseconds * 1.0e9), transcendentals=0, bytes_accessed=int(microseconds * 3.0e6)
    )


def shaped(*shape):
    return jax.ShapeDtypeStruct(shape, f32)


VMEM = pl.BlockSpec(memory_space=pltpu.VMEM)
SMEM = pl.BlockSpec(memory_space=pltpu.SMEM)
HBM = pl.BlockSpec(memory_space=pltpu.HBM)
ANY = pl.BlockSpec(memory_space=pl.ANY)


def loading_call(features, right_side, noise_var, inv_scale, block_pairs, size):
    depth = features.shape[0]
    probes = right_side.shape[0]
    half = min(depth, (depth + probes) // 16 * 8)
    shapes = [
        (half, size),
        (depth + probes - half, size),
        (depth, size),
        (probes, size),
        (depth, size),
        (probes, size),
        (1, size),
        (1, depth),
        (8, 128),
    ]
    return pl.pallas_call(
        loading_kernel,
        in_specs=[HBM] * 5,
        out_specs=[VMEM] * len(shapes),
        out_shape=[pltpu.VMEM(shape, f32) for shape in shapes],
        scratch_shapes=[
            pltpu.VMEM(block_pairs.shape, jnp.int32),
            pltpu.SemaphoreType.DMA((len(shapes) + 1,)),
        ],
        cost_estimate=taking(2),
        compiler_params=params(16),
    )(features, right_side, noise_var, inv_scale, block_pairs)


def diagonal_call(signal, raw, scale, direction, rows):
    depth, size = raw.shape
    probes = direction.shape[0]
    return pl.pallas_call(
        diagonal_kernel,
        in_specs=[SMEM, VMEM, VMEM, VMEM],
        out_specs=[VMEM] * 5,
        out_shape=[
            pltpu.VMEM((rows, size), bf16),
            pltpu.VMEM((probes, size), f32),
            pltpu.VMEM((size, 4 * depth), bf16),
            pltpu.VMEM((4 * depth, size), bf16),
            pltpu.VMEM((probes, size), bf16),
        ],
        scratch_shapes=[pltpu.VMEM((2, CHUNK, CHUNK), f32)],
        cost_estimate=taking(4),
        compiler_params=params(16),
    )(signal, raw, scale, direction)


def lower_diagonal_call(signal, left, right, half, upper, crossed, rows):
    probes, size = upper.shape
    return pl.pallas_call(
        lower_diagonal_kernel,
        in_specs=[SMEM] + [VMEM] * 5,
        out_specs=[VMEM] * 2,
        out_shape=[pltpu.VMEM((rows, size), bf16), pltpu.VMEM((probes, size), f32)],
        scratch_shapes=[pltpu.VMEM((2, CHUNK, CHUNK), f32)],
        cost_estimate=taking(4),
        compiler_params=params(16),
    )(signal, left, right, half, upper, crossed)


def crossing_call(signal, *arrays):
    raw_next, direction = arrays[1], arrays[8]
    depth, size = raw_next.shape
    probes = direction.shape[0]
    return pl.pallas_call(
        crossing_kernel,
        in_specs=[SMEM] + [VMEM] * len(arrays),
        out_specs=[VMEM] * 6,
        out_shape=[
            pltpu.VMEM((size, size), bf16),
            pltpu.VMEM((8, size), f32),
            pltpu.VMEM((probes, size), f32),
            pltpu.VMEM((probes + 8, size), f32),
            pltpu.VMEM((probes, size), f32),
            pltpu.VMEM((8, 128), f32),
        ],
        scratch_shapes=[
            pltpu.VMEM((4 * depth, size), bf16),
            pltpu.VMEM((probes, size), bf16),
            pltpu.VMEM((2, CHUNK, CHUNK), f32),
            pltpu.VMEM((8, size), f32),
            pltpu.VMEM((size, 128), f32),
        ],
        cost_estimate=taking(12),
        compiler_params=params(16),
    )(signal, *arrays)


def over_call(mark, tile, image):
    return pl.pallas_call(
        over_kernel,
        in_specs=[VMEM] * 3,
        out_specs=VMEM,
        out_shape=pltpu.VMEM(image.shape, f32),
        cost_estimate=taking(2),
        compiler_params=params(16),
    )(mark, tile, image)


def second_diagonal_call(upper, lower, row_sums, noise, image, got):
    probes, size = image.shape
    return pl.pallas_call(
        second_diagonal_kernel,
        in_specs=[VMEM] * 6,
        out_specs=VMEM,
        out_shape=pltpu.VMEM((probes, size), f32),
        scratch_shapes=[pltpu.VMEM((2 * probes, size), bf16)],
        cost_estimate=taking(2),
        compiler_params=params(16),
    )(upper, lower, row_sums, noise, image, got)


def second_call(devices, *arrays):
    probes, size = arrays[2].shape
    return pl.pallas_call(
        second_kernel,
        in_specs=[VMEM] * len(arrays),
        out_specs=[VMEM] * 2,
        out_shape=[pltpu.VMEM((probes, size), f32), pltpu.VMEM((devices, 8, 128), f32)],
        cost_estimate=taking(4),
        compiler_params=params(16),
    )(*arrays)


def final_call(sums, right_side, images, images2):
    probes = right_side.shape[0]
    size = images[0].shape[1]
    members = len(images)
    return pl.pallas_call(
        final_kernel,
        in_specs=[VMEM] * (2 + 2 * members),
        out_specs=[HBM, HBM],
        out_shape=[shaped(*right_side.shape)] * 2,
        scratch_shapes=[
            pltpu.VMEM((members, probes, size), f32),
            pltpu.VMEM((members, probes, size), f32),
            pltpu.SemaphoreType.DMA((2, members)),
        ],
        cost_estimate=taking(3),
        compiler_params=params(16),
    )(sums, right_side, *images, *images2)


def device_of(block):
    members = lax.axis_size("pair")
    group, at = divmod(block, members)
    return group * members + (at ^ ((members - 1) * (group & 1)))


def moved(x, distance):
    count = lax.axis_size(BOTH[0]) * lax.axis_size(BOTH[1])
    route = [
        (device_of(i), device_of(i + distance)) for i in range(count) if 0 <= i + distance < count
    ]
    return lax.ppermute(x, BOTH, route)


def exchanged(x, distance):
    count = lax.axis_size(BOTH[0]) * lax.axis_size(BOTH[1])
    return lax.ppermute(x, BOTH, [(i, i ^ distance) for i in range(count)])


def sent_from_next_group(x, aside):
    members = lax.axis_size("pair")
    route = []
    for g in range(lax.axis_size("blk") - 1):
        target = device_of(g * members + members - 1)
        route.append(((target + members) ^ aside, target))
    return lax.ppermute(x, BOTH, route)


def own_block_body(features, inv_scale, signal, noise_var, right_side, block_pairs):
    members = lax.axis_size("pair")
    devices = members * lax.axis_size("blk")
    size = features.shape[1] // members
    probes = right_side.shape[0]

    features, begins, scale, noise, listing = (
        pltpu.with_memory_space_constraint(x, pltpu.HBM)
        for x in (features, right_side, inv_scale[None, :], noise_var[None, :], block_pairs.T)
    )
    send, send_rest, raw, direction, raw_next, dir_next, noise, scale, found = loading_call(
        features, begins, noise, scale, listing, size
    )
    spans = [1 << k for k in range(members.bit_length() - 1)]
    sent = sent_from_next_group(send, 0)
    sent_rest = sent_from_next_group(send_rest, members - 1)
    found = found + exchanged(found, spans[-1])
    split = UPPER_STRIPS * CHUNK
    tile, diagonal, left, right, half = diagonal_call(signal, raw, scale, direction, split)
    for span in reversed(spans[:-1]):
        found, left = lax.optimization_barrier((found, left))
        found = found + exchanged(found, span)
    cross_tile, row_sums, crossed, over, next_dir, mark = crossing_call(
        signal, found, raw_next, dir_next, sent, sent_rest, scale, left, half, direction, noise
    )
    got = moved(over, 1)
    lower_tile, own = lower_diagonal_call(signal, left, right, half, diagonal, crossed, size - split)
    part = moved(own, -1)
    image = own + got[:probes]
    images = {0: image}
    for span in spans:
        images[span] = exchanged(image, span)
    over2 = over_call(mark, cross_tile, image)
    partial = second_diagonal_call(tile, lower_tile, row_sums, noise, image, got)
    own2, sums = second_call(
        devices, mark, cross_tile, direction, next_dir, image, part, over, over2, partial
    )
    image2 = own2 + moved(over2, 1)
    images2 = {0: image2}
    for span in spans:
        images2[span] = exchanged(image2, span)
    image2, images, sums = lax.optimization_barrier((image2, images, sums))
    sums = lax.all_to_all(sums, BOTH, 0, 0)
    images, images2, sums = lax.optimization_barrier((images, images2, sums))
    for held in (images, images2):
        for span in spans:
            for at in range(1, span):
                held[at + span] = exchanged(held[span], at)
    return tuple(
        final_call(
            sums,
            right_side,
            [images[k] for k in range(members)],
            [images2[k] for k in range(members)],
        )
    )


def passed_along(block, axis, distance):
    devices = range(lax.axis_size(axis))
    route = [(i - distance, i) for i in devices if i - distance in devices]
    return lax.ppermute(block, axis, route)


def kernel_tile(left_scaled, right_scaled, amplitude):
    cross = lax.dot_general(
        left_scaled,
        right_scaled,
        (((0,), (0,)), ((), ())),
        precision=lax.Precision.HIGHEST,
        preferred_element_type=jnp.float32,
    )
    left_norms = jnp.sum(left_scaled * left_scaled, axis=0)
    right_norms = jnp.sum(right_scaled * right_scaled, axis=0)
    squared = (left_norms[:, None] + right_norms[None, :] - 2.0 * cross) / left_scaled.shape[0]
    distance = jnp.sqrt(jnp.maximum(squared, 0.0))
    stretched = root_three * distance
    ratio = distance / taper_radius
    taper = jnp.maximum(1.0 - ratio, 0.0) ** 4 * (1.0 + 4.0 * ratio)
    return amplitude * (1.0 + stretched) * jnp.exp(-stretched) * taper


def block_terms(left_scaled, right_scaled, left_dir, right_dir, amplitude):
    block_rows = left_scaled.shape[1]
    row_step = min(512, block_rows)
    left_half = left_dir.astype(jnp.bfloat16)
    right_half = right_dir.astype(jnp.bfloat16)

    def rows_visit(position, carried):
        toward_left, toward_right, row_sums, col_sums = carried
        offset = position * row_step
        kernel_rows = kernel_tile(
            lax.dynamic_slice_in_dim(left_scaled, offset, row_step, 1), right_scaled, amplitude
        )
        rows_half = kernel_rows.astype(jnp.bfloat16)
        product = lax.dot_general(
            right_half, rows_half, (((1,), (1,)), ((), ())), preferred_element_type=jnp.float32
        )
        toward_left = lax.dynamic_update_slice_in_dim(toward_left, product, offset, 1)
        toward_right = toward_right + jnp.dot(
            lax.dynamic_slice_in_dim(left_half, offset, row_step, 1),
            rows_half,
            preferred_element_type=jnp.float32,
        )
        row_sums = lax.dynamic_update_slice_in_dim(
            row_sums, jnp.sum(kernel_rows, axis=1), offset, 0
        )
        col_sums = col_sums + jnp.sum(kernel_rows, axis=0)
        return (toward_left, toward_right, row_sums, col_sums)

    zeros_dir = jnp.zeros(left_dir.shape, jnp.float32)
    zeros_row = jnp.zeros((block_rows,), jnp.float32)
    return lax.fori_loop(
        0, block_rows // row_step, rows_visit, (zeros_dir, zeros_dir, zeros_row, zeros_row)
    )


def body(features, inv_scale, signal, noise_var, right_side, block_pairs):
    local_rows = features.shape[1]
    blocks_here = local_rows // BS
    amplitude = signal[0]
    scaled = features * inv_scale[:, None]
    beyond = passed_along(scaled[:, :BS], "blk", -1)
    reach_scaled = jnp.concatenate([scaled, beyond], axis=1)
    base_block = lax.axis_index("blk") * blocks_here
    members = lax.axis_size("pair")
    listing = lax.all_gather(block_pairs, "pair", axis=0, tiled=True)
    living = (listing[:, 0] >= 0).astype(jnp.int32)
    ranked = jnp.cumsum(living) - living
    wanted = lax.axis_index("pair") + members * jnp.arange(block_pairs.shape[0], dtype=jnp.int32)
    matched = (ranked[None, :] == wanted[:, None]) & (living[None, :] > 0)
    chosen = jnp.sum(jnp.where(matched[:, :, None], listing[None, :, :], 0), axis=1)
    my_pairs = jnp.where(jnp.any(matched, axis=1)[:, None], chosen, -1)
    active = jnp.maximum((jnp.sum(living) - lax.axis_index("pair") + members - 1) // members, 0)
    row_local = my_pairs[:, 0] - base_block
    col_local = my_pairs[:, 1] - base_block
    solution = jnp.zeros_like(right_side)
    residual = right_side
    direction = right_side
    norm_now = lax.psum(jnp.sum(residual * residual, axis=1), "blk")
    for iteration in range(ITERS):
        ahead_dir = passed_along(direction[:, :BS], "blk", -1)
        reach_dir = jnp.concatenate([direction, ahead_dir], axis=1)

        def visit(slot_index, summed):
            row_start = row_local[slot_index] * BS
            col_start = col_local[slot_index] * BS
            crossing = (row_local[slot_index] != col_local[slot_index]).astype(jnp.float32)
            left_dir = lax.dynamic_slice_in_dim(reach_dir, row_start, BS, 1)
            right_dir = lax.dynamic_slice_in_dim(reach_dir, col_start, BS, 1)
            toward_left, toward_right, row_sums, col_sums = block_terms(
                lax.dynamic_slice_in_dim(reach_scaled, row_start, BS, 1),
                lax.dynamic_slice_in_dim(reach_scaled, col_start, BS, 1),
                left_dir,
                right_dir,
                amplitude,
            )
            term_left = toward_left + crossing * row_sums[None, :] * left_dir
            term_right = crossing * (toward_right + col_sums[None, :] * right_dir)
            summed = lax.dynamic_update_slice_in_dim(
                summed, lax.dynamic_slice_in_dim(summed, row_start, BS, 1) + term_left, row_start, 1
            )
            summed = lax.dynamic_update_slice_in_dim(
                summed,
                lax.dynamic_slice_in_dim(summed, col_start, BS, 1) + term_right,
                col_start,
                1,
            )
            return summed

        summed = lax.fori_loop(0, active, visit, jnp.zeros(reach_dir.shape, jnp.float32))
        own_part = summed[:, :local_rows]
        next_part = summed[:, local_rows:]
        own_sum, next_sum = lax.psum((own_part, next_part), "pair")
        entering = passed_along(next_sum, "blk", 1)
        coupled = jnp.concatenate([own_sum[:, :BS] + entering, own_sum[:, BS:]], axis=1)
        applied = noise_var[None, :] * direction + coupled
        last_turn = iteration + 1 == ITERS
        curvature = lax.psum(jnp.sum(direction * applied, axis=1), "blk")
        step_size = norm_now / curvature
        solution = solution + step_size[:, None] * direction
        residual = residual - step_size[:, None] * applied
        if not last_turn:
            norm_next = lax.psum(jnp.sum(residual * residual, axis=1), "blk")
            direction = residual + (norm_next / norm_now)[:, None] * direction
            norm_now = norm_next
    return (solution, residual)


def solution(mesh):
    members = mesh.shape["pair"]
    groups = mesh.shape["blk"]

    def chosen(features, *rest):
        one_block_each = features.shape[1] == members * BS and BS % CHUNK == 0 and BS > UPPER_STRIPS * CHUNK
        powers = members > 1 and members & (members - 1) == 0 and groups & (groups - 1) == 0
        fitting = 3 * rest[3].shape[0] <= 128 and rest[3].shape[0] % 8 == 0
        each = own_block_body if one_block_each and powers and fitting else body
        return each(features, *rest)

    placed = (P(None, "blk"), P(), P(), P("blk"), P(None, "blk"), P(("blk", "pair"), None))
    return jax.shard_map(
        chosen,
        mesh=mesh,
        in_specs=placed,
        out_specs=(P(None, "blk"), P(None, "blk")),
        check_vma=False,
    )
```

```python
import functools
import math

import jax
import jax.numpy as jnp
from jax import lax
from jax.experimental import pallas as pl
from jax.experimental.pallas import tpu as pltpu
from jax.sharding import PartitionSpec as P

BS = 2048
ITERS = 2

f32 = jnp.float32
bf16 = jnp.bfloat16
root_three = 1.7320508075688772
taper_radius = 2.0
BOTH = ("blk", "pair")
NT = (((1,), (1,)), ((), ()))
CHUNK = 256
UPPER_STRIPS = 2

RATE = taper_radius * root_three * math.log2(math.e)
NEAR = math.log2(math.e)
FAR = RATE / 4.0
UNIT = NEAR * FAR * RATE**4


def parts_of(x):
    high = x.astype(bf16)
    rest = x - high.astype(f32)
    middle = rest.astype(bf16)
    low = (rest - middle.astype(f32)).astype(bf16)
    return high, middle, low


def norm_parts(points, axis, first):
    norms = jnp.sum(points * points, axis=axis, keepdims=True)
    high, middle, low = (x.astype(f32) for x in parts_of(norms))
    at = lax.broadcasted_iota(jnp.int32, points.shape, axis)
    ones = jnp.where(at < 6, 1.0, 0.0)
    placed = jnp.where(at == first + 2, low, ones)
    placed = jnp.where(at == first + 1, middle, placed)
    return jnp.where(at == first, high, placed).astype(bf16)


def left_parts(points):
    turned = points.T
    high, middle, _ = parts_of(turned)
    return jnp.concatenate([high, high, middle, norm_parts(turned, 1, 0)], axis=1)


def right_parts(points):
    high, middle, _ = parts_of(-2.0 * points)
    return jnp.concatenate([high, middle, high, norm_parts(points, 0, 3)], axis=0)


def points_of(features, inv_scale):
    depth = features.shape[0]
    scale = jnp.broadcast_to(inv_scale, (8, depth)).T[:, 0:1]
    return features * scale * (RATE / (taper_radius * math.sqrt(depth)))


def level_of(signal):
    return jnp.log2(jnp.full((1, CHUNK), signal * (1.0 / UNIT), f32))


def kernel_values(squared, level):
    squared = jnp.maximum(squared, 1e-30)
    s = squared * lax.rsqrt(squared)
    decay = jnp.exp2(level - s)
    u = jnp.maximum(RATE - s, 0.0)
    u2 = u * u
    return ((s + NEAR) * (s + FAR) * decay) * (u2 * u2)


def dot(a, b):
    return jnp.dot(a, b, preferred_element_type=f32)


def dot_nt(a, b):
    return lax.dot_general(a, b, NT, preferred_element_type=f32)


def own_block():
    members = lax.axis_size("pair")
    return lax.axis_index("pair") ^ ((members - 1) * (lax.axis_index("blk") & 1))


def found_in(listing, shape):
    wanted = lax.axis_index("blk") * lax.axis_size("pair") + lax.broadcasted_iota(jnp.int32, shape, 1)
    found = jnp.zeros(shape, f32)
    for slot in range(listing.shape[1]):
        first, second = listing[0:1, slot : slot + 1], listing[1:2, slot : slot + 1]
        found = jnp.where((first == wanted) & (second == wanted + 1), 1.0, found)
    return found


def is_live(found):
    lane = lax.broadcasted_iota(jnp.int32, found.shape, 1)
    return jnp.max(jnp.where(lane == own_block(), found, 0.0)) > 0.0


def cut(at):
    return slice(at * CHUNK, (at + 1) * CHUNK)


def two_sum(a, b):
    total = a + b
    back = total - a
    return total, (a - (total - back)) + (b - back)


def two_product(a, b):
    def halves(x):
        big = x * 4097.0
        high = big - (big - x)
        return high, x - high

    product = a * b
    a_high, a_low = halves(a)
    b_high, b_low = halves(b)
    error = ((a_high * b_high - product) + a_high * b_low + a_low * b_high) + a_low * b_low
    return product, error


def plus(x, y):
    total, error = two_sum(x[0], y[0])
    return two_sum(total, error + (x[1] + y[1]))


def times(x, factor):
    product, error = two_product(x[0], factor)
    return two_sum(product, error + x[1] * factor)


def lane_tiles_sum(x):
    high = x[:, 0:128]
    low = jnp.zeros_like(high)
    for at in range(128, x.shape[1], 128):
        high, error = two_sum(high, x[:, at : at + 128])
        low = low + error
    return high, low


def rows_sum(high, low):
    parts = [(high[at : at + 8], low[at : at + 8]) for at in range(0, 128, 8)]
    while len(parts) > 1:
        parts = [
            (total, error + (x[1] + y[1]))
            for x, y in zip(parts[::2], parts[1::2])
            for total, error in (two_sum(x[0], y[0]),)
        ]
    high, low = parts[0]
    for shift in (4, 2, 1):
        high, error = two_sum(high, pltpu.roll(high, shift, 0))
        low = low + pltpu.roll(low, shift, 0) + error
    return high, low


def lane_tiles_plain(x):
    total = x[:, 0:128]
    for at in range(128, x.shape[1], 128):
        total = total + x[:, at : at + 128]
    return total


def padded(pieces):
    rows = sum(piece.shape[0] for piece in pieces)
    return jnp.concatenate([*pieces, jnp.zeros((128 - rows, 128), f32)], axis=0)


def loading_kernel(
    features,
    right_side,
    noise_var,
    inv_scale,
    block_pairs,
    send,
    send_rest,
    raw,
    direction,
    raw_next,
    next_dir,
    noise,
    scale,
    found,
    listing,
    sems,
):
    size = raw.shape[1]
    depth = raw.shape[0]
    cut_at = send.shape[0]
    mine = own_block()
    after = jnp.minimum(mine + 1, lax.axis_size("pair") - 1)
    here = pl.ds(pl.multiple_of(mine * size, size), size)
    there = pl.ds(pl.multiple_of(after * size, size), size)
    moves = [
        (features.at[:cut_at, :size], send),
        (features.at[cut_at:, :size], send_rest.at[: depth - cut_at]),
        (right_side.at[:, :size], send_rest.at[depth - cut_at :]),
        (features.at[:, here], raw),
        (right_side.at[:, here], direction),
        (features.at[:, there], raw_next),
        (right_side.at[:, there], next_dir),
        (noise_var.at[:, here], noise),
        (inv_scale, scale),
        (block_pairs, listing),
    ]
    copies = [
        pltpu.make_async_copy(source, target, sems.at[k])
        for k, (source, target) in enumerate(moves)
    ]
    for copy in copies:
        copy.start()
    for copy in copies:
        copy.wait()
    found[...] = found_in(listing, found.shape)


def diagonal_products(level, first, tile, own, left, right, half, ahead):
    size = tile.shape[1]
    count = size // CHUNK
    begin = first // CHUNK
    order = [
        (row, col) for row in range(begin, begin + tile.shape[0] // CHUNK) for col in range(row, count)
    ]

    def argument(k):
        row, col = order[k]
        ahead[k % 2] = dot(left[cut(row), :], right[:, cut(col)])

    def product(k):
        row, col = order[k]
        block = tile[cut(row - begin), cut(col)]
        own[:, cut(col)] += dot(half[:, cut(row)], block)
        if col > row:
            own[:, cut(row)] += dot_nt(half[:, cut(col)], block)

    argument(0)
    for k, (row, col) in enumerate(order):
        if k + 1 < len(order):
            argument(k + 1)
        if k:
            product(k - 1)
        tile[cut(row - begin), cut(col)] = kernel_values(ahead[k % 2], level).astype(bf16)
    product(len(order) - 1)


def diagonal_kernel(signal, raw, scale, direction, tile, own, left, right, half, ahead):
    points = points_of(raw[...], scale[...])
    left[...] = left_parts(points)
    right[...] = right_parts(points)
    half[...] = direction[...].astype(bf16)
    own[...] = jnp.zeros_like(own)
    diagonal_products(level_of(signal[0]), 0, tile, own, left, right, half, ahead)


def lower_diagonal_kernel(signal, left, right, half, upper, crossed, tile, own, ahead):
    own[...] = upper[...] + crossed[...]
    first = tile.shape[1] - tile.shape[0]
    diagonal_products(level_of(signal[0]), first, tile, own, left, right, half, ahead)


def crossing_kernel(
    signal,
    found,
    raw_next,
    dir_next,
    sent,
    sent_rest,
    scale,
    left,
    half,
    direction,
    noise,
    tile,
    row_sums,
    own,
    over,
    next_dir,
    mark,
    right,
    half_next,
    ahead,
    col_part,
    row_part,
):
    size = tile.shape[0]
    probes = own.shape[0]
    last = own_block() == lax.axis_size("pair") - 1
    rest = raw_next.shape[0] - sent.shape[0]
    next_dir[...] = jnp.where(last, sent_rest[rest:], dir_next[...])
    live = is_live(found[...])
    mark[...] = jnp.where(live, jnp.ones(mark.shape, f32), jnp.zeros(mark.shape, f32))
    own[...] = jnp.zeros_like(own)
    over[...] = jnp.zeros_like(over)
    row_sums[...] = jnp.zeros_like(row_sums)

    @pl.when(live)
    def _():
        level = level_of(signal[0])
        raw = jnp.concatenate([sent[...], sent_rest[:rest]], axis=0)
        raw = jnp.where(last, raw, raw_next[...])
        right[...] = right_parts(points_of(raw, scale[...]))
        half_next[...] = next_dir[...].astype(bf16)
        col_part[...] = jnp.zeros_like(col_part)
        row_part[...] = jnp.zeros_like(row_part)
        count = size // CHUNK
        order = [(row, col) for row in range(count) for col in range(count)]

        def argument(k):
            row, col = order[k]
            ahead[k % 2] = dot(left[cut(row), :], right[:, cut(col)])

        def product(k):
            row, col = order[k]
            block = tile[cut(row), cut(col)]
            over[:probes, cut(col)] += dot(half[:, cut(row)], block)
            own[:, cut(row)] += dot_nt(half_next[:, cut(col)], block)

        argument(0)
        for k, (row, col) in enumerate(order):
            if k + 1 < len(order):
                argument(k + 1)
            if k:
                product(k - 1)
            values = kernel_values(ahead[k % 2], level)
            tile[cut(row), cut(col)] = values.astype(bf16)
            col_part[:, cut(col)] += jnp.sum(values.reshape(CHUNK // 8, 8, CHUNK), axis=0)
            along = values[:, 0:128]
            for lane in range(128, CHUNK, 128):
                along = along + values[:, lane : lane + 128]
            row_part[cut(row), :] += along
        product(len(order) - 1)
        row_sums[...] = lax.dot_general(
            jnp.ones((8, 128), f32),
            row_part[...],
            NT,
            precision=lax.Precision.HIGHEST,
            preferred_element_type=f32,
        )
        columns = jnp.sum(col_part[...], axis=0, keepdims=True)
        over[:probes] += columns * next_dir[...]
        over[probes : probes + 1] = columns

    own[...] += (noise[...] + row_sums[0:1, :]) * direction[...]


def both_parts(x):
    high = x.astype(bf16)
    return jnp.concatenate([high, (x - high.astype(f32)).astype(bf16)], axis=0)


def folded(x):
    half = x.shape[0] // 2
    return x[:half] + x[half:]


def shift_of(signal):
    return signal + 1.0


def over_kernel(signal, mark, tile, image, direction, over2):
    live = jnp.max(mark[...]) > 0.0

    @pl.when(live)
    def _():
        shifted = image[...] - shift_of(signal[0]) * direction[...]
        over2[...] = folded(dot(both_parts(shifted), tile[...]))

    @pl.when(jnp.logical_not(live))
    def _():
        over2[...] = jnp.zeros_like(over2)


def second_diagonal_kernel(
    signal, upper, lower, row_sums, noise, image, got, direction, own2, both
):
    size = upper.shape[1]
    probes = image.shape[0]
    shift = shift_of(signal[0])
    here = image[...] - shift * direction[...]
    both[...] = both_parts(here)
    own2[...] = (noise[...] + row_sums[0:1, :] + got[probes : probes + 1, :]) * here
    own2[...] += shift * image[...]
    for tile, first in ((upper, 0), (lower, upper.shape[0])):
        for at in range(first, first + tile.shape[0], CHUNK):
            rows = slice(at, at + CHUNK)
            inside = slice(at - first, at - first + CHUNK)
            rest = slice(at + CHUNK, size)
            own2[:, at:] += folded(dot(both[:, rows], tile[inside, at:]))
            if at + CHUNK < size:
                own2[:, rows] += folded(dot_nt(both[:, rest], tile[inside, rest]))


def second_kernel(
    signal, mark, cross_tile, direction, next_dir, image, part, over, over2, partial, own2, sums
):
    probes = image.shape[0]
    here = image[...]
    own2[...] = partial[...]
    there = part[...] + over[:probes]

    @pl.when(jnp.max(mark[...]) > 0.0)
    def _():
        shifted = there - shift_of(signal[0]) * next_dir[...]
        own2[...] += folded(dot_nt(both_parts(shifted), cross_tile[...]))

    begin = direction[...]
    mine = own2[...]
    theirs = over2[...]
    squares = here * here
    exact = [lane_tiles_sum(x) for x in (begin * begin, begin * here, squares)]
    plain = [
        lane_tiles_plain(x)
        for x in (squares + begin * mine + next_dir[...] * theirs, here * mine + there * theirs)
    ]
    high, low = rows_sum(padded([x for x, _ in exact]).T, padded([x for _, x in exact]).T)
    rest = jnp.sum(padded(plain).T, axis=0, keepdims=True)
    row = lax.broadcasted_iota(jnp.int32, high.shape, 0)
    tile = jnp.where(row == 0, high, jnp.where(row == 1, low, jnp.where(row == 2, rest, 0.0)))
    for k in range(sums.shape[0]):
        sums[k] = tile


def final_kernel(sums, right_side, *rest):
    members = lax.axis_size("pair")
    images, images2 = rest[:members], rest[members : 2 * members]
    solution_out, residual_out, solved, left_over, put_sems = rest[2 * members :]
    probes, size = solved.shape[1:]
    mine = own_block()

    def block(k):
        return pl.ds(pl.multiple_of((mine ^ k) * size, size), size)

    runs = [two_sum(sums[k], sums[k + 4]) for k in range(4)]
    for k in range(8, sums.shape[0]):
        total, error = runs[k % 4]
        total, missed = two_sum(total, sums[k])
        runs[k % 4] = (total, error + missed)
    while len(runs) > 1:
        joined = []
        for (a, a_error), (b, b_error) in zip(runs[::2], runs[1::2]):
            total, missed = two_sum(a, b)
            joined.append((total, a_error + b_error + missed))
        runs = joined
    total, error = runs[0]
    total, error = padded([total]).T, padded([error]).T
    square, form, image_square = (
        (total[at : at + probes, 0:1], total[at : at + probes, 1:2] + error[at : at + probes, 0:1])
        for at in (0, probes, 2 * probes)
    )
    mixed, image_form = (total[at : at + probes, 2:3] for at in (0, probes))
    alpha = square[0] / form[0]
    new = plus(plus(square, times(form, -2.0 * alpha)), times(times(image_square, alpha), alpha))[0]
    beta = new / square[0]
    less = form[0] - alpha * mixed
    curvature = (less + alpha * alpha * image_form) + beta * ((form[0] + less) + beta * form[0])
    alpha2 = new / curvature
    puts = []
    for k in range(members):
        begin = right_side[:, block(k)]
        image = images[k][...]
        after = begin - alpha * image
        solved[k] = alpha * begin + alpha2 * (after + beta * begin)
        left_over[k] = after - alpha2 * ((image - alpha * images2[k][...]) + beta * image)
        for at, (source, target) in enumerate(((solved, solution_out), (left_over, residual_out))):
            puts.append(
                pltpu.make_async_copy(source.at[k], target.at[:, block(k)], put_sems.at[at, k])
            )
            puts[-1].start()
    for put in puts:
        put.wait()


def params(mebibytes):
    return pltpu.CompilerParams(vmem_limit_bytes=mebibytes << 20)


def taking(microseconds):
    return pl.CostEstimate(
        flops=int(microseconds * 1.0e9), transcendentals=0, bytes_accessed=int(microseconds * 3.0e6)
    )


def shaped(*shape):
    return jax.ShapeDtypeStruct(shape, f32)


VMEM = pl.BlockSpec(memory_space=pltpu.VMEM)
SMEM = pl.BlockSpec(memory_space=pltpu.SMEM)
HBM = pl.BlockSpec(memory_space=pltpu.HBM)
ANY = pl.BlockSpec(memory_space=pl.ANY)


def loading_call(features, right_side, noise_var, inv_scale, block_pairs, size):
    depth = features.shape[0]
    probes = right_side.shape[0]
    half = min(depth, (depth + probes) // 16 * 8)
    shapes = [
        (half, size),
        (depth + probes - half, size),
        (depth, size),
        (probes, size),
        (depth, size),
        (probes, size),
        (1, size),
        (1, depth),
        (8, 128),
    ]
    return pl.pallas_call(
        loading_kernel,
        in_specs=[HBM] * 5,
        out_specs=[VMEM] * len(shapes),
        out_shape=[pltpu.VMEM(shape, f32) for shape in shapes],
        scratch_shapes=[
            pltpu.VMEM(block_pairs.shape, jnp.int32),
            pltpu.SemaphoreType.DMA((len(shapes) + 1,)),
        ],
        cost_estimate=taking(2),
        compiler_params=params(16),
    )(features, right_side, noise_var, inv_scale, block_pairs)


def diagonal_call(signal, raw, scale, direction, rows):
    depth, size = raw.shape
    probes = direction.shape[0]
    return pl.pallas_call(
        diagonal_kernel,
        in_specs=[SMEM, VMEM, VMEM, VMEM],
        out_specs=[VMEM] * 5,
        out_shape=[
            pltpu.VMEM((rows, size), bf16),
            pltpu.VMEM((probes, size), f32),
            pltpu.VMEM((size, 4 * depth), bf16),
            pltpu.VMEM((4 * depth, size), bf16),
            pltpu.VMEM((probes, size), bf16),
        ],
        scratch_shapes=[pltpu.VMEM((2, CHUNK, CHUNK), f32)],
        cost_estimate=taking(4),
        compiler_params=params(16),
    )(signal, raw, scale, direction)


def lower_diagonal_call(signal, left, right, half, upper, crossed, rows):
    probes, size = upper.shape
    return pl.pallas_call(
        lower_diagonal_kernel,
        in_specs=[SMEM] + [VMEM] * 5,
        out_specs=[VMEM] * 2,
        out_shape=[pltpu.VMEM((rows, size), bf16), pltpu.VMEM((probes, size), f32)],
        scratch_shapes=[pltpu.VMEM((2, CHUNK, CHUNK), f32)],
        cost_estimate=taking(4),
        compiler_params=params(16),
    )(signal, left, right, half, upper, crossed)


def crossing_call(signal, *arrays):
    raw_next, direction = arrays[1], arrays[8]
    depth, size = raw_next.shape
    probes = direction.shape[0]
    return pl.pallas_call(
        crossing_kernel,
        in_specs=[SMEM] + [VMEM] * len(arrays),
        out_specs=[VMEM] * 6,
        out_shape=[
            pltpu.VMEM((size, size), bf16),
            pltpu.VMEM((8, size), f32),
            pltpu.VMEM((probes, size), f32),
            pltpu.VMEM((probes + 8, size), f32),
            pltpu.VMEM((probes, size), f32),
            pltpu.VMEM((8, 128), f32),
        ],
        scratch_shapes=[
            pltpu.VMEM((4 * depth, size), bf16),
            pltpu.VMEM((probes, size), bf16),
            pltpu.VMEM((2, CHUNK, CHUNK), f32),
            pltpu.VMEM((8, size), f32),
            pltpu.VMEM((size, 128), f32),
        ],
        cost_estimate=taking(12),
        compiler_params=params(16),
    )(signal, *arrays)


def over_call(signal, mark, tile, image, direction):
    return pl.pallas_call(
        over_kernel,
        in_specs=[SMEM] + [VMEM] * 4,
        out_specs=VMEM,
        out_shape=pltpu.VMEM(image.shape, f32),
        cost_estimate=taking(2),
        compiler_params=params(16),
    )(signal, mark, tile, image, direction)


def second_diagonal_call(signal, upper, lower, row_sums, noise, image, got, direction):
    probes, size = image.shape
    return pl.pallas_call(
        second_diagonal_kernel,
        in_specs=[SMEM] + [VMEM] * 7,
        out_specs=VMEM,
        out_shape=pltpu.VMEM((probes, size), f32),
        scratch_shapes=[pltpu.VMEM((2 * probes, size), bf16)],
        cost_estimate=taking(2),
        compiler_params=params(16),
    )(signal, upper, lower, row_sums, noise, image, got, direction)


def second_call(devices, signal, *arrays):
    probes, size = arrays[2].shape
    return pl.pallas_call(
        second_kernel,
        in_specs=[SMEM] + [VMEM] * len(arrays),
        out_specs=[VMEM] * 2,
        out_shape=[pltpu.VMEM((probes, size), f32), pltpu.VMEM((devices, 8, 128), f32)],
        cost_estimate=taking(4),
        compiler_params=params(16),
    )(signal, *arrays)


def final_call(sums, right_side, images, images2):
    probes = right_side.shape[0]
    size = images[0].shape[1]
    members = len(images)
    return pl.pallas_call(
        final_kernel,
        in_specs=[VMEM] * (2 + 2 * members),
        out_specs=[HBM, HBM],
        out_shape=[shaped(*right_side.shape)] * 2,
        scratch_shapes=[
            pltpu.VMEM((members, probes, size), f32),
            pltpu.VMEM((members, probes, size), f32),
            pltpu.SemaphoreType.DMA((2, members)),
        ],
        cost_estimate=taking(3),
        compiler_params=params(16),
    )(sums, right_side, *images, *images2)


def device_of(block):
    members = lax.axis_size("pair")
    group, at = divmod(block, members)
    return group * members + (at ^ ((members - 1) * (group & 1)))


def moved(x, distance):
    count = lax.axis_size(BOTH[0]) * lax.axis_size(BOTH[1])
    route = [
        (device_of(i), device_of(i + distance)) for i in range(count) if 0 <= i + distance < count
    ]
    return lax.ppermute(x, BOTH, route)


def exchanged(x, distance):
    count = lax.axis_size(BOTH[0]) * lax.axis_size(BOTH[1])
    return lax.ppermute(x, BOTH, [(i, i ^ distance) for i in range(count)])


def sent_from_next_group(x, aside):
    members = lax.axis_size("pair")
    route = []
    for g in range(lax.axis_size("blk") - 1):
        target = device_of(g * members + members - 1)
        route.append(((target + members) ^ aside, target))
    return lax.ppermute(x, BOTH, route)


def own_block_body(features, inv_scale, signal, noise_var, right_side, block_pairs):
    members = lax.axis_size("pair")
    devices = members * lax.axis_size("blk")
    size = features.shape[1] // members
    probes = right_side.shape[0]

    features, begins, scale, noise, listing = (
        pltpu.with_memory_space_constraint(x, pltpu.HBM)
        for x in (features, right_side, inv_scale[None, :], noise_var[None, :], block_pairs.T)
    )
    send, send_rest, raw, direction, raw_next, dir_next, noise, scale, found = loading_call(
        features, begins, noise, scale, listing, size
    )
    spans = [1 << k for k in range(members.bit_length() - 1)]
    sent = sent_from_next_group(send, 0)
    sent_rest = sent_from_next_group(send_rest, members - 1)
    found = found + exchanged(found, spans[-1])
    split = UPPER_STRIPS * CHUNK
    tile, diagonal, left, right, half = diagonal_call(signal, raw, scale, direction, split)
    for span in reversed(spans[:-1]):
        found, left = lax.optimization_barrier((found, left))
        found = found + exchanged(found, span)
    cross_tile, row_sums, crossed, over, next_dir, mark = crossing_call(
        signal, found, raw_next, dir_next, sent, sent_rest, scale, left, half, direction, noise
    )
    got = moved(over, 1)
    lower_tile, own = lower_diagonal_call(signal, left, right, half, diagonal, crossed, size - split)
    part = moved(own, -1)
    image = own + got[:probes]
    images = {0: image}
    for span in spans:
        images[span] = exchanged(image, span)
    over2 = over_call(signal, mark, cross_tile, image, direction)
    partial = second_diagonal_call(
        signal, tile, lower_tile, row_sums, noise, image, got, direction
    )
    own2, sums = second_call(
        devices, signal, mark, cross_tile, direction, next_dir, image, part, over, over2, partial
    )
    image2 = own2 + moved(over2, 1)
    images2 = {0: image2}
    for span in spans:
        images2[span] = exchanged(image2, span)
    image2, images, sums = lax.optimization_barrier((image2, images, sums))
    sums = lax.all_to_all(sums, BOTH, 0, 0)
    images, images2, sums = lax.optimization_barrier((images, images2, sums))
    for held in (images, images2):
        for span in spans:
            for at in range(1, span):
                held[at + span] = exchanged(held[span], at)
    return tuple(
        final_call(
            sums,
            right_side,
            [images[k] for k in range(members)],
            [images2[k] for k in range(members)],
        )
    )


def passed_along(block, axis, distance):
    devices = range(lax.axis_size(axis))
    route = [(i - distance, i) for i in devices if i - distance in devices]
    return lax.ppermute(block, axis, route)


def kernel_tile(left_scaled, right_scaled, amplitude):
    cross = lax.dot_general(
        left_scaled,
        right_scaled,
        (((0,), (0,)), ((), ())),
        precision=lax.Precision.HIGHEST,
        preferred_element_type=jnp.float32,
    )
    left_norms = jnp.sum(left_scaled * left_scaled, axis=0)
    right_norms = jnp.sum(right_scaled * right_scaled, axis=0)
    squared = (left_norms[:, None] + right_norms[None, :] - 2.0 * cross) / left_scaled.shape[0]
    distance = jnp.sqrt(jnp.maximum(squared, 0.0))
    stretched = root_three * distance
    ratio = distance / taper_radius
    taper = jnp.maximum(1.0 - ratio, 0.0) ** 4 * (1.0 + 4.0 * ratio)
    return amplitude * (1.0 + stretched) * jnp.exp(-stretched) * taper


def block_terms(left_scaled, right_scaled, left_dir, right_dir, amplitude):
    block_rows = left_scaled.shape[1]
    row_step = min(512, block_rows)
    left_half = left_dir.astype(jnp.bfloat16)
    right_half = right_dir.astype(jnp.bfloat16)

    def rows_visit(position, carried):
        toward_left, toward_right, row_sums, col_sums = carried
        offset = position * row_step
        kernel_rows = kernel_tile(
            lax.dynamic_slice_in_dim(left_scaled, offset, row_step, 1), right_scaled, amplitude
        )
        rows_half = kernel_rows.astype(jnp.bfloat16)
        product = lax.dot_general(
            right_half, rows_half, (((1,), (1,)), ((), ())), preferred_element_type=jnp.float32
        )
        toward_left = lax.dynamic_update_slice_in_dim(toward_left, product, offset, 1)
        toward_right = toward_right + jnp.dot(
            lax.dynamic_slice_in_dim(left_half, offset, row_step, 1),
            rows_half,
            preferred_element_type=jnp.float32,
        )
        row_sums = lax.dynamic_update_slice_in_dim(
            row_sums, jnp.sum(kernel_rows, axis=1), offset, 0
        )
        col_sums = col_sums + jnp.sum(kernel_rows, axis=0)
        return (toward_left, toward_right, row_sums, col_sums)

    zeros_dir = jnp.zeros(left_dir.shape, jnp.float32)
    zeros_row = jnp.zeros((block_rows,), jnp.float32)
    return lax.fori_loop(
        0, block_rows // row_step, rows_visit, (zeros_dir, zeros_dir, zeros_row, zeros_row)
    )


def body(features, inv_scale, signal, noise_var, right_side, block_pairs):
    local_rows = features.shape[1]
    blocks_here = local_rows // BS
    amplitude = signal[0]
    scaled = features * inv_scale[:, None]
    beyond = passed_along(scaled[:, :BS], "blk", -1)
    reach_scaled = jnp.concatenate([scaled, beyond], axis=1)
    base_block = lax.axis_index("blk") * blocks_here
    members = lax.axis_size("pair")
    listing = lax.all_gather(block_pairs, "pair", axis=0, tiled=True)
    living = (listing[:, 0] >= 0).astype(jnp.int32)
    ranked = jnp.cumsum(living) - living
    wanted = lax.axis_index("pair") + members * jnp.arange(block_pairs.shape[0], dtype=jnp.int32)
    matched = (ranked[None, :] == wanted[:, None]) & (living[None, :] > 0)
    chosen = jnp.sum(jnp.where(matched[:, :, None], listing[None, :, :], 0), axis=1)
    my_pairs = jnp.where(jnp.any(matched, axis=1)[:, None], chosen, -1)
    active = jnp.maximum((jnp.sum(living) - lax.axis_index("pair") + members - 1) // members, 0)
    row_local = my_pairs[:, 0] - base_block
    col_local = my_pairs[:, 1] - base_block
    solution = jnp.zeros_like(right_side)
    residual = right_side
    direction = right_side
    norm_now = lax.psum(jnp.sum(residual * residual, axis=1), "blk")
    for iteration in range(ITERS):
        ahead_dir = passed_along(direction[:, :BS], "blk", -1)
        reach_dir = jnp.concatenate([direction, ahead_dir], axis=1)

        def visit(slot_index, summed):
            row_start = row_local[slot_index] * BS
            col_start = col_local[slot_index] * BS
            crossing = (row_local[slot_index] != col_local[slot_index]).astype(jnp.float32)
            left_dir = lax.dynamic_slice_in_dim(reach_dir, row_start, BS, 1)
            right_dir = lax.dynamic_slice_in_dim(reach_dir, col_start, BS, 1)
            toward_left, toward_right, row_sums, col_sums = block_terms(
                lax.dynamic_slice_in_dim(reach_scaled, row_start, BS, 1),
                lax.dynamic_slice_in_dim(reach_scaled, col_start, BS, 1),
                left_dir,
                right_dir,
                amplitude,
            )
            term_left = toward_left + crossing * row_sums[None, :] * left_dir
            term_right = crossing * (toward_right + col_sums[None, :] * right_dir)
            summed = lax.dynamic_update_slice_in_dim(
                summed, lax.dynamic_slice_in_dim(summed, row_start, BS, 1) + term_left, row_start, 1
            )
            summed = lax.dynamic_update_slice_in_dim(
                summed,
                lax.dynamic_slice_in_dim(summed, col_start, BS, 1) + term_right,
                col_start,
                1,
            )
            return summed

        summed = lax.fori_loop(0, active, visit, jnp.zeros(reach_dir.shape, jnp.float32))
        own_part = summed[:, :local_rows]
        next_part = summed[:, local_rows:]
        own_sum, next_sum = lax.psum((own_part, next_part), "pair")
        entering = passed_along(next_sum, "blk", 1)
        coupled = jnp.concatenate([own_sum[:, :BS] + entering, own_sum[:, BS:]], axis=1)
        applied = noise_var[None, :] * direction + coupled
        last_turn = iteration + 1 == ITERS
        curvature = lax.psum(jnp.sum(direction * applied, axis=1), "blk")
        step_size = norm_now / curvature
        solution = solution + step_size[:, None] * direction
        residual = residual - step_size[:, None] * applied
        if not last_turn:
            norm_next = lax.psum(jnp.sum(residual * residual, axis=1), "blk")
            direction = residual + (norm_next / norm_now)[:, None] * direction
            norm_now = norm_next
    return (solution, residual)


def solution(mesh):
    members = mesh.shape["pair"]
    groups = mesh.shape["blk"]

    def chosen(features, *rest):
        one_block_each = features.shape[1] == members * BS and BS % CHUNK == 0 and BS > UPPER_STRIPS * CHUNK
        powers = members > 1 and members & (members - 1) == 0 and groups & (groups - 1) == 0
        fitting = 3 * rest[3].shape[0] <= 128 and rest[3].shape[0] % 8 == 0
        each = own_block_body if one_block_each and powers and fitting else body
        return each(features, *rest)

    placed = (P(None, "blk"), P(), P(), P("blk"), P(None, "blk"), P(("blk", "pair"), None))
    return jax.shard_map(
        chosen,
        mesh=mesh,
        in_specs=placed,
        out_specs=(P(None, "blk"), P(None, "blk")),
        check_vma=False,
    )
```

```python
import functools
import math

import jax
import jax.numpy as jnp
from jax import lax
from jax.experimental import pallas as pl
from jax.experimental.pallas import tpu as pltpu
from jax.sharding import PartitionSpec as P

BS = 2048
ITERS = 2

f32 = jnp.float32
bf16 = jnp.bfloat16
root_three = 1.7320508075688772
taper_radius = 2.0
BOTH = ("blk", "pair")
NT = (((1,), (1,)), ((), ()))
CHUNK = 256
UPPER_STRIPS = 2

RATE = taper_radius * root_three * math.log2(math.e)
NEAR = math.log2(math.e)
FAR = RATE / 4.0
UNIT = NEAR * FAR * RATE**4


def parts_of(x):
    high = x.astype(bf16)
    rest = x - high.astype(f32)
    middle = rest.astype(bf16)
    low = (rest - middle.astype(f32)).astype(bf16)
    return high, middle, low


def norm_parts(points, axis, first):
    norms = jnp.sum(points * points, axis=axis, keepdims=True)
    high, middle, low = (x.astype(f32) for x in parts_of(norms))
    at = lax.broadcasted_iota(jnp.int32, points.shape, axis)
    ones = jnp.where(at < 6, 1.0, 0.0)
    placed = jnp.where(at == first + 2, low, ones)
    placed = jnp.where(at == first + 1, middle, placed)
    return jnp.where(at == first, high, placed).astype(bf16)


def left_parts(points):
    turned = points.T
    high, middle, _ = parts_of(turned)
    return jnp.concatenate([high, high, middle, norm_parts(turned, 1, 0)], axis=1)


def right_parts(points):
    high, middle, _ = parts_of(-2.0 * points)
    return jnp.concatenate([high, middle, high, norm_parts(points, 0, 3)], axis=0)


def points_of(features, inv_scale):
    depth = features.shape[0]
    scale = jnp.broadcast_to(inv_scale, (8, depth)).T[:, 0:1]
    return features * scale * (RATE / (taper_radius * math.sqrt(depth)))


def level_of(signal):
    return jnp.log2(jnp.full((1, CHUNK), signal * (1.0 / UNIT), f32))


def kernel_values(squared, level):
    squared = jnp.maximum(squared, 1e-30)
    s = squared * lax.rsqrt(squared)
    decay = jnp.exp2(level - s)
    u = jnp.maximum(RATE - s, 0.0)
    u2 = u * u
    return ((s + NEAR) * (s + FAR) * decay) * (u2 * u2)


def dot(a, b):
    return jnp.dot(a, b, preferred_element_type=f32)


def dot_nt(a, b):
    return lax.dot_general(a, b, NT, preferred_element_type=f32)


def own_block():
    members = lax.axis_size("pair")
    return lax.axis_index("pair") ^ ((members - 1) * (lax.axis_index("blk") & 1))


def found_in(listing, shape):
    wanted = lax.axis_index("blk") * lax.axis_size("pair") + lax.broadcasted_iota(jnp.int32, shape, 1)
    found = jnp.zeros(shape, f32)
    for slot in range(listing.shape[1]):
        first, second = listing[0:1, slot : slot + 1], listing[1:2, slot : slot + 1]
        found = jnp.where((first == wanted) & (second == wanted + 1), 1.0, found)
    return found


def is_live(found):
    lane = lax.broadcasted_iota(jnp.int32, found.shape, 1)
    return jnp.max(jnp.where(lane == own_block(), found, 0.0)) > 0.0


def cut(at):
    return slice(at * CHUNK, (at + 1) * CHUNK)


def two_sum(a, b):
    total = a + b
    back = total - a
    return total, (a - (total - back)) + (b - back)


def two_product(a, b):
    def halves(x):
        big = x * 4097.0
        high = big - (big - x)
        return high, x - high

    product = a * b
    a_high, a_low = halves(a)
    b_high, b_low = halves(b)
    error = ((a_high * b_high - product) + a_high * b_low + a_low * b_high) + a_low * b_low
    return product, error


def plus(x, y):
    total, error = two_sum(x[0], y[0])
    return two_sum(total, error + (x[1] + y[1]))


def times(x, factor):
    product, error = two_product(x[0], factor)
    return two_sum(product, error + x[1] * factor)


def lane_tiles_sum(x):
    high = x[:, 0:128]
    low = jnp.zeros_like(high)
    for at in range(128, x.shape[1], 128):
        high, error = two_sum(high, x[:, at : at + 128])
        low = low + error
    return high, low


def rows_sum(high, low):
    parts = [(high[at : at + 8], low[at : at + 8]) for at in range(0, 128, 8)]
    while len(parts) > 1:
        parts = [
            (total, error + (x[1] + y[1]))
            for x, y in zip(parts[::2], parts[1::2])
            for total, error in (two_sum(x[0], y[0]),)
        ]
    high, low = parts[0]
    for shift in (4, 2, 1):
        high, error = two_sum(high, pltpu.roll(high, shift, 0))
        low = low + pltpu.roll(low, shift, 0) + error
    return high, low


def lane_tiles_plain(x):
    total = x[:, 0:128]
    for at in range(128, x.shape[1], 128):
        total = total + x[:, at : at + 128]
    return total


def padded(pieces):
    rows = sum(piece.shape[0] for piece in pieces)
    return jnp.concatenate([*pieces, jnp.zeros((128 - rows, 128), f32)], axis=0)


def loading_kernel(
    features,
    right_side,
    noise_var,
    inv_scale,
    block_pairs,
    send,
    send_rest,
    raw,
    direction,
    raw_next,
    next_dir,
    noise,
    scale,
    found,
    listing,
    sems,
):
    size = raw.shape[1]
    depth = raw.shape[0]
    cut_at = send.shape[0]
    mine = own_block()
    after = jnp.minimum(mine + 1, lax.axis_size("pair") - 1)
    here = pl.ds(pl.multiple_of(mine * size, size), size)
    there = pl.ds(pl.multiple_of(after * size, size), size)
    moves = [
        (features.at[:cut_at, :size], send),
        (features.at[cut_at:, :size], send_rest.at[: depth - cut_at]),
        (right_side.at[:, :size], send_rest.at[depth - cut_at :]),
        (features.at[:, here], raw),
        (right_side.at[:, here], direction),
        (features.at[:, there], raw_next),
        (right_side.at[:, there], next_dir),
        (noise_var.at[:, here], noise),
        (inv_scale, scale),
        (block_pairs, listing),
    ]
    copies = [
        pltpu.make_async_copy(source, target, sems.at[k])
        for k, (source, target) in enumerate(moves)
    ]
    for copy in copies:
        copy.start()
    for copy in copies:
        copy.wait()
    found[...] = found_in(listing, found.shape)


def diagonal_products(level, first, tile, own, left, right, half, ahead):
    size = tile.shape[1]
    count = size // CHUNK
    begin = first // CHUNK
    order = [
        (row, col) for row in range(begin, begin + tile.shape[0] // CHUNK) for col in range(row, count)
    ]

    def argument(k):
        row, col = order[k]
        ahead[k % 2] = dot(left[cut(row), :], right[:, cut(col)])

    def product(k):
        row, col = order[k]
        block = tile[cut(row - begin), cut(col)]
        own[:, cut(col)] += dot(half[:, cut(row)], block)
        if col > row:
            own[:, cut(row)] += dot_nt(half[:, cut(col)], block)

    argument(0)
    for k, (row, col) in enumerate(order):
        if k + 1 < len(order):
            argument(k + 1)
        if k:
            product(k - 1)
        tile[cut(row - begin), cut(col)] = kernel_values(ahead[k % 2], level).astype(bf16)
    product(len(order) - 1)


def diagonal_kernel(signal, raw, scale, direction, tile, own, left, right, half, ahead):
    points = points_of(raw[...], scale[...])
    left[...] = left_parts(points)
    right[...] = right_parts(points)
    half[...] = direction[...].astype(bf16)
    own[...] = jnp.zeros_like(own)
    diagonal_products(level_of(signal[0]), 0, tile, own, left, right, half, ahead)


def lower_diagonal_kernel(signal, left, right, half, upper, crossed, tile, own, ahead):
    own[...] = upper[...] + crossed[...]
    first = tile.shape[1] - tile.shape[0]
    diagonal_products(level_of(signal[0]), first, tile, own, left, right, half, ahead)


def crossing_kernel(
    signal,
    found,
    raw_next,
    dir_next,
    sent,
    sent_rest,
    scale,
    left,
    half,
    direction,
    noise,
    tile,
    row_sums,
    own,
    over,
    next_dir,
    mark,
    right,
    half_next,
    ahead,
    col_part,
    row_part,
):
    size = tile.shape[0]
    probes = own.shape[0]
    last = own_block() == lax.axis_size("pair") - 1
    rest = raw_next.shape[0] - sent.shape[0]
    next_dir[...] = jnp.where(last, sent_rest[rest:], dir_next[...])
    live = is_live(found[...])
    mark[...] = jnp.where(live, jnp.ones(mark.shape, f32), jnp.zeros(mark.shape, f32))
    own[...] = jnp.zeros_like(own)
    over[...] = jnp.zeros_like(over)
    row_sums[...] = jnp.zeros_like(row_sums)

    @pl.when(live)
    def _():
        level = level_of(signal[0])
        raw = jnp.concatenate([sent[...], sent_rest[:rest]], axis=0)
        raw = jnp.where(last, raw, raw_next[...])
        right[...] = right_parts(points_of(raw, scale[...]))
        half_next[...] = next_dir[...].astype(bf16)
        col_part[...] = jnp.zeros_like(col_part)
        row_part[...] = jnp.zeros_like(row_part)
        count = size // CHUNK
        order = [(row, col) for row in range(count) for col in range(count)]

        def argument(k):
            row, col = order[k]
            ahead[k % 2] = dot(left[cut(row), :], right[:, cut(col)])

        def product(k):
            row, col = order[k]
            block = tile[cut(row), cut(col)]
            over[:probes, cut(col)] += dot(half[:, cut(row)], block)
            own[:, cut(row)] += dot_nt(half_next[:, cut(col)], block)

        argument(0)
        for k, (row, col) in enumerate(order):
            if k + 1 < len(order):
                argument(k + 1)
            if k:
                product(k - 1)
            values = kernel_values(ahead[k % 2], level)
            tile[cut(row), cut(col)] = values.astype(bf16)
            col_part[:, cut(col)] += jnp.sum(values.reshape(CHUNK // 8, 8, CHUNK), axis=0)
            along = values[:, 0:128]
            for lane in range(128, CHUNK, 128):
                along = along + values[:, lane : lane + 128]
            row_part[cut(row), :] += along
        product(len(order) - 1)
        row_sums[...] = lax.dot_general(
            jnp.ones((8, 128), f32),
            row_part[...],
            NT,
            precision=lax.Precision.HIGHEST,
            preferred_element_type=f32,
        )
        columns = jnp.sum(col_part[...], axis=0, keepdims=True)
        over[:probes] += columns * next_dir[...]
        over[probes : probes + 1] = columns

    own[...] += (noise[...] + row_sums[0:1, :]) * direction[...]


def both_parts(x):
    high = x.astype(bf16)
    return jnp.concatenate([high, (x - high.astype(f32)).astype(bf16)], axis=0)


def folded(x):
    half = x.shape[0] // 2
    return x[:half] + x[half:]


def shift_of(signal):
    return signal + 1.0


def over_kernel(signal, mark, tile, image, direction, over2):
    live = jnp.max(mark[...]) > 0.0

    @pl.when(live)
    def _():
        shifted = image[...] - shift_of(signal[0]) * direction[...]
        over2[...] = folded(dot(both_parts(shifted), tile[...]))

    @pl.when(jnp.logical_not(live))
    def _():
        over2[...] = jnp.zeros_like(over2)


def second_diagonal_kernel(
    signal, upper, lower, row_sums, noise, image, got, direction, own2, both
):
    size = upper.shape[1]
    probes = image.shape[0]
    shift = shift_of(signal[0])
    here = image[...] - shift * direction[...]
    both[...] = both_parts(here)
    own2[...] = (noise[...] + row_sums[0:1, :] + got[probes : probes + 1, :]) * here
    own2[...] += shift * image[...]
    for tile, first in ((upper, 0), (lower, upper.shape[0])):
        for at in range(first, first + tile.shape[0], CHUNK):
            rows = slice(at, at + CHUNK)
            inside = slice(at - first, at - first + CHUNK)
            rest = slice(at + CHUNK, size)
            own2[:, at:] += folded(dot(both[:, rows], tile[inside, at:]))
            if at + CHUNK < size:
                own2[:, rows] += folded(dot_nt(both[:, rest], tile[inside, rest]))


def second_kernel(
    signal, mark, cross_tile, direction, next_dir, image, part, over, over2, partial, own2, sums
):
    probes = image.shape[0]
    here = image[...]
    own2[...] = partial[...]
    there = part[...] + over[:probes]

    @pl.when(jnp.max(mark[...]) > 0.0)
    def _():
        shifted = there - shift_of(signal[0]) * next_dir[...]
        own2[...] += folded(dot_nt(both_parts(shifted), cross_tile[...]))

    begin = direction[...]
    mine = own2[...]
    theirs = over2[...]
    squares = here * here
    exact = [lane_tiles_sum(x) for x in (begin * begin, begin * here, squares)]
    plain = [
        lane_tiles_plain(x)
        for x in (squares + begin * mine + next_dir[...] * theirs, here * mine + there * theirs)
    ]
    high, low = rows_sum(padded([x for x, _ in exact]).T, padded([x for _, x in exact]).T)
    rest = jnp.sum(padded(plain).T, axis=0, keepdims=True)
    row = lax.broadcasted_iota(jnp.int32, high.shape, 0)
    tile = jnp.where(row == 0, high, jnp.where(row == 1, low, jnp.where(row == 2, rest, 0.0)))
    for k in range(sums.shape[0]):
        sums[k] = tile


def final_kernel(sums, right_side, *rest):
    members = lax.axis_size("pair")
    images, images2 = rest[:members], rest[members : 2 * members]
    solution_out, residual_out, solved, left_over, put_sems = rest[2 * members :]
    probes, size = solved.shape[1:]
    mine = own_block()

    def block(k):
        return pl.ds(pl.multiple_of((mine ^ k) * size, size), size)

    runs = [two_sum(sums[k], sums[k + 4]) for k in range(4)]
    for k in range(8, sums.shape[0]):
        total, error = runs[k % 4]
        total, missed = two_sum(total, sums[k])
        runs[k % 4] = (total, error + missed)
    while len(runs) > 1:
        joined = []
        for (a, a_error), (b, b_error) in zip(runs[::2], runs[1::2]):
            total, missed = two_sum(a, b)
            joined.append((total, a_error + b_error + missed))
        runs = joined
    total, error = runs[0]
    total, error = padded([total]).T, padded([error]).T
    square, form, image_square = (
        (total[at : at + probes, 0:1], total[at : at + probes, 1:2] + error[at : at + probes, 0:1])
        for at in (0, probes, 2 * probes)
    )
    mixed, image_form = (total[at : at + probes, 2:3] for at in (0, probes))
    alpha = square[0] / form[0]
    new = plus(plus(square, times(form, -2.0 * alpha)), times(times(image_square, alpha), alpha))[0]
    beta = new / square[0]
    less = form[0] - alpha * mixed
    curvature = (less + alpha * alpha * image_form) + beta * ((form[0] + less) + beta * form[0])
    alpha2 = new / curvature
    puts = []
    for k in range(members):
        begin = right_side[:, block(k)]
        image = images[k][...]
        after = begin - alpha * image
        solved[k] = alpha * begin + alpha2 * (after + beta * begin)
        left_over[k] = after - alpha2 * ((image - alpha * images2[k][...]) + beta * image)
        for at, (source, target) in enumerate(((solved, solution_out), (left_over, residual_out))):
            puts.append(
                pltpu.make_async_copy(source.at[k], target.at[:, block(k)], put_sems.at[at, k])
            )
            puts[-1].start()
    for put in puts:
        put.wait()


def params(mebibytes):
    return pltpu.CompilerParams(vmem_limit_bytes=mebibytes << 20)


def taking(microseconds):
    return pl.CostEstimate(
        flops=int(microseconds * 1.0e9), transcendentals=0, bytes_accessed=int(microseconds * 3.0e6)
    )


def shaped(*shape):
    return jax.ShapeDtypeStruct(shape, f32)


VMEM = pl.BlockSpec(memory_space=pltpu.VMEM)
SMEM = pl.BlockSpec(memory_space=pltpu.SMEM)
HBM = pl.BlockSpec(memory_space=pltpu.HBM)
ANY = pl.BlockSpec(memory_space=pl.ANY)


def loading_call(features, right_side, noise_var, inv_scale, block_pairs, size):
    depth = features.shape[0]
    probes = right_side.shape[0]
    half = min(depth, (depth + probes) * 5 // 64 * 8)
    shapes = [
        (half, size),
        (depth + probes - half, size),
        (depth, size),
        (probes, size),
        (depth, size),
        (probes, size),
        (1, size),
        (1, depth),
        (8, 128),
    ]
    return pl.pallas_call(
        loading_kernel,
        in_specs=[HBM] * 5,
        out_specs=[VMEM] * len(shapes),
        out_shape=[pltpu.VMEM(shape, f32) for shape in shapes],
        scratch_shapes=[
            pltpu.VMEM(block_pairs.shape, jnp.int32),
            pltpu.SemaphoreType.DMA((len(shapes) + 1,)),
        ],
        cost_estimate=taking(2),
        compiler_params=params(16),
    )(features, right_side, noise_var, inv_scale, block_pairs)


def diagonal_call(signal, raw, scale, direction, rows):
    depth, size = raw.shape
    probes = direction.shape[0]
    return pl.pallas_call(
        diagonal_kernel,
        in_specs=[SMEM, VMEM, VMEM, VMEM],
        out_specs=[VMEM] * 5,
        out_shape=[
            pltpu.VMEM((rows, size), bf16),
            pltpu.VMEM((probes, size), f32),
            pltpu.VMEM((size, 4 * depth), bf16),
            pltpu.VMEM((4 * depth, size), bf16),
            pltpu.VMEM((probes, size), bf16),
        ],
        scratch_shapes=[pltpu.VMEM((2, CHUNK, CHUNK), f32)],
        cost_estimate=taking(4),
        compiler_params=params(16),
    )(signal, raw, scale, direction)


def lower_diagonal_call(signal, left, right, half, upper, crossed, rows):
    probes, size = upper.shape
    return pl.pallas_call(
        lower_diagonal_kernel,
        in_specs=[SMEM] + [VMEM] * 5,
        out_specs=[VMEM] * 2,
        out_shape=[pltpu.VMEM((rows, size), bf16), pltpu.VMEM((probes, size), f32)],
        scratch_shapes=[pltpu.VMEM((2, CHUNK, CHUNK), f32)],
        cost_estimate=taking(4),
        compiler_params=params(16),
    )(signal, left, right, half, upper, crossed)


def crossing_call(signal, *arrays):
    raw_next, direction = arrays[1], arrays[8]
    depth, size = raw_next.shape
    probes = direction.shape[0]
    return pl.pallas_call(
        crossing_kernel,
        in_specs=[SMEM] + [VMEM] * len(arrays),
        out_specs=[VMEM] * 6,
        out_shape=[
            pltpu.VMEM((size, size), bf16),
            pltpu.VMEM((8, size), f32),
            pltpu.VMEM((probes, size), f32),
            pltpu.VMEM((probes + 8, size), f32),
            pltpu.VMEM((probes, size), f32),
            pltpu.VMEM((8, 128), f32),
        ],
        scratch_shapes=[
            pltpu.VMEM((4 * depth, size), bf16),
            pltpu.VMEM((probes, size), bf16),
            pltpu.VMEM((2, CHUNK, CHUNK), f32),
            pltpu.VMEM((8, size), f32),
            pltpu.VMEM((size, 128), f32),
        ],
        cost_estimate=taking(12),
        compiler_params=params(16),
    )(signal, *arrays)


def over_call(signal, mark, tile, image, direction):
    return pl.pallas_call(
        over_kernel,
        in_specs=[SMEM] + [VMEM] * 4,
        out_specs=VMEM,
        out_shape=pltpu.VMEM(image.shape, f32),
        cost_estimate=taking(2),
        compiler_params=params(16),
    )(signal, mark, tile, image, direction)


def second_diagonal_call(signal, upper, lower, row_sums, noise, image, got, direction):
    probes, size = image.shape
    return pl.pallas_call(
        second_diagonal_kernel,
        in_specs=[SMEM] + [VMEM] * 7,
        out_specs=VMEM,
        out_shape=pltpu.VMEM((probes, size), f32),
        scratch_shapes=[pltpu.VMEM((2 * probes, size), bf16)],
        cost_estimate=taking(2),
        compiler_params=params(16),
    )(signal, upper, lower, row_sums, noise, image, got, direction)


def second_call(devices, signal, *arrays):
    probes, size = arrays[2].shape
    return pl.pallas_call(
        second_kernel,
        in_specs=[SMEM] + [VMEM] * len(arrays),
        out_specs=[VMEM] * 2,
        out_shape=[pltpu.VMEM((probes, size), f32), pltpu.VMEM((devices, 8, 128), f32)],
        cost_estimate=taking(4),
        compiler_params=params(16),
    )(signal, *arrays)


def final_call(sums, right_side, images, images2):
    probes = right_side.shape[0]
    size = images[0].shape[1]
    members = len(images)
    return pl.pallas_call(
        final_kernel,
        in_specs=[VMEM] * (2 + 2 * members),
        out_specs=[HBM, HBM],
        out_shape=[shaped(*right_side.shape)] * 2,
        scratch_shapes=[
            pltpu.VMEM((members, probes, size), f32),
            pltpu.VMEM((members, probes, size), f32),
            pltpu.SemaphoreType.DMA((2, members)),
        ],
        cost_estimate=taking(3),
        compiler_params=params(16),
    )(sums, right_side, *images, *images2)


def device_of(block):
    members = lax.axis_size("pair")
    group, at = divmod(block, members)
    return group * members + (at ^ ((members - 1) * (group & 1)))


def moved(x, distance):
    count = lax.axis_size(BOTH[0]) * lax.axis_size(BOTH[1])
    route = [
        (device_of(i), device_of(i + distance)) for i in range(count) if 0 <= i + distance < count
    ]
    return lax.ppermute(x, BOTH, route)


def exchanged(x, distance):
    count = lax.axis_size(BOTH[0]) * lax.axis_size(BOTH[1])
    return lax.ppermute(x, BOTH, [(i, i ^ distance) for i in range(count)])


def sent_from_next_group(x, aside):
    members = lax.axis_size("pair")
    route = []
    for g in range(lax.axis_size("blk") - 1):
        target = device_of(g * members + members - 1)
        route.append(((target + members) ^ aside, target))
    return lax.ppermute(x, BOTH, route)


def own_block_body(features, inv_scale, signal, noise_var, right_side, block_pairs):
    members = lax.axis_size("pair")
    devices = members * lax.axis_size("blk")
    size = features.shape[1] // members
    probes = right_side.shape[0]

    features, begins, scale, noise, listing = (
        pltpu.with_memory_space_constraint(x, pltpu.HBM)
        for x in (features, right_side, inv_scale[None, :], noise_var[None, :], block_pairs.T)
    )
    send, send_rest, raw, direction, raw_next, dir_next, noise, scale, found = loading_call(
        features, begins, noise, scale, listing, size
    )
    spans = [1 << k for k in range(members.bit_length() - 1)]
    sent = sent_from_next_group(send, 0)
    sent_rest = sent_from_next_group(send_rest, members - 1)
    found = found + exchanged(found, spans[-1])
    split = UPPER_STRIPS * CHUNK
    tile, diagonal, left, right, half = diagonal_call(signal, raw, scale, direction, split)
    for span in reversed(spans[:-1]):
        found, left = lax.optimization_barrier((found, left))
        found = found + exchanged(found, span)
    cross_tile, row_sums, crossed, over, next_dir, mark = crossing_call(
        signal, found, raw_next, dir_next, sent, sent_rest, scale, left, half, direction, noise
    )
    got = moved(over, 1)
    lower_tile, own = lower_diagonal_call(signal, left, right, half, diagonal, crossed, size - split)
    part = moved(own, -1)
    image = own + got[:probes]
    images = {0: image}
    for span in spans:
        images[span] = exchanged(image, span)
    over2 = over_call(signal, mark, cross_tile, image, direction)
    partial = second_diagonal_call(
        signal, tile, lower_tile, row_sums, noise, image, got, direction
    )
    own2, sums = second_call(
        devices, signal, mark, cross_tile, direction, next_dir, image, part, over, over2, partial
    )
    image2 = own2 + moved(over2, 1)
    images2 = {0: image2}
    for span in spans:
        images2[span] = exchanged(image2, span)
    image2, images, sums = lax.optimization_barrier((image2, images, sums))
    sums = lax.all_to_all(sums, BOTH, 0, 0)
    images, images2, sums = lax.optimization_barrier((images, images2, sums))
    for held in (images, images2):
        for span in spans:
            for at in range(1, span):
                held[at + span] = exchanged(held[span], at)
    return tuple(
        final_call(
            sums,
            right_side,
            [images[k] for k in range(members)],
            [images2[k] for k in range(members)],
        )
    )


def passed_along(block, axis, distance):
    devices = range(lax.axis_size(axis))
    route = [(i - distance, i) for i in devices if i - distance in devices]
    return lax.ppermute(block, axis, route)


def kernel_tile(left_scaled, right_scaled, amplitude):
    cross = lax.dot_general(
        left_scaled,
        right_scaled,
        (((0,), (0,)), ((), ())),
        precision=lax.Precision.HIGHEST,
        preferred_element_type=jnp.float32,
    )
    left_norms = jnp.sum(left_scaled * left_scaled, axis=0)
    right_norms = jnp.sum(right_scaled * right_scaled, axis=0)
    squared = (left_norms[:, None] + right_norms[None, :] - 2.0 * cross) / left_scaled.shape[0]
    distance = jnp.sqrt(jnp.maximum(squared, 0.0))
    stretched = root_three * distance
    ratio = distance / taper_radius
    taper = jnp.maximum(1.0 - ratio, 0.0) ** 4 * (1.0 + 4.0 * ratio)
    return amplitude * (1.0 + stretched) * jnp.exp(-stretched) * taper


def block_terms(left_scaled, right_scaled, left_dir, right_dir, amplitude):
    block_rows = left_scaled.shape[1]
    row_step = min(512, block_rows)
    left_half = left_dir.astype(jnp.bfloat16)
    right_half = right_dir.astype(jnp.bfloat16)

    def rows_visit(position, carried):
        toward_left, toward_right, row_sums, col_sums = carried
        offset = position * row_step
        kernel_rows = kernel_tile(
            lax.dynamic_slice_in_dim(left_scaled, offset, row_step, 1), right_scaled, amplitude
        )
        rows_half = kernel_rows.astype(jnp.bfloat16)
        product = lax.dot_general(
            right_half, rows_half, (((1,), (1,)), ((), ())), preferred_element_type=jnp.float32
        )
        toward_left = lax.dynamic_update_slice_in_dim(toward_left, product, offset, 1)
        toward_right = toward_right + jnp.dot(
            lax.dynamic_slice_in_dim(left_half, offset, row_step, 1),
            rows_half,
            preferred_element_type=jnp.float32,
        )
        row_sums = lax.dynamic_update_slice_in_dim(
            row_sums, jnp.sum(kernel_rows, axis=1), offset, 0
        )
        col_sums = col_sums + jnp.sum(kernel_rows, axis=0)
        return (toward_left, toward_right, row_sums, col_sums)

    zeros_dir = jnp.zeros(left_dir.shape, jnp.float32)
    zeros_row = jnp.zeros((block_rows,), jnp.float32)
    return lax.fori_loop(
        0, block_rows // row_step, rows_visit, (zeros_dir, zeros_dir, zeros_row, zeros_row)
    )


def body(features, inv_scale, signal, noise_var, right_side, block_pairs):
    local_rows = features.shape[1]
    blocks_here = local_rows // BS
    amplitude = signal[0]
    scaled = features * inv_scale[:, None]
    beyond = passed_along(scaled[:, :BS], "blk", -1)
    reach_scaled = jnp.concatenate([scaled, beyond], axis=1)
    base_block = lax.axis_index("blk") * blocks_here
    members = lax.axis_size("pair")
    listing = lax.all_gather(block_pairs, "pair", axis=0, tiled=True)
    living = (listing[:, 0] >= 0).astype(jnp.int32)
    ranked = jnp.cumsum(living) - living
    wanted = lax.axis_index("pair") + members * jnp.arange(block_pairs.shape[0], dtype=jnp.int32)
    matched = (ranked[None, :] == wanted[:, None]) & (living[None, :] > 0)
    chosen = jnp.sum(jnp.where(matched[:, :, None], listing[None, :, :], 0), axis=1)
    my_pairs = jnp.where(jnp.any(matched, axis=1)[:, None], chosen, -1)
    active = jnp.maximum((jnp.sum(living) - lax.axis_index("pair") + members - 1) // members, 0)
    row_local = my_pairs[:, 0] - base_block
    col_local = my_pairs[:, 1] - base_block
    solution = jnp.zeros_like(right_side)
    residual = right_side
    direction = right_side
    norm_now = lax.psum(jnp.sum(residual * residual, axis=1), "blk")
    for iteration in range(ITERS):
        ahead_dir = passed_along(direction[:, :BS], "blk", -1)
        reach_dir = jnp.concatenate([direction, ahead_dir], axis=1)

        def visit(slot_index, summed):
            row_start = row_local[slot_index] * BS
            col_start = col_local[slot_index] * BS
            crossing = (row_local[slot_index] != col_local[slot_index]).astype(jnp.float32)
            left_dir = lax.dynamic_slice_in_dim(reach_dir, row_start, BS, 1)
            right_dir = lax.dynamic_slice_in_dim(reach_dir, col_start, BS, 1)
            toward_left, toward_right, row_sums, col_sums = block_terms(
                lax.dynamic_slice_in_dim(reach_scaled, row_start, BS, 1),
                lax.dynamic_slice_in_dim(reach_scaled, col_start, BS, 1),
                left_dir,
                right_dir,
                amplitude,
            )
            term_left = toward_left + crossing * row_sums[None, :] * left_dir
            term_right = crossing * (toward_right + col_sums[None, :] * right_dir)
            summed = lax.dynamic_update_slice_in_dim(
                summed, lax.dynamic_slice_in_dim(summed, row_start, BS, 1) + term_left, row_start, 1
            )
            summed = lax.dynamic_update_slice_in_dim(
                summed,
                lax.dynamic_slice_in_dim(summed, col_start, BS, 1) + term_right,
                col_start,
                1,
            )
            return summed

        summed = lax.fori_loop(0, active, visit, jnp.zeros(reach_dir.shape, jnp.float32))
        own_part = summed[:, :local_rows]
        next_part = summed[:, local_rows:]
        own_sum, next_sum = lax.psum((own_part, next_part), "pair")
        entering = passed_along(next_sum, "blk", 1)
        coupled = jnp.concatenate([own_sum[:, :BS] + entering, own_sum[:, BS:]], axis=1)
        applied = noise_var[None, :] * direction + coupled
        last_turn = iteration + 1 == ITERS
        curvature = lax.psum(jnp.sum(direction * applied, axis=1), "blk")
        step_size = norm_now / curvature
        solution = solution + step_size[:, None] * direction
        residual = residual - step_size[:, None] * applied
        if not last_turn:
            norm_next = lax.psum(jnp.sum(residual * residual, axis=1), "blk")
            direction = residual + (norm_next / norm_now)[:, None] * direction
            norm_now = norm_next
    return (solution, residual)


def solution(mesh):
    members = mesh.shape["pair"]
    groups = mesh.shape["blk"]

    def chosen(features, *rest):
        one_block_each = features.shape[1] == members * BS and BS % CHUNK == 0 and BS > UPPER_STRIPS * CHUNK
        powers = members > 1 and members & (members - 1) == 0 and groups & (groups - 1) == 0
        fitting = 3 * rest[3].shape[0] <= 128 and rest[3].shape[0] % 8 == 0
        each = own_block_body if one_block_each and powers and fitting else body
        return each(features, *rest)

    placed = (P(None, "blk"), P(), P(), P("blk"), P(None, "blk"), P(("blk", "pair"), None))
    return jax.shard_map(
        chosen,
        mesh=mesh,
        in_specs=placed,
        out_specs=(P(None, "blk"), P(None, "blk")),
        check_vma=False,
    )
```
